32 devices in a mesh: dp: 8 (over y, x, core), space: 4 (over z).
Axes of the slice: x: 2, y: 2, z: 4, core: 2. Of those that a mesh axis runs over, the one named last changes fastest.
Arguments:
- features: bfloat16 [8, 24, 32, 1024], P('dp', 'space'), may hold values from -6 to 6
- labels: int32 [8, 24, 32], P('dp', 'space'), may hold values from 0 to 2
- pixel_weight: int32 [8, 24, 32], P('dp', 'space'), may hold values from 1 to 4
- conv_weight: bfloat16 [1024, 9, 128], replicated, may hold values from -0.0625 to 0.0625
- conv_bias: float32 [128], replicated, may hold values from -3 to 3
- class_weight: bfloat16 [128, 3], replicated, may hold values from -1.5 to 1.5
Outputs:
- features_grad: float32 [8, 24, 32, 1024], P('dp', 'space')
- weight_grad: float32 [9216, 128], P(('dp', 'space'))
The draws below stay inside these ranges and needn't reach their ends.
All inputs are finite; a program needn't handle non-finite values.
Results may differ from the reference program's by a relative error of at most 0.011.
Values may be sent and summed in bfloat16 or wider, within the bound.
No kernel may reach another device: no remote copies, remote signals or barrier semaphores. Data moves between devices by JAX's collectives and lax.ppermute only.
A program may use at most 64 MiB of HBM per device.

```python
import jax
import jax.numpy as jnp
from jax import lax

CIN = 1024
COUT = 128
NCLS = 3
TAPS = 9
DILATION_SIZE = 6
COLS = 32
NIMG = 8
HEIGHT = 24


def place_ends(result, stream_key, smallest, high):
    dims = result.shape
    index_at = [jax.random.randint(jax.random.fold_in(stream_key, axis), (), 0, dims[axis]) for axis in range(len(dims))]
    result = result.at[tuple(index_at)].set(smallest)
    longest = dims.index(max(dims))
    index_at[longest] = (index_at[longest] + 1) % dims[longest]
    return result.at[tuple(index_at)].set(high)


def steps_of(key, dims, shards, smallest, largest):
    gain, own = 1.0, jax.random.fold_in(key, 6)
    for axis_at, parts in shards:
        heights = jnp.exp(jax.random.uniform(jax.random.fold_in(own, axis_at), (parts,), jnp.float32, smallest / len(shards), largest / len(shards)))
        gain = gain * jnp.repeat(heights, dims[axis_at] // parts).reshape([-1 if axis == axis_at else 1 for axis in range(len(dims))])
    return gain


def noise(stream_key, shape, spread, limit, split=(), kind=jnp.bfloat16):
    array = spread * jax.random.normal(stream_key, shape, jnp.float32)
    if split:
        array = array * steps_of(stream_key, shape, split, -0.22, 0.18)
    return jnp.clip(array, -limit, limit).astype(kind)


def setup_inputs(seed: int = 0) -> dict:
    splits = jax.random.split(jax.random.key(seed), 7)
    return {
        "features": noise(splits[0], (NIMG, HEIGHT, COLS, CIN), 1.0, 6.0, ((0, 8), (1, 4))),
        "labels": place_ends(jax.random.randint(splits[1], (NIMG, HEIGHT, COLS), 0, NCLS), jax.random.fold_in(splits[1], 1), 0, NCLS - 1).astype(jnp.int32),
        "pixel_weight": place_ends(jax.random.randint(splits[2], (NIMG, HEIGHT, COLS), 1, 5), jax.random.fold_in(splits[2], 1), 1, 4).astype(jnp.int32),
        "conv_weight": noise(splits[3], (CIN, TAPS, COUT), (CIN * TAPS) ** -0.5, 0.0625),
        "conv_bias": noise(splits[4], (COUT,), 0.5, 3.0, (), jnp.float32),
        "class_weight": noise(splits[5], (COUT, NCLS), 0.25, 1.5),
    }


def one_image(conv_weight, conv_bias, class_weight, input_image, label_map, weight_map):
    image_height, image_width, input_width = input_image.shape
    output_width = conv_weight.shape[2]
    pixel_count = image_height * image_width
    padded_input = jnp.pad(input_image, ((DILATION_SIZE, DILATION_SIZE), (DILATION_SIZE, DILATION_SIZE), (0, 0)))
    preact = jnp.zeros((pixel_count, output_width), jnp.float32)
    for tap_row in range(3):
        for column_tap in range(3):
            input_piece = padded_input[tap_row * DILATION_SIZE:tap_row * DILATION_SIZE + image_height, column_tap * DILATION_SIZE:column_tap * DILATION_SIZE + image_width].reshape(pixel_count, input_width)
            preact = preact + jnp.dot(input_piece, conv_weight[:, 3 * tap_row + column_tap, :], preferred_element_type=jnp.float32)
    preact = preact + conv_bias
    sigmoid_z = jax.nn.sigmoid(preact)
    hidden = (preact * sigmoid_z).astype(jnp.bfloat16)
    logits = jnp.dot(hidden, class_weight, preferred_element_type=jnp.float32)
    exponent = jnp.exp(logits)
    chances = exponent / jnp.sum(exponent, axis=1, keepdims=True)
    classes = jnp.arange(NCLS, dtype=jnp.int32)[None, :]
    onehot = (label_map.reshape(pixel_count, 1) == classes).astype(jnp.float32)
    grad_logits = weight_map.reshape(pixel_count, 1).astype(jnp.float32) * (chances - onehot)
    hidden_grad = jnp.dot(grad_logits, class_weight.astype(jnp.float32).T, precision=lax.Precision.HIGHEST)
    preact_gradient = (hidden_grad * sigmoid_z * (1.0 + preact * (1.0 - sigmoid_z))).astype(jnp.bfloat16)
    padded_gradient = jnp.pad(preact_gradient.reshape(image_height, image_width, output_width), ((DILATION_SIZE, DILATION_SIZE), (DILATION_SIZE, DILATION_SIZE), (0, 0)))
    flat_image = input_image.reshape(pixel_count, input_width)
    feature_grad = jnp.zeros((pixel_count, input_width), jnp.float32)
    tap_grads = []
    for tap_row in range(3):
        for column_tap in range(3):
            upper_row = (2 - tap_row) * DILATION_SIZE
            left_column = (2 - column_tap) * DILATION_SIZE
            input_piece = padded_gradient[upper_row:upper_row + image_height, left_column:left_column + image_width].reshape(pixel_count, output_width)
            feature_grad = feature_grad + lax.dot_general(input_piece, conv_weight[:, 3 * tap_row + column_tap, :], (((1,), (1,)), ((), ())), preferred_element_type=jnp.float32)
            tap_grads.append(lax.dot_general(flat_image, input_piece, (((0,), (0,)), ((), ())), preferred_element_type=jnp.float32))
    return feature_grad.reshape(image_height, image_width, input_width), jnp.stack(tap_grads, axis=1)


def reference(features, labels, pixel_weight, conv_weight, conv_bias, class_weight):
    def image_step(carry, inputs):
        input_image, label_map, weight_map = inputs
        feature_grad, kernel_grad = one_image(conv_weight, conv_bias, class_weight, input_image, label_map, weight_map)
        return carry + kernel_grad, feature_grad

    initial = jnp.zeros(conv_weight.shape, jnp.float32)
    summed, features_grad = lax.scan(image_step, initial, (features, labels, pixel_weight))
    weight_grad = (summed / NIMG).reshape(conv_weight.shape[0] * conv_weight.shape[1], conv_weight.shape[2])
    return features_grad, weight_grad
```

```python
import jax
import jax.numpy as jnp
from jax import lax
from jax.sharding import PartitionSpec as P

DILATION_SIZE = 6


def channel_plan(channels, taps, replicas, bands):
    rows = channels * taps // (replicas * bands)
    starts = [[(d * bands + s) * rows // taps for d in range(replicas)] for s in range(bands)]
    offsets = [[(d * bands + s) * rows % taps for d in range(replicas)] for s in range(bands)]
    cover = max(-(-(off + rows) // taps) for line in offsets for off in line)
    picks = [[min(c + k, channels - 1) for c in line for k in range(cover)] for line in starts]
    return rows, cover, picks, offsets


def column_shift(array, by):
    width = array.shape[1]
    if by == 0:
        return array
    if by > 0:
        return jnp.pad(array[:, by:], ((0, 0), (0, by), (0, 0)))
    return jnp.pad(array[:, : width + by], ((0, 0), (-by, 0), (0, 0)))


def on_device(features, labels, pixel_weight, conv_weight, conv_bias, class_weight):
    image = features[0]
    band_rows, columns, channels = image.shape
    taps, width = conv_weight.shape[1:]
    pixels = band_rows * columns
    replicas = lax.axis_size("dp")
    bands = lax.axis_size("space")
    band = lax.axis_index("space")
    reach = DILATION_SIZE

    block_rows, cover, picks, offsets = channel_plan(channels, taps, replicas, bands)
    flat = image.reshape(pixels, channels)
    if block_rows % taps == 0:
        split = flat.reshape(pixels, replicas, bands, cover).transpose(2, 0, 1, 3)
        split = split.reshape(bands, pixels, replicas * cover)
    else:
        order = jnp.array([c for line in picks for c in line], jnp.int32)
        split = jnp.take(flat, order, axis=1).reshape(pixels, bands, replicas * cover).transpose(1, 0, 2)
    whole = lax.all_to_all(split, "space", 0, 0)

    product = lax.dot_general(
        flat, conv_weight, (((1,), (0,)), ((), ())), preferred_element_type=jnp.float32
    ).reshape(band_rows, columns, taps, width)
    parts = [
        sum(column_shift(product[:, :, 3 * a + b], (b - 1) * reach) for b in range(3)) for a in range(3)
    ]
    spread = sum(
        jnp.pad(parts[a], (((2 - a) * reach, a * reach), (0, 0), (0, 0))) for a in range(3)
    )
    before = spread[:reach].astype(jnp.bfloat16)
    after = spread[reach + band_rows :].astype(jnp.bfloat16)
    index = jnp.arange(bands)[:, None, None, None]
    blocks = jnp.where(index == band - 1, before, jnp.where(index == band + 1, after, jnp.bfloat16(0)))
    came = lax.all_to_all(blocks, "space", 0, 0)
    from_above = jnp.sum(jnp.where(index == band - 1, came, 0), axis=0, dtype=jnp.float32)
    from_below = jnp.sum(jnp.where(index == band + 1, came, 0), axis=0, dtype=jnp.float32)
    middle = spread[reach : reach + band_rows]
    middle = middle + jnp.pad(from_above, ((0, band_rows - reach), (0, 0), (0, 0)))
    middle = middle + jnp.pad(from_below, ((band_rows - reach, 0), (0, 0), (0, 0)))
    preact = middle.reshape(pixels, width) + conv_bias

    sigmoid_z = jax.nn.sigmoid(preact)
    hidden = (preact * sigmoid_z).astype(jnp.bfloat16)
    logits = jnp.dot(hidden, class_weight, preferred_element_type=jnp.float32)
    exponent = jnp.exp(logits)
    chances = exponent / jnp.sum(exponent, axis=1, keepdims=True)
    classes = lax.broadcasted_iota(jnp.int32, (1, class_weight.shape[1]), 1)
    onehot = (labels.reshape(pixels, 1) == classes).astype(jnp.float32)
    grad_logits = pixel_weight.reshape(pixels, 1).astype(jnp.float32) * (chances - onehot)
    hidden_grad = jnp.dot(
        grad_logits, class_weight.astype(jnp.float32).T, precision=lax.Precision.HIGHEST
    )
    gradient = (hidden_grad * sigmoid_z * (1.0 + preact * (1.0 - sigmoid_z))).astype(jnp.bfloat16)

    gathered = lax.all_to_all(
        jnp.broadcast_to(gradient[None], (bands, pixels, width)), "space", 0, 0
    ).reshape(bands * band_rows, columns, width)
    wide = jnp.pad(gathered, ((reach, reach), (reach, reach), (0, 0)))
    tap_views = [
        wide[(2 - a) * reach : (2 - a) * reach + bands * band_rows, (2 - b) * reach : (2 - b) * reach + columns]
        for a in range(3)
        for b in range(3)
    ]
    shifted = jnp.concatenate(
        [view.reshape(bands * pixels, width) for view in tap_views], axis=1
    )
    kernel_grad = lax.dot_general(
        whole.reshape(bands * pixels, replicas * cover),
        shifted,
        (((0,), (0,)), ((), ())),
        preferred_element_type=jnp.float32,
    )
    blocks = kernel_grad.astype(jnp.bfloat16).reshape(replicas, cover, taps * width)
    came = lax.all_to_all(blocks, "dp", 0, 0)
    weight_grad = jnp.sum(came.astype(jnp.float32), axis=0) / replicas
    weight_grad = weight_grad.reshape(cover * taps, width)
    if block_rows % taps:
        me = lax.axis_index("dp")
        weight_grad = lax.dynamic_slice_in_dim(weight_grad, jnp.array(offsets)[band, me], block_rows)

    local = lax.dynamic_slice_in_dim(shifted, band * pixels, pixels)
    feature_grad = lax.dot_general(
        local.reshape(pixels, taps, width),
        conv_weight,
        (((1, 2), (1, 2)), ((), ())),
        preferred_element_type=jnp.float32,
    )
    return feature_grad.reshape(1, band_rows, columns, channels), weight_grad


def solution(mesh):
    placed = (
        P("dp", "space", None, None),
        P("dp", "space", None),
        P("dp", "space", None),
        P(),
        P(),
        P(),
    )
    return jax.shard_map(
        on_device,
        mesh=mesh,
        in_specs=placed,
        out_specs=(P("dp", "space", None, None), P(("dp", "space"), None)),
        check_vma=False,
    )
```

```python
import functools

import jax
import jax.numpy as jnp
from jax import lax
from jax.experimental import pallas as pl
from jax.experimental.pallas import tpu as pltpu
from jax.sharding import PartitionSpec as P

DILATION_SIZE = 6
VMEM_LIMIT = 48 * 1024 * 1024


def channel_plan(channels, taps, replicas, bands):
    rows = channels * taps // (replicas * bands)
    starts = [[(d * bands + s) * rows // taps for d in range(replicas)] for s in range(bands)]
    offsets = [[(d * bands + s) * rows % taps for d in range(replicas)] for s in range(bands)]
    cover = max(-(-(off + rows) // taps) for line in offsets for off in line)
    picks = [[min(c + k, channels - 1) for c in line for k in range(cover)] for line in starts]
    return rows, cover, picks, offsets


def shift_columns(array, by, columns):
    if by == 0:
        return array
    size = array.shape[0]
    column = lax.broadcasted_iota(jnp.int32, array.shape, 0) % columns + by
    moved = pltpu.roll(array, (-by) % size, 0)
    return jnp.where((column >= 0) & (column < columns), moved, 0.0)


def forward_kernel(columns, reach, x_ref, w_ref, middle_ref, halo_ref):
    step = pl.program_id(0)
    band = lax.axis_index("space")
    bands = halo_ref.shape[0]
    pixels = x_ref.shape[0]
    width = w_ref.shape[2]
    edge = reach * columns
    weight = jnp.concatenate([w_ref[b] for b in range(3)], axis=1)
    product = jnp.dot(x_ref[...], weight, preferred_element_type=jnp.float32)
    part = sum(
        shift_columns(product[:, b * width : (b + 1) * width], (b - 1) * reach, columns)
        for b in range(3)
    )

    @pl.when(step == 0)
    def _():
        halo_ref[...] = jnp.zeros_like(halo_ref)
        if pixels > edge:
            middle_ref[:edge] = jnp.zeros((edge, width), jnp.float32)
            middle_ref[edge:] = part[: pixels - edge]

        @pl.when(band + 1 < bands)
        def _():
            halo_ref[jnp.minimum(band + 1, bands - 1)] = part[pixels - edge :].astype(halo_ref.dtype)

    @pl.when(step == 1)
    def _():
        if pixels > edge:
            middle_ref[...] += part
        else:
            middle_ref[...] = part

    @pl.when(step == 2)
    def _():
        if pixels > edge:
            middle_ref[: pixels - edge] += part[edge:]

        @pl.when(band > 0)
        def _():
            halo_ref[jnp.maximum(band - 1, 0)] = part[:edge].astype(halo_ref.dtype)


def forward(flat, weight, bands, columns, reach):
    pixels, channels = flat.shape
    taps, _, width = weight.shape
    return pl.pallas_call(
        functools.partial(forward_kernel, columns, reach),
        grid=(3,),
        in_specs=[
            pl.BlockSpec((pixels, channels), lambda i: (0, 0)),
            pl.BlockSpec((3, channels, width), lambda i: (i, 0, 0)),
        ],
        out_specs=[
            pl.BlockSpec((pixels, width), lambda i: (0, 0)),
            pl.BlockSpec((bands, reach * columns, width), lambda i: (0, 0, 0)),
        ],
        out_shape=[
            jax.ShapeDtypeStruct((pixels, width), jnp.float32),
            jax.ShapeDtypeStruct((bands, reach * columns, width), jnp.bfloat16),
        ],
        compiler_params=pltpu.CompilerParams(vmem_limit_bytes=VMEM_LIMIT),
        cost_estimate=pl.CostEstimate(
            flops=2 * pixels * channels * taps * width,
            bytes_accessed=2 * taps * channels * width + 2 * pixels * channels,
            transcendentals=0,
        ),
        name="forward",
    )(flat, weight)


def arrange_kernel(replicas, cover, x_ref, out_ref):
    bands = out_ref.shape[0]
    x = x_ref[...]
    for s in range(bands):
        out_ref[s] = jnp.concatenate(
            [x[:, (d * bands + s) * cover : (d * bands + s + 1) * cover] for d in range(replicas)],
            axis=1,
        )


def arrange(flat, bands, replicas, cover):
    pixels, channels = flat.shape
    return pl.pallas_call(
        functools.partial(arrange_kernel, replicas, cover),
        out_shape=jax.ShapeDtypeStruct((bands, pixels, replicas * cover), flat.dtype),
        compiler_params=pltpu.CompilerParams(vmem_limit_bytes=VMEM_LIMIT),
        cost_estimate=pl.CostEstimate(
            flops=0, bytes_accessed=4 * pixels * channels, transcendentals=0
        ),
        name="arrange",
    )(flat)


def pointwise_kernel(
    edge, middle_ref, halo_ref, bias_ref, class_ref, label_ref, scale_ref, feature_ref, out_ref
):
    band = lax.axis_index("space")
    bands = halo_ref.shape[0]
    pixels, width = middle_ref.shape
    above = halo_ref[jnp.maximum(band - 1, 0)].astype(jnp.float32)
    below = halo_ref[jnp.minimum(band + 1, bands - 1)].astype(jnp.float32)
    above = jnp.where(band > 0, above, 0.0)
    below = jnp.where(band + 1 < bands, below, 0.0)
    if pixels > edge:
        none = jnp.zeros((pixels - edge, width), jnp.float32)
        above = jnp.concatenate([above, none], axis=0)
        below = jnp.concatenate([none, below], axis=0)
    preact = middle_ref[...] + above + below + bias_ref[...]
    sigmoid_z = jax.nn.sigmoid(preact)
    hidden = (preact * sigmoid_z).astype(jnp.bfloat16)
    classes = class_ref[...]
    logits = lax.dot_general(
        hidden, classes, (((1,), (1,)), ((), ())), preferred_element_type=jnp.float32
    )
    exponent = jnp.exp(logits)
    chances = exponent / jnp.sum(exponent, axis=1, keepdims=True)
    index = lax.broadcasted_iota(jnp.int32, chances.shape, 1)
    onehot = jnp.where(label_ref[...] == index, 1.0, 0.0)
    grad_logits = scale_ref[...].astype(jnp.float32) * (chances - onehot)
    wide = classes.astype(jnp.float32)
    hidden_grad = sum(
        grad_logits[:, k : k + 1] * wide[k : k + 1] for k in range(classes.shape[0])
    )
    gradient = hidden_grad * sigmoid_z * (1.0 + preact * (1.0 - sigmoid_z))
    gradient = gradient.astype(out_ref.dtype)
    for s in range(bands):
        out_ref[s, :, :width] = gradient
        out_ref[s, :, width:] = feature_ref[s]


def pointwise(middle, halo, bias, classes, labels, scale, features):
    pixels, width = middle.shape
    bands, edge, _ = halo.shape
    extra = features.shape[2]
    return pl.pallas_call(
        functools.partial(pointwise_kernel, edge),
        out_shape=jax.ShapeDtypeStruct((bands, pixels, width + extra), jnp.bfloat16),
        compiler_params=pltpu.CompilerParams(vmem_limit_bytes=VMEM_LIMIT),
        cost_estimate=pl.CostEstimate(
            flops=30 * pixels * width,
            bytes_accessed=4 * bands * pixels * (width + extra),
            transcendentals=pixels * width,
        ),
        name="pointwise",
    )(middle, halo, bias, classes, labels, scale, features)


def shifted_taps(gradient, columns, reach):
    wide = gradient.astype(jnp.float32)
    return jnp.concatenate(
        [shift_columns(wide, (1 - b) * reach, columns).astype(jnp.bfloat16) for b in range(3)],
        axis=1,
    )


def kernel_grad_kernel(columns, reach, in_ref, out_ref):
    width = out_ref.shape[1] // 9
    bands, pixels, lanes = in_ref.shape
    together = in_ref[...].reshape(bands * pixels, lanes)
    total = bands * pixels
    edge = reach * columns
    shifted = shifted_taps(together[:, :width], columns, reach)
    features = together[:, width:]
    contract = (((0,), (0,)), ((), ()))
    for a in range(3):
        if a == 0:
            left, right = features[: total - edge], shifted[edge:]
        elif a == 1:
            left, right = features, shifted
        else:
            left, right = features[edge:], shifted[: total - edge]
        block = lax.dot_general(left, right, contract, preferred_element_type=jnp.float32)
        out_ref[:, 3 * a * width : 3 * (a + 1) * width] = block.astype(out_ref.dtype)


def kernel_grad(gathered, width, columns, reach):
    bands, pixels, lanes = gathered.shape
    extra = lanes - width
    return pl.pallas_call(
        functools.partial(kernel_grad_kernel, columns, reach),
        out_shape=jax.ShapeDtypeStruct((extra, 9 * width), jnp.bfloat16),
        compiler_params=pltpu.CompilerParams(vmem_limit_bytes=VMEM_LIMIT),
        cost_estimate=pl.CostEstimate(
            flops=18 * bands * pixels * extra * width,
            bytes_accessed=2 * bands * pixels * lanes + 18 * extra * width,
            transcendentals=0,
        ),
        name="kernel_grad",
    )(gathered)


def feature_grad_kernel(columns, reach, g_ref, w_ref, out_ref):
    band = lax.axis_index("space")
    bands, pixels, width = g_ref.shape
    edge = reach * columns
    own = g_ref[band]
    above = g_ref[jnp.maximum(band - 1, 0)][pixels - edge :]
    below = g_ref[jnp.minimum(band + 1, bands - 1)][:edge]
    above = jnp.where(band > 0, above, jnp.zeros_like(above))
    below = jnp.where(band + 1 < bands, below, jnp.zeros_like(below))
    stack = shifted_taps(jnp.concatenate([above, own, below], axis=0), columns, reach)
    taps = jnp.concatenate(
        [stack[(2 - a) * edge : (2 - a) * edge + pixels] for a in range(3)], axis=1
    )
    weight = jnp.concatenate([w_ref[t] for t in range(9)], axis=1)
    out_ref[...] = lax.dot_general(
        taps, weight, (((1,), (1,)), ((), ())), preferred_element_type=jnp.float32
    )


def feature_grad(gathered, weight, columns, reach):
    bands, pixels, _ = gathered.shape
    taps, channels, width = weight.shape
    step = 256 if channels % 256 == 0 else channels
    return pl.pallas_call(
        functools.partial(feature_grad_kernel, columns, reach),
        grid=(channels // step,),
        in_specs=[
            pl.BlockSpec((bands, pixels, width), lambda i: (0, 0, 0)),
            pl.BlockSpec((taps, step, width), lambda i: (0, i, 0)),
        ],
        out_specs=pl.BlockSpec((pixels, step), lambda i: (0, i)),
        out_shape=jax.ShapeDtypeStruct((pixels, channels), jnp.float32),
        compiler_params=pltpu.CompilerParams(vmem_limit_bytes=VMEM_LIMIT),
        cost_estimate=pl.CostEstimate(
            flops=2 * pixels * taps * channels * width,
            bytes_accessed=2 * taps * channels * width + 4 * pixels * channels,
            transcendentals=0,
        ),
        name="feature_grad",
    )(gathered, weight)


def final_kernel(in_ref, out_ref):
    replicas, cover, lanes = in_ref.shape
    width = out_ref.shape[1]
    taps = lanes // width
    total = in_ref[0].astype(jnp.float32)
    for d in range(1, replicas):
        total += in_ref[d].astype(jnp.float32)
    total = total / replicas
    for t in range(taps):
        out_ref[pl.ds(t, cover, stride=taps), :] = total[:, t * width : (t + 1) * width]


def final(came, width):
    replicas, cover, lanes = came.shape
    return pl.pallas_call(
        final_kernel,
        out_shape=jax.ShapeDtypeStruct((cover * lanes // width, width), jnp.float32),
        compiler_params=pltpu.CompilerParams(vmem_limit_bytes=VMEM_LIMIT),
        name="final_sum",
    )(came)


def on_device(features, labels, pixel_weight, conv_weight, conv_bias, class_weight):
    image = features[0]
    band_rows, columns, channels = image.shape
    taps, width = conv_weight.shape[1:]
    pixels = band_rows * columns
    replicas = lax.axis_size("dp")
    bands = lax.axis_size("space")
    reach = DILATION_SIZE

    flat = image.reshape(pixels, channels)
    weight = conv_weight.transpose(1, 0, 2)
    middle, halo = forward(flat, weight, bands, columns, reach)
    halo = lax.all_to_all(halo, "space", 0, 0)

    block_rows, cover, picks, offsets = channel_plan(channels, taps, replicas, bands)
    if block_rows % taps == 0:
        split = arrange(flat, bands, replicas, cover)
    else:
        order = jnp.array([c for line in picks for c in line], jnp.int32)
        split = jnp.take(flat, order, axis=1)
        split = split.reshape(pixels, bands, replicas * cover).transpose(1, 0, 2)

    packed = pointwise(
        middle,
        halo,
        conv_bias.reshape(1, width),
        class_weight.T,
        labels.reshape(pixels, 1),
        pixel_weight.reshape(pixels, 1),
        split,
    )
    gathered = lax.all_to_all(packed, "space", 0, 0)
    partial_grad = kernel_grad(gathered, width, columns, reach)
    came = lax.all_to_all(partial_grad.reshape(replicas, cover, taps * width), "dp", 0, 0)
    weight_grad = final(came, width)
    if block_rows % taps:
        start = jnp.array(offsets)[lax.axis_index("space"), lax.axis_index("dp")]
        weight_grad = lax.dynamic_slice_in_dim(weight_grad, start, block_rows)

    grad = feature_grad(gathered[:, :, :width], weight, columns, reach)
    return grad.reshape(1, band_rows, columns, channels), weight_grad


def solution(mesh):
    placed = (
        P("dp", "space", None, None),
        P("dp", "space", None),
        P("dp", "space", None),
        P(),
        P(),
        P(),
    )
    return jax.shard_map(
        on_device,
        mesh=mesh,
        in_specs=placed,
        out_specs=(P("dp", "space", None, None), P(("dp", "space"), None)),
        check_vma=False,
    )
```

```python
import functools

import jax
import jax.numpy as jnp
from jax import lax
from jax.experimental import pallas as pl
from jax.experimental.pallas import tpu as pltpu
from jax.sharding import PartitionSpec as P

DILATION_SIZE = 6
VMEM_LIMIT = 16 * 1024 * 1024
VMEM_WHOLE = 60 * 1024 * 1024


def channel_plan(channels, taps, replicas, bands):
    rows = channels * taps // (replicas * bands)
    starts = [[(d * bands + s) * rows // taps for d in range(replicas)] for s in range(bands)]
    offsets = [[(d * bands + s) * rows % taps for d in range(replicas)] for s in range(bands)]
    cover = max(-(-(off + rows) // taps) for line in offsets for off in line)
    picks = [[min(c + k, channels - 1) for c in line for k in range(cover)] for line in starts]
    return rows, cover, picks, offsets


def shift_columns(array, by, columns):
    if by == 0:
        return array
    size = array.shape[0]
    column = lax.broadcasted_iota(jnp.int32, array.shape, 0) % columns + by
    moved = pltpu.roll(array, (-by) % size, 0)
    return jnp.where((column >= 0) & (column < columns), moved, 0.0)


def forward_kernel(columns, reach, x_ref, w_ref, middle_ref, halo_ref):
    step = pl.program_id(0)
    band = lax.axis_index("space")
    bands = halo_ref.shape[0]
    pixels = x_ref.shape[0]
    width = w_ref.shape[2]
    edge = reach * columns
    weight = jnp.concatenate([w_ref[b] for b in range(3)], axis=1)
    product = jnp.dot(x_ref[...], weight, preferred_element_type=jnp.float32)
    part = sum(
        shift_columns(product[:, b * width : (b + 1) * width], (b - 1) * reach, columns)
        for b in range(3)
    )

    @pl.when(step == 0)
    def _():
        halo_ref[...] = jnp.zeros_like(halo_ref)
        if pixels > edge:
            middle_ref[:edge] = jnp.zeros((edge, width), jnp.float32)
            middle_ref[edge:] = part[: pixels - edge]

        @pl.when(band + 1 < bands)
        def _():
            halo_ref[jnp.minimum(band + 1, bands - 1)] = part[pixels - edge :].astype(halo_ref.dtype)

    @pl.when(step == 1)
    def _():
        if pixels > edge:
            middle_ref[...] += part
        else:
            middle_ref[...] = part

    @pl.when(step == 2)
    def _():
        if pixels > edge:
            middle_ref[: pixels - edge] += part[edge:]

        @pl.when(band > 0)
        def _():
            halo_ref[jnp.maximum(band - 1, 0)] = part[:edge].astype(halo_ref.dtype)


def forward(flat, weight, bands, columns, reach):
    pixels, channels = flat.shape
    taps, _, width = weight.shape
    return pl.pallas_call(
        functools.partial(forward_kernel, columns, reach),
        grid=(3,),
        in_specs=[
            pl.BlockSpec((pixels, channels), lambda i: (0, 0)),
            pl.BlockSpec((3, channels, width), lambda i: (i, 0, 0)),
        ],
        out_specs=[
            pl.BlockSpec((pixels, width), lambda i: (0, 0)),
            pl.BlockSpec((bands, reach * columns, width), lambda i: (0, 0, 0)),
        ],
        out_shape=[
            jax.ShapeDtypeStruct((pixels, width), jnp.float32),
            jax.ShapeDtypeStruct((bands, reach * columns, width), jnp.bfloat16),
        ],
        compiler_params=pltpu.CompilerParams(vmem_limit_bytes=VMEM_WHOLE),
        cost_estimate=pl.CostEstimate(
            flops=2 * pixels * channels * taps * width,
            bytes_accessed=2 * taps * channels * width + 2 * pixels * channels,
            transcendentals=0,
        ),
        name="forward",
    )(flat, weight)


def arrange_kernel(replicas, cover, x_ref, after_ref, out_ref):
    del after_ref
    bands = out_ref.shape[0]
    x = x_ref[...]
    for s in range(bands):
        out_ref[s] = jnp.concatenate(
            [x[:, (d * bands + s) * cover : (d * bands + s + 1) * cover] for d in range(replicas)],
            axis=1,
        )


def arrange(flat, after, bands, replicas, cover):
    pixels, channels = flat.shape
    return pl.pallas_call(
        functools.partial(arrange_kernel, replicas, cover),
        in_specs=[pl.BlockSpec(memory_space=pltpu.VMEM), pl.BlockSpec(memory_space=pl.ANY)],
        out_shape=jax.ShapeDtypeStruct((bands, pixels, replicas * cover), flat.dtype),
        compiler_params=pltpu.CompilerParams(vmem_limit_bytes=VMEM_LIMIT),
        cost_estimate=pl.CostEstimate(
            flops=0, bytes_accessed=4 * pixels * channels, transcendentals=0
        ),
        name="arrange",
    )(flat, after)


def pointwise_kernel(
    edge, middle_ref, halo_ref, bias_ref, class_ref, label_ref, scale_ref, out_ref
):
    band = lax.axis_index("space")
    bands = halo_ref.shape[0]
    pixels, width = middle_ref.shape
    above = halo_ref[jnp.maximum(band - 1, 0)].astype(jnp.float32)
    below = halo_ref[jnp.minimum(band + 1, bands - 1)].astype(jnp.float32)
    above = jnp.where(band > 0, above, 0.0)
    below = jnp.where(band + 1 < bands, below, 0.0)
    if pixels > edge:
        none = jnp.zeros((pixels - edge, width), jnp.float32)
        above = jnp.concatenate([above, none], axis=0)
        below = jnp.concatenate([none, below], axis=0)
    preact = middle_ref[...] + above + below + bias_ref[...]
    sigmoid_z = jax.nn.sigmoid(preact)
    hidden = (preact * sigmoid_z).astype(jnp.bfloat16)
    classes = class_ref[...]
    logits = lax.dot_general(
        hidden, classes, (((1,), (1,)), ((), ())), preferred_element_type=jnp.float32
    )
    exponent = jnp.exp(logits)
    chances = exponent / jnp.sum(exponent, axis=1, keepdims=True)
    index = lax.broadcasted_iota(jnp.int32, chances.shape, 1)
    onehot = jnp.where(label_ref[...] == index, 1.0, 0.0)
    grad_logits = scale_ref[...].astype(jnp.float32) * (chances - onehot)
    wide = classes.astype(jnp.float32)
    hidden_grad = sum(
        grad_logits[:, k : k + 1] * wide[k : k + 1] for k in range(classes.shape[0])
    )
    gradient = hidden_grad * sigmoid_z * (1.0 + preact * (1.0 - sigmoid_z))
    gradient = gradient.astype(out_ref.dtype)
    for s in range(bands):
        out_ref[s] = gradient


def pointwise(middle, halo, bias, classes, labels, scale):
    pixels, width = middle.shape
    bands, edge, _ = halo.shape
    return pl.pallas_call(
        functools.partial(pointwise_kernel, edge),
        out_shape=jax.ShapeDtypeStruct((bands, pixels, width), jnp.bfloat16),
        compiler_params=pltpu.CompilerParams(vmem_limit_bytes=VMEM_LIMIT),
        cost_estimate=pl.CostEstimate(
            flops=30 * pixels * width,
            bytes_accessed=2 * bands * pixels * width + 4 * pixels * width,
            transcendentals=pixels * width,
        ),
        name="pointwise",
    )(middle, halo, bias, classes, labels, scale)


def shifted_taps(gradient, columns, reach):
    wide = gradient.astype(jnp.float32)
    return jnp.concatenate(
        [shift_columns(wide, (1 - b) * reach, columns).astype(jnp.bfloat16) for b in range(3)],
        axis=1,
    )


def kernel_grad_kernel(columns, reach, g_ref, *refs):
    out_ref, padded = refs[-2:]
    bands, pixels, width = g_ref.shape
    edge = reach * columns
    total = bands * pixels
    band = lax.axis_index("space")
    shifted = shifted_taps(g_ref[...].reshape(total, width), columns, reach)
    padded[:edge] = jnp.zeros((edge, 3 * width), padded.dtype)
    padded[edge : edge + total] = shifted
    padded[edge + total :] = jnp.zeros((edge, 3 * width), padded.dtype)
    grad = None
    for k in range(bands):
        first = lax.rem(band + bands - k, bands) * pixels
        right = jnp.concatenate(
            [padded[pl.ds(pl.multiple_of(first + (2 - a) * edge, 16), pixels)] for a in range(3)], axis=1
        )
        term = lax.dot_general(
            refs[k][...], right, (((0,), (0,)), ((), ())), preferred_element_type=jnp.float32
        )
        grad = term if grad is None else grad + term
    out_ref[...] = grad.astype(out_ref.dtype)


def kernel_grad(gathered, blocks, columns, reach):
    bands, pixels, width = gathered.shape
    extra = blocks[0].shape[1]
    edge = reach * columns
    return pl.pallas_call(
        functools.partial(kernel_grad_kernel, columns, reach),
        out_shape=jax.ShapeDtypeStruct((extra, 9 * width), jnp.bfloat16),
        scratch_shapes=[pltpu.VMEM((bands * pixels + 2 * edge, 3 * width), jnp.bfloat16)],
        compiler_params=pltpu.CompilerParams(vmem_limit_bytes=VMEM_LIMIT),
        cost_estimate=pl.CostEstimate(
            flops=18 * bands * pixels * extra * width,
            bytes_accessed=2 * bands * pixels * (width + extra) + 18 * extra * width,
            transcendentals=0,
        ),
        name="kernel_grad",
    )(gathered, *blocks)


def feature_grad_kernel(columns, reach, g_ref, w_ref, out_ref):
    band = lax.axis_index("space")
    bands, pixels, width = g_ref.shape
    edge = reach * columns
    own = g_ref[band]
    above = g_ref[jnp.maximum(band - 1, 0)][pixels - edge :]
    below = g_ref[jnp.minimum(band + 1, bands - 1)][:edge]
    above = jnp.where(band > 0, above, jnp.zeros_like(above))
    below = jnp.where(band + 1 < bands, below, jnp.zeros_like(below))
    stack = shifted_taps(jnp.concatenate([above, own, below], axis=0), columns, reach)
    taps = jnp.concatenate(
        [stack[(2 - a) * edge : (2 - a) * edge + pixels] for a in range(3)], axis=1
    )
    weight = jnp.concatenate([w_ref[t] for t in range(9)], axis=1)
    out_ref[...] = lax.dot_general(
        taps, weight, (((1,), (1,)), ((), ())), preferred_element_type=jnp.float32
    )


def feature_grad(gathered, weight, columns, reach):
    bands, pixels, _ = gathered.shape
    taps, channels, width = weight.shape
    step = 256 if channels % 256 == 0 else channels
    return pl.pallas_call(
        functools.partial(feature_grad_kernel, columns, reach),
        grid=(channels // step,),
        in_specs=[
            pl.BlockSpec((bands, pixels, width), lambda i: (0, 0, 0)),
            pl.BlockSpec((taps, step, width), lambda i: (0, i, 0)),
        ],
        out_specs=pl.BlockSpec((pixels, step), lambda i: (0, i)),
        out_shape=jax.ShapeDtypeStruct((pixels, channels), jnp.float32),
        compiler_params=pltpu.CompilerParams(vmem_limit_bytes=VMEM_LIMIT),
        cost_estimate=pl.CostEstimate(
            flops=2 * pixels * taps * channels * width,
            bytes_accessed=2 * taps * channels * width + 4 * pixels * channels,
            transcendentals=0,
        ),
        name="feature_grad",
    )(gathered, weight)


def final_kernel(in_ref, out_ref):
    replicas, cover, lanes = in_ref.shape
    width = out_ref.shape[1]
    taps = lanes // width
    total = in_ref[0].astype(jnp.float32)
    for d in range(1, replicas):
        total += in_ref[d].astype(jnp.float32)
    total = total / replicas
    for t in range(taps):
        out_ref[pl.ds(t, cover, stride=taps), :] = total[:, t * width : (t + 1) * width]


def final(came, width):
    replicas, cover, lanes = came.shape
    return pl.pallas_call(
        final_kernel,
        out_shape=jax.ShapeDtypeStruct((cover * lanes // width, width), jnp.float32),
        compiler_params=pltpu.CompilerParams(vmem_limit_bytes=VMEM_LIMIT),
        name="final_sum",
    )(came)


def on_device(features, labels, pixel_weight, conv_weight, conv_bias, class_weight):
    image = features[0]
    band_rows, columns, channels = image.shape
    taps, width = conv_weight.shape[1:]
    pixels = band_rows * columns
    replicas = lax.axis_size("dp")
    bands = lax.axis_size("space")
    reach = DILATION_SIZE

    flat = image.reshape(pixels, channels)
    weight = conv_weight.transpose(1, 0, 2)
    middle, halo = forward(flat, weight, bands, columns, reach)
    came = lax.all_to_all(halo, "space", 0, 0)

    block_rows, cover, picks, offsets = channel_plan(channels, taps, replicas, bands)
    if block_rows % taps == 0:
        split = arrange(flat, middle, bands, replicas, cover)
    else:
        order = jnp.array([c for line in picks for c in line], jnp.int32)
        split = jnp.take(flat, order, axis=1)
        split = split.reshape(pixels, bands, replicas * cover).transpose(1, 0, 2)
    band = lax.axis_index("space")
    blocks = []
    for k in range(bands):
        block = lax.dynamic_index_in_dim(split, (band + k) % bands, keepdims=False)
        if k:
            block = lax.ppermute(block, "space", [(i, (i + k) % bands) for i in range(bands)])
        blocks.append(block)

    gradient = pointwise(
        middle,
        came,
        conv_bias.reshape(1, width),
        class_weight.T,
        labels.reshape(pixels, 1),
        pixel_weight.reshape(pixels, 1),
    )
    gathered = lax.all_to_all(gradient, "space", 0, 0)
    partial_grad = kernel_grad(gathered, blocks, columns, reach)
    came = lax.all_to_all(partial_grad.reshape(replicas, cover, taps * width), "dp", 0, 0)
    weight_grad = final(came, width)
    if block_rows % taps:
        start = jnp.array(offsets)[band, lax.axis_index("dp")]
        weight_grad = lax.dynamic_slice_in_dim(weight_grad, start, block_rows)

    grad = feature_grad(gathered, weight, columns, reach)
    return grad.reshape(1, band_rows, columns, channels), weight_grad


def solution(mesh):
    placed = (
        P("dp", "space", None, None),
        P("dp", "space", None),
        P("dp", "space", None),
        P(),
        P(),
        P(),
    )
    return jax.shard_map(
        on_device,
        mesh=mesh,
        in_specs=placed,
        out_specs=(P("dp", "space", None, None), P(("dp", "space"), None)),
        check_vma=False,
    )
```

```python
import functools

import jax
import jax.numpy as jnp
from jax import lax
from jax.experimental import pallas as pl
from jax.experimental.pallas import tpu as pltpu
from jax.sharding import PartitionSpec as P

DILATION_SIZE = 6
VMEM_LIMIT = 16 * 1024 * 1024


def channel_plan(channels, taps, replicas, bands):
    rows = channels * taps // (replicas * bands)
    starts = [[(d * bands + s) * rows // taps for d in range(replicas)] for s in range(bands)]
    offsets = [[(d * bands + s) * rows % taps for d in range(replicas)] for s in range(bands)]
    cover = max(-(-(off + rows) // taps) for line in offsets for off in line)
    picks = [[min(c + k, channels - 1) for c in line for k in range(cover)] for line in starts]
    return rows, cover, picks, offsets


def shift_columns(array, by, columns):
    if by == 0:
        return array
    size = array.shape[0]
    column = lax.broadcasted_iota(jnp.int32, array.shape, 0) % columns + by
    moved = pltpu.roll(array, (-by) % size, 0)
    return jnp.where((column >= 0) & (column < columns), moved, 0.0)


def tap_row(x, w_ref, a, columns, reach):
    width = w_ref.shape[2]
    weight = jnp.concatenate([w_ref[3 * a + b] for b in range(3)], axis=1)
    product = jnp.dot(x, weight, preferred_element_type=jnp.float32)
    return sum(
        shift_columns(product[:, b * width : (b + 1) * width], (b - 1) * reach, columns)
        for b in range(3)
    )


def halo_kernel(columns, reach, x_ref, w_ref, after_ref, down_ref, up_ref):
    del after_ref
    pixels, edge = x_ref.shape[0], reach * columns
    down_ref[...] = tap_row(x_ref[pixels - edge :], w_ref, 0, columns, reach).astype(down_ref.dtype)
    up_ref[...] = tap_row(x_ref[:edge], w_ref, 2, columns, reach).astype(up_ref.dtype)


def halo(flat, weight, after, columns, reach):
    pixels, channels = flat.shape
    width = weight.shape[2]
    edge = reach * columns
    vmem = pl.BlockSpec(memory_space=pltpu.VMEM)
    return pl.pallas_call(
        functools.partial(halo_kernel, columns, reach),
        in_specs=[vmem, vmem, pl.BlockSpec(memory_space=pltpu.HBM)],
        out_shape=[jax.ShapeDtypeStruct((edge, width), jnp.bfloat16)] * 2,
        compiler_params=pltpu.CompilerParams(vmem_limit_bytes=VMEM_LIMIT),
        cost_estimate=pl.CostEstimate(
            flops=12 * edge * channels * width,
            bytes_accessed=12 * channels * width + 2 * pixels * channels,
            transcendentals=0,
        ),
        name="halo",
    )(flat, weight, after)


def middle_kernel(columns, reach, x_ref, w_ref, after_ref, out_ref):
    del after_ref
    pixels, edge = x_ref.shape[0], reach * columns
    out_ref[...] = tap_row(x_ref[...], w_ref, 1, columns, reach)
    if pixels > edge:
        out_ref[edge:] += tap_row(x_ref[: pixels - edge], w_ref, 0, columns, reach)
        out_ref[: pixels - edge] += tap_row(x_ref[edge:], w_ref, 2, columns, reach)


def middle_taps(flat, weight, after, columns, reach):
    pixels, channels = flat.shape
    width = weight.shape[2]
    vmem = pl.BlockSpec(memory_space=pltpu.VMEM)
    return pl.pallas_call(
        functools.partial(middle_kernel, columns, reach),
        in_specs=[vmem, vmem, pl.BlockSpec(memory_space=pl.ANY)],
        out_shape=jax.ShapeDtypeStruct((pixels, width), jnp.float32),
        compiler_params=pltpu.CompilerParams(vmem_limit_bytes=VMEM_LIMIT),
        cost_estimate=pl.CostEstimate(
            flops=6 * pixels * channels * width,
            bytes_accessed=6 * channels * width + 2 * pixels * channels,
            transcendentals=0,
        ),
        name="middle_taps",
    )(flat, weight, after)


def arrange_kernel(replicas, cover, x_ref, out_ref, room, sems):
    bands = out_ref.shape[0]
    x = x_ref[...]
    copies = [pltpu.make_async_copy(room.at[s], out_ref.at[s], sems.at[s]) for s in range(bands)]
    for s in range(bands):
        room[s] = jnp.concatenate(
            [x[:, (d * bands + s) * cover : (d * bands + s + 1) * cover] for d in range(replicas)],
            axis=1,
        )
        copies[s].start()
    for copy in copies:
        copy.wait()


def arrange(flat, bands, replicas, cover):
    pixels, channels = flat.shape
    shape = (bands, pixels, replicas * cover)
    return pl.pallas_call(
        functools.partial(arrange_kernel, replicas, cover),
        in_specs=[pl.BlockSpec(memory_space=pltpu.VMEM)],
        out_specs=pl.BlockSpec(memory_space=pltpu.HBM),
        out_shape=jax.ShapeDtypeStruct(shape, flat.dtype),
        scratch_shapes=[pltpu.VMEM(shape, flat.dtype), pltpu.SemaphoreType.DMA((bands,))],
        compiler_params=pltpu.CompilerParams(vmem_limit_bytes=VMEM_LIMIT),
        cost_estimate=pl.CostEstimate(
            flops=0, bytes_accessed=4 * pixels * channels, transcendentals=0
        ),
        name="arrange",
    )(flat)


def pointwise_kernel(
    middle_ref, above_ref, below_ref, bias_ref, class_ref, label_ref, scale_ref, after_ref,
    out_ref, room, sems
):
    del after_ref
    bands = out_ref.shape[0]
    pixels, width = middle_ref.shape
    edge = above_ref.shape[0]
    above = above_ref[...].astype(jnp.float32)
    below = below_ref[...].astype(jnp.float32)
    if pixels > edge:
        none = jnp.zeros((pixels - edge, width), jnp.float32)
        above = jnp.concatenate([above, none], axis=0)
        below = jnp.concatenate([none, below], axis=0)
    preact = middle_ref[...] + above + below + bias_ref[...]
    sigmoid_z = jax.nn.sigmoid(preact)
    hidden = (preact * sigmoid_z).astype(jnp.bfloat16)
    classes = class_ref[...]
    logits = lax.dot_general(
        hidden, classes, (((1,), (1,)), ((), ())), preferred_element_type=jnp.float32
    )
    exponent = jnp.exp(logits)
    chances = exponent / jnp.sum(exponent, axis=1, keepdims=True)
    index = lax.broadcasted_iota(jnp.int32, chances.shape, 1)
    onehot = jnp.where(label_ref[...] == index, 1.0, 0.0)
    grad_logits = scale_ref[...].astype(jnp.float32) * (chances - onehot)
    wide = classes.astype(jnp.float32)
    hidden_grad = sum(
        grad_logits[:, k : k + 1] * wide[k : k + 1] for k in range(classes.shape[0])
    )
    gradient = hidden_grad * sigmoid_z * (1.0 + preact * (1.0 - sigmoid_z))
    room[...] = gradient.astype(out_ref.dtype)
    copies = [pltpu.make_async_copy(room, out_ref.at[s], sems.at[s]) for s in range(bands)]
    for copy in copies:
        copy.start()
    for copy in copies:
        copy.wait()


def pointwise(middle, above, below, bias, classes, labels, scale, after, bands):
    pixels, width = middle.shape
    vmem = pl.BlockSpec(memory_space=pltpu.VMEM)
    return pl.pallas_call(
        pointwise_kernel,
        in_specs=[vmem] * 7 + [pl.BlockSpec(memory_space=pl.ANY)],
        out_specs=pl.BlockSpec(memory_space=pltpu.HBM),
        out_shape=jax.ShapeDtypeStruct((bands, pixels, width), jnp.bfloat16),
        scratch_shapes=[
            pltpu.VMEM((pixels, width), jnp.bfloat16),
            pltpu.SemaphoreType.DMA((bands,)),
        ],
        compiler_params=pltpu.CompilerParams(vmem_limit_bytes=VMEM_LIMIT),
        cost_estimate=pl.CostEstimate(
            flops=30 * pixels * width,
            bytes_accessed=2 * bands * pixels * width + 8 * pixels * width,
            transcendentals=pixels * width,
        ),
        name="pointwise",
    )(middle, above, below, bias, classes, labels, scale, after)


def shifted_taps(gradient, columns, reach):
    wide = gradient.astype(jnp.float32)
    return jnp.concatenate(
        [shift_columns(wide, (1 - b) * reach, columns).astype(jnp.bfloat16) for b in range(3)],
        axis=1,
    )


def kernel_grad_kernel(columns, reach, g_ref, x_ref, out_ref, room, sems):
    bands, pixels, width = g_ref.shape
    total = bands * pixels
    edge = reach * columns
    shifted = shifted_taps(g_ref[...].reshape(total, width), columns, reach)
    features = x_ref[...].reshape(total, x_ref.shape[2])
    copies = []
    for a in range(3):
        if a == 0:
            left, right = features[: total - edge], shifted[edge:]
        elif a == 1:
            left, right = features, shifted
        else:
            left, right = features[edge:], shifted[: total - edge]
        block = lax.dot_general(
            left, right, (((0,), (0,)), ((), ())), preferred_element_type=jnp.float32
        )
        room[a] = block.astype(room.dtype)
        lanes = pl.ds(3 * a * width, 3 * width)
        copies.append(pltpu.make_async_copy(room.at[a], out_ref.at[:, lanes], sems.at[a]))
        copies[-1].start()
    for copy in copies:
        copy.wait()


def kernel_grad(gathered, features, columns, reach):
    bands, pixels, width = gathered.shape
    extra = features.shape[2]
    vmem = pl.BlockSpec(memory_space=pltpu.VMEM)
    return pl.pallas_call(
        functools.partial(kernel_grad_kernel, columns, reach),
        in_specs=[vmem, vmem],
        out_specs=pl.BlockSpec(memory_space=pltpu.HBM),
        out_shape=jax.ShapeDtypeStruct((extra, 9 * width), jnp.bfloat16),
        scratch_shapes=[
            pltpu.VMEM((3, extra, 3 * width), jnp.bfloat16),
            pltpu.SemaphoreType.DMA((3,)),
        ],
        compiler_params=pltpu.CompilerParams(vmem_limit_bytes=VMEM_LIMIT),
        cost_estimate=pl.CostEstimate(
            flops=18 * bands * pixels * extra * width,
            bytes_accessed=2 * bands * pixels * (width + extra) + 18 * extra * width,
            transcendentals=0,
        ),
        name="kernel_grad",
    )(gathered, features)


def feature_grad_kernel(columns, reach, g_ref, w_ref, out_ref):
    band = lax.axis_index("space")
    bands, pixels, width = g_ref.shape
    edge = reach * columns
    own = g_ref[band]
    above = g_ref[jnp.maximum(band - 1, 0)][pixels - edge :]
    below = g_ref[jnp.minimum(band + 1, bands - 1)][:edge]
    above = jnp.where(band > 0, above, jnp.zeros_like(above))
    below = jnp.where(band + 1 < bands, below, jnp.zeros_like(below))
    stack = shifted_taps(jnp.concatenate([above, own, below], axis=0), columns, reach)
    taps = jnp.concatenate(
        [stack[(2 - a) * edge : (2 - a) * edge + pixels] for a in range(3)], axis=1
    )
    weight = jnp.concatenate([w_ref[t] for t in range(9)], axis=1)
    out_ref[...] = lax.dot_general(
        taps, weight, (((1,), (1,)), ((), ())), preferred_element_type=jnp.float32
    )


def feature_grad(gathered, weight, columns, reach):
    bands, pixels, _ = gathered.shape
    taps, channels, width = weight.shape
    step = 256 if channels % 256 == 0 else channels
    return pl.pallas_call(
        functools.partial(feature_grad_kernel, columns, reach),
        grid=(channels // step,),
        in_specs=[
            pl.BlockSpec((bands, pixels, width), lambda i: (0, 0, 0)),
            pl.BlockSpec((taps, step, width), lambda i: (0, i, 0)),
        ],
        out_specs=pl.BlockSpec((pixels, step), lambda i: (0, i)),
        out_shape=jax.ShapeDtypeStruct((pixels, channels), jnp.float32),
        compiler_params=pltpu.CompilerParams(vmem_limit_bytes=VMEM_LIMIT),
        cost_estimate=pl.CostEstimate(
            flops=2 * pixels * taps * channels * width,
            bytes_accessed=2 * taps * channels * width + 4 * pixels * channels,
            transcendentals=0,
        ),
        name="feature_grad",
    )(gathered, weight)


def final_kernel(in_ref, out_ref):
    replicas, cover, lanes = in_ref.shape
    width = out_ref.shape[1]
    taps = lanes // width
    total = in_ref[0].astype(jnp.float32)
    for d in range(1, replicas):
        total += in_ref[d].astype(jnp.float32)
    total = total / replicas
    for t in range(taps):
        out_ref[pl.ds(t, cover, stride=taps), :] = total[:, t * width : (t + 1) * width]


def final(came, width):
    replicas, cover, lanes = came.shape
    return pl.pallas_call(
        final_kernel,
        out_shape=jax.ShapeDtypeStruct((cover * lanes // width, width), jnp.float32),
        compiler_params=pltpu.CompilerParams(vmem_limit_bytes=VMEM_LIMIT),
        name="final_sum",
    )(came)


def on_device(features, labels, pixel_weight, conv_weight, conv_bias, class_weight):
    image = features[0]
    band_rows, columns, channels = image.shape
    taps, width = conv_weight.shape[1:]
    pixels = band_rows * columns
    replicas = lax.axis_size("dp")
    bands = lax.axis_size("space")
    reach = DILATION_SIZE

    flat = image.reshape(pixels, channels)
    weight = conv_weight.transpose(1, 0, 2)
    block_rows, cover, picks, offsets = channel_plan(channels, taps, replicas, bands)
    if block_rows % taps == 0:
        split = arrange(flat, bands, replicas, cover)
    else:
        order = jnp.array([c for line in picks for c in line], jnp.int32)
        split = jnp.take(flat, order, axis=1)
        split = split.reshape(pixels, bands, replicas * cover).transpose(1, 0, 2)
    whole = lax.all_to_all(split, "space", 0, 0)

    down, up = halo(flat, weight, split, columns, reach)
    above = lax.ppermute(down, "space", [(i, i + 1) for i in range(bands - 1)])
    below = lax.ppermute(up, "space", [(i + 1, i) for i in range(bands - 1)])
    middle = middle_taps(flat, weight, up, columns, reach)

    gradient = pointwise(
        middle,
        above,
        below,
        conv_bias.reshape(1, width),
        class_weight.T,
        labels.reshape(pixels, 1),
        pixel_weight.reshape(pixels, 1),
        whole,
        bands,
    )
    gathered = lax.all_to_all(gradient, "space", 0, 0)
    partial_grad = kernel_grad(gathered, whole, columns, reach)
    came = lax.all_to_all(partial_grad.reshape(replicas, cover, taps * width), "dp", 0, 0)
    weight_grad = final(came, width)
    if block_rows % taps:
        start = jnp.array(offsets)[lax.axis_index("space"), lax.axis_index("dp")]
        weight_grad = lax.dynamic_slice_in_dim(weight_grad, start, block_rows)

    grad = feature_grad(gathered, weight, columns, reach)
    return grad.reshape(1, band_rows, columns, channels), weight_grad


def solution(mesh):
    placed = (
        P("dp", "space", None, None),
        P("dp", "space", None),
        P("dp", "space", None),
        P(),
        P(),
        P(),
    )
    return jax.shard_map(
        on_device,
        mesh=mesh,
        in_specs=placed,
        out_specs=(P("dp", "space", None, None), P(("dp", "space"), None)),
        check_vma=False,
    )
```

```python
import functools

import jax
import jax.numpy as jnp
from jax import lax
from jax.experimental import pallas as pl
from jax.experimental.pallas import tpu as pltpu
from jax.sharding import PartitionSpec as P

DILATION_SIZE = 6
VMEM_LIMIT = 16 * 1024 * 1024
VMEM_WHOLE = 62 * 1024 * 1024


def channel_plan(channels, taps, replicas, bands):
    rows = channels * taps // (replicas * bands)
    starts = [[(d * bands + s) * rows // taps for d in range(replicas)] for s in range(bands)]
    offsets = [[(d * bands + s) * rows % taps for d in range(replicas)] for s in range(bands)]
    cover = max(-(-(off + rows) // taps) for line in offsets for off in line)
    picks = [[min(c + k, channels - 1) for c in line for k in range(cover)] for line in starts]
    return rows, cover, picks, offsets


def shift_columns(array, by, columns):
    if by == 0:
        return array
    size = array.shape[0]
    column = lax.broadcasted_iota(jnp.int32, array.shape, 0) % columns + by
    moved = pltpu.roll(array, (-by) % size, 0)
    return jnp.where((column >= 0) & (column < columns), moved, 0.0)


def tap_row(x, w_ref, a, columns, reach):
    width = w_ref.shape[2]
    weight = jnp.concatenate([w_ref[3 * a + b] for b in range(3)], axis=1)
    product = jnp.dot(x, weight, preferred_element_type=jnp.float32)
    return sum(
        shift_columns(product[:, b * width : (b + 1) * width], (b - 1) * reach, columns)
        for b in range(3)
    )


def prepare_kernel(
    columns, reach, replicas, cover, x_hbm, w_hbm, *refs
):
    outs, (x_ref, w_ref, room, halo, x_sem, w_sems, out_sems, halo_sems) = refs[:-8], refs[-8:]
    down_hbm, up_hbm = outs[:2]
    pixels, edge = x_ref.shape[0], reach * columns
    load = pltpu.make_async_copy(x_hbm, x_ref, x_sem)
    load.start()
    rows = [0, 2]
    loads = [
        pltpu.make_async_copy(w_hbm.at[pl.ds(3 * a, 3)], w_ref.at[pl.ds(3 * a, 3)], w_sems.at[a])
        for a in rows
    ]
    for copy in loads:
        copy.start()
    load.wait()
    copies = []
    if len(outs) == 3:
        x = x_ref[...]
        bands = room.shape[0]
        for s in range(bands):
            room[s] = jnp.concatenate(
                [x[:, (d * bands + s) * cover : (d * bands + s + 1) * cover] for d in range(replicas)],
                axis=1,
            )
            copies.append(pltpu.make_async_copy(room.at[s], outs[2].at[s], out_sems.at[s]))
            copies[-1].start()
    for k, a in enumerate(rows):
        loads[k].wait()
        x = x_ref[pixels - edge :] if a == 0 else x_ref[:edge]
        halo[k] = tap_row(x, w_ref, a, columns, reach).astype(halo.dtype)
        copies.append(pltpu.make_async_copy(halo.at[k], (down_hbm, up_hbm)[k], halo_sems.at[k]))
        copies[-1].start()
    for copy in copies:
        copy.wait()


def prepare(flat, weight, columns, reach, bands, replicas, cover, blocks):
    pixels, channels = flat.shape
    taps, _, width = weight.shape
    edge = reach * columns
    hbm = pl.BlockSpec(memory_space=pltpu.HBM)
    shape = (bands, pixels, replicas * cover)
    out_shape = [jax.ShapeDtypeStruct((edge, width), jnp.bfloat16)] * 2
    if blocks:
        out_shape.append(jax.ShapeDtypeStruct(shape, flat.dtype))
    return pl.pallas_call(
        functools.partial(prepare_kernel, columns, reach, replicas, cover),
        in_specs=[hbm, hbm],
        out_specs=[hbm] * len(out_shape),
        out_shape=out_shape,
        scratch_shapes=[
            pltpu.VMEM((pixels, channels), flat.dtype),
            pltpu.VMEM((taps, channels, width), weight.dtype),
            pltpu.VMEM(shape, flat.dtype),
            pltpu.VMEM((2, edge, width), jnp.bfloat16),
            pltpu.SemaphoreType.DMA,
            pltpu.SemaphoreType.DMA((3,)),
            pltpu.SemaphoreType.DMA((bands,)),
            pltpu.SemaphoreType.DMA((2,)),
        ],
        compiler_params=pltpu.CompilerParams(vmem_limit_bytes=VMEM_WHOLE),
        cost_estimate=pl.CostEstimate(
            flops=12 * edge * channels * width,
            bytes_accessed=12 * channels * width + 6 * pixels * channels,
            transcendentals=0,
        ),
        name="prepare",
    )(flat, weight)


def middle_kernel(columns, reach, x_ref, w_ref, after_ref, out_ref):
    del after_ref
    pixels, edge = x_ref.shape[0], reach * columns
    out_ref[...] = tap_row(x_ref[...], w_ref, 1, columns, reach)
    if pixels > edge:
        out_ref[edge:] += tap_row(x_ref[: pixels - edge], w_ref, 0, columns, reach)
        out_ref[: pixels - edge] += tap_row(x_ref[edge:], w_ref, 2, columns, reach)


def middle_taps(flat, weight, after, columns, reach):
    pixels, channels = flat.shape
    width = weight.shape[2]
    vmem = pl.BlockSpec(memory_space=pltpu.VMEM)
    return pl.pallas_call(
        functools.partial(middle_kernel, columns, reach),
        in_specs=[vmem, vmem, pl.BlockSpec(memory_space=pl.ANY)],
        out_shape=jax.ShapeDtypeStruct((pixels, width), jnp.float32),
        compiler_params=pltpu.CompilerParams(vmem_limit_bytes=VMEM_LIMIT),
        cost_estimate=pl.CostEstimate(
            flops=6 * pixels * channels * width,
            bytes_accessed=6 * channels * width + 2 * pixels * channels,
            transcendentals=0,
        ),
        name="middle_taps",
    )(flat, weight, after)


def pointwise_kernel(
    middle_ref, above_ref, below_ref, bias_ref, class_ref, label_ref, scale_ref, after_ref,
    out_ref, room, sems
):
    del after_ref
    bands = out_ref.shape[0]
    pixels, width = middle_ref.shape
    edge = above_ref.shape[0]
    above = above_ref[...].astype(jnp.float32)
    below = below_ref[...].astype(jnp.float32)
    if pixels > edge:
        none = jnp.zeros((pixels - edge, width), jnp.float32)
        above = jnp.concatenate([above, none], axis=0)
        below = jnp.concatenate([none, below], axis=0)
    preact = middle_ref[...] + above + below + bias_ref[...]
    sigmoid_z = jax.nn.sigmoid(preact)
    hidden = (preact * sigmoid_z).astype(jnp.bfloat16)
    classes = class_ref[...]
    logits = lax.dot_general(
        hidden, classes, (((1,), (1,)), ((), ())), preferred_element_type=jnp.float32
    )
    exponent = jnp.exp(logits)
    chances = exponent / jnp.sum(exponent, axis=1, keepdims=True)
    index = lax.broadcasted_iota(jnp.int32, chances.shape, 1)
    onehot = jnp.where(label_ref[...] == index, 1.0, 0.0)
    grad_logits = scale_ref[...].astype(jnp.float32) * (chances - onehot)
    wide = classes.astype(jnp.float32)
    hidden_grad = sum(
        grad_logits[:, k : k + 1] * wide[k : k + 1] for k in range(classes.shape[0])
    )
    gradient = hidden_grad * sigmoid_z * (1.0 + preact * (1.0 - sigmoid_z))
    room[...] = gradient.astype(out_ref.dtype)
    copies = [pltpu.make_async_copy(room, out_ref.at[s], sems.at[s]) for s in range(bands)]
    for copy in copies:
        copy.start()
    for copy in copies:
        copy.wait()


def pointwise(middle, above, below, bias, classes, labels, scale, after, bands):
    pixels, width = middle.shape
    vmem = pl.BlockSpec(memory_space=pltpu.VMEM)
    return pl.pallas_call(
        pointwise_kernel,
        in_specs=[vmem] * 7 + [pl.BlockSpec(memory_space=pl.ANY)],
        out_specs=pl.BlockSpec(memory_space=pltpu.HBM),
        out_shape=jax.ShapeDtypeStruct((bands, pixels, width), jnp.bfloat16),
        scratch_shapes=[
            pltpu.VMEM((pixels, width), jnp.bfloat16),
            pltpu.SemaphoreType.DMA((bands,)),
        ],
        compiler_params=pltpu.CompilerParams(vmem_limit_bytes=VMEM_LIMIT),
        cost_estimate=pl.CostEstimate(
            flops=30 * pixels * width,
            bytes_accessed=2 * bands * pixels * width + 8 * pixels * width,
            transcendentals=pixels * width,
        ),
        name="pointwise",
    )(middle, above, below, bias, classes, labels, scale, after)


def shifted_taps(gradient, columns, reach):
    wide = gradient.astype(jnp.float32)
    return jnp.concatenate(
        [shift_columns(wide, (1 - b) * reach, columns).astype(jnp.bfloat16) for b in range(3)],
        axis=1,
    )


def kernel_grad_kernel(columns, reach, g_ref, x_ref, out_ref):
    bands, pixels, width = g_ref.shape
    total = bands * pixels
    edge = reach * columns
    shifted = shifted_taps(g_ref[...].reshape(total, width), columns, reach)
    features = x_ref[...].reshape(total, x_ref.shape[2])
    for a in range(3):
        if a == 0:
            left, right = features[: total - edge], shifted[edge:]
        elif a == 1:
            left, right = features, shifted
        else:
            left, right = features[edge:], shifted[: total - edge]
        block = lax.dot_general(
            left, right, (((0,), (0,)), ((), ())), preferred_element_type=jnp.float32
        )
        out_ref[:, 3 * a * width : 3 * (a + 1) * width] = block.astype(out_ref.dtype)


def kernel_grad(gathered, features, columns, reach):
    bands, pixels, width = gathered.shape
    extra = features.shape[2]
    return pl.pallas_call(
        functools.partial(kernel_grad_kernel, columns, reach),
        out_shape=jax.ShapeDtypeStruct((extra, 9 * width), jnp.bfloat16),
        compiler_params=pltpu.CompilerParams(vmem_limit_bytes=VMEM_LIMIT),
        cost_estimate=pl.CostEstimate(
            flops=18 * bands * pixels * extra * width,
            bytes_accessed=2 * bands * pixels * (width + extra) + 18 * extra * width,
            transcendentals=0,
        ),
        name="kernel_grad",
    )(gathered, features)


def feature_grad_kernel(columns, reach, g_ref, w_ref, out_ref):
    band = lax.axis_index("space")
    bands, pixels, width = g_ref.shape
    edge = reach * columns
    own = g_ref[band]
    above = g_ref[jnp.maximum(band - 1, 0)][pixels - edge :]
    below = g_ref[jnp.minimum(band + 1, bands - 1)][:edge]
    above = jnp.where(band > 0, above, jnp.zeros_like(above))
    below = jnp.where(band + 1 < bands, below, jnp.zeros_like(below))
    stack = shifted_taps(jnp.concatenate([above, own, below], axis=0), columns, reach)
    taps = jnp.concatenate(
        [stack[(2 - a) * edge : (2 - a) * edge + pixels] for a in range(3)], axis=1
    )
    weight = jnp.concatenate([w_ref[t] for t in range(9)], axis=1)
    out_ref[...] = lax.dot_general(
        taps, weight, (((1,), (1,)), ((), ())), preferred_element_type=jnp.float32
    )


def feature_grad(gathered, weight, columns, reach):
    bands, pixels, _ = gathered.shape
    taps, channels, width = weight.shape
    step = 256 if channels % 256 == 0 else channels
    return pl.pallas_call(
        functools.partial(feature_grad_kernel, columns, reach),
        grid=(channels // step,),
        in_specs=[
            pl.BlockSpec((bands, pixels, width), lambda i: (0, 0, 0)),
            pl.BlockSpec((taps, step, width), lambda i: (0, i, 0)),
        ],
        out_specs=pl.BlockSpec((pixels, step), lambda i: (0, i)),
        out_shape=jax.ShapeDtypeStruct((pixels, channels), jnp.float32),
        compiler_params=pltpu.CompilerParams(vmem_limit_bytes=VMEM_LIMIT),
        cost_estimate=pl.CostEstimate(
            flops=2 * pixels * taps * channels * width,
            bytes_accessed=2 * taps * channels * width + 4 * pixels * channels,
            transcendentals=0,
        ),
        name="feature_grad",
    )(gathered, weight)


def final_kernel(in_ref, out_ref):
    replicas, cover, lanes = in_ref.shape
    width = out_ref.shape[1]
    taps = lanes // width
    total = in_ref[0].astype(jnp.float32)
    for d in range(1, replicas):
        total += in_ref[d].astype(jnp.float32)
    total = total / replicas
    for t in range(taps):
        out_ref[pl.ds(t, cover, stride=taps), :] = total[:, t * width : (t + 1) * width]


def final(came, width):
    replicas, cover, lanes = came.shape
    return pl.pallas_call(
        final_kernel,
        out_shape=jax.ShapeDtypeStruct((cover * lanes // width, width), jnp.float32),
        compiler_params=pltpu.CompilerParams(vmem_limit_bytes=VMEM_LIMIT),
        name="final_sum",
    )(came)


def on_device(features, labels, pixel_weight, conv_weight, conv_bias, class_weight):
    image = features[0]
    band_rows, columns, channels = image.shape
    taps, width = conv_weight.shape[1:]
    pixels = band_rows * columns
    replicas = lax.axis_size("dp")
    bands = lax.axis_size("space")
    reach = DILATION_SIZE

    flat = image.reshape(pixels, channels)
    weight = conv_weight.transpose(1, 0, 2)
    block_rows, cover, picks, offsets = channel_plan(channels, taps, replicas, bands)
    even = block_rows % taps == 0
    down, up, *split = prepare(flat, weight, columns, reach, bands, replicas, cover, even)
    if not even:
        order = jnp.array([c for line in picks for c in line], jnp.int32)
        blocks = jnp.take(flat, order, axis=1).reshape(pixels, bands, replicas * cover)
        split = [blocks.transpose(1, 0, 2)]
    whole = lax.all_to_all(split[0], "space", 0, 0)

    above = lax.ppermute(down, "space", [(i, i + 1) for i in range(bands - 1)])
    below = lax.ppermute(up, "space", [(i + 1, i) for i in range(bands - 1)])
    middle = middle_taps(flat, weight, up, columns, reach)

    gradient = pointwise(
        middle,
        above,
        below,
        conv_bias.reshape(1, width),
        class_weight.T,
        labels.reshape(pixels, 1),
        pixel_weight.reshape(pixels, 1),
        whole,
        bands,
    )
    gathered = lax.all_to_all(gradient, "space", 0, 0)
    partial_grad = kernel_grad(gathered, whole, columns, reach)
    came = lax.all_to_all(partial_grad.reshape(replicas, cover, taps * width), "dp", 0, 0)
    weight_grad = final(came, width)
    if not even:
        start = jnp.array(offsets)[lax.axis_index("space"), lax.axis_index("dp")]
        weight_grad = lax.dynamic_slice_in_dim(weight_grad, start, block_rows)

    grad = feature_grad(gathered, weight, columns, reach)
    return grad.reshape(1, band_rows, columns, channels), weight_grad


def solution(mesh):
    placed = (
        P("dp", "space", None, None),
        P("dp", "space", None),
        P("dp", "space", None),
        P(),
        P(),
        P(),
    )
    return jax.shard_map(
        on_device,
        mesh=mesh,
        in_specs=placed,
        out_specs=(P("dp", "space", None, None), P(("dp", "space"), None)),
        check_vma=False,
    )
```

```python
import functools

import jax
import jax.numpy as jnp
from jax import lax
from jax.experimental import pallas as pl
from jax.experimental.pallas import tpu as pltpu
from jax.sharding import PartitionSpec as P

DILATION_SIZE = 6
VMEM_LIMIT = 16 * 1024 * 1024
VMEM_WHOLE = 62 * 1024 * 1024


def channel_plan(channels, taps, replicas, bands):
    rows = channels * taps // (replicas * bands)
    starts = [[(d * bands + s) * rows // taps for d in range(replicas)] for s in range(bands)]
    offsets = [[(d * bands + s) * rows % taps for d in range(replicas)] for s in range(bands)]
    cover = max(-(-(off + rows) // taps) for line in offsets for off in line)
    picks = [[min(c + k, channels - 1) for c in line for k in range(cover)] for line in starts]
    return rows, cover, picks, offsets


def shift_columns(array, by, columns):
    if by == 0:
        return array
    size = array.shape[0]
    column = lax.broadcasted_iota(jnp.int32, array.shape, 0) % columns + by
    moved = pltpu.roll(array, (-by) % size, 0)
    return jnp.where((column >= 0) & (column < columns), moved, 0.0)


def tap_row(x, w_ref, a, columns, reach):
    width = w_ref.shape[2]
    weight = jnp.concatenate([w_ref[3 * a + b] for b in range(3)], axis=1)
    product = jnp.dot(x, weight, preferred_element_type=jnp.float32)
    return sum(
        shift_columns(product[:, b * width : (b + 1) * width], (b - 1) * reach, columns)
        for b in range(3)
    )


def prepare_kernel(
    columns, reach, replicas, cover, x_hbm, w_hbm, *refs
):
    outs, (x_ref, w_ref, room, halo, x_sem, w_sems, out_sems, halo_sems) = refs[:-8], refs[-8:]
    down_hbm, up_hbm = outs[:2]
    pixels, edge = x_ref.shape[0], reach * columns
    load = pltpu.make_async_copy(x_hbm, x_ref, x_sem)
    load.start()
    rows = [0, 2]
    loads = [
        pltpu.make_async_copy(w_hbm.at[pl.ds(3 * a, 3)], w_ref.at[pl.ds(3 * a, 3)], w_sems.at[a])
        for a in rows
    ]
    for copy in loads:
        copy.start()
    load.wait()
    copies = []
    if len(outs) == 3:
        x = x_ref[...]
        bands = room.shape[0]
        for s in range(bands):
            room[s] = jnp.concatenate(
                [x[:, (d * bands + s) * cover : (d * bands + s + 1) * cover] for d in range(replicas)],
                axis=1,
            )
            copies.append(pltpu.make_async_copy(room.at[s], outs[2].at[s], out_sems.at[s]))
            copies[-1].start()
    for k, a in enumerate(rows):
        loads[k].wait()
        x = x_ref[pixels - edge :] if a == 0 else x_ref[:edge]
        halo[k] = tap_row(x, w_ref, a, columns, reach).astype(halo.dtype)
        copies.append(pltpu.make_async_copy(halo.at[k], (down_hbm, up_hbm)[k], halo_sems.at[k]))
        copies[-1].start()
    for copy in copies:
        copy.wait()


def prepare(flat, weight, columns, reach, bands, replicas, cover, blocks):
    pixels, channels = flat.shape
    taps, _, width = weight.shape
    edge = reach * columns
    hbm = pl.BlockSpec(memory_space=pltpu.HBM)
    shape = (bands, pixels, replicas * cover)
    out_shape = [jax.ShapeDtypeStruct((edge, width), jnp.bfloat16)] * 2
    if blocks:
        out_shape.append(jax.ShapeDtypeStruct(shape, flat.dtype))
    return pl.pallas_call(
        functools.partial(prepare_kernel, columns, reach, replicas, cover),
        in_specs=[hbm, hbm],
        out_specs=[hbm] * len(out_shape),
        out_shape=out_shape,
        scratch_shapes=[
            pltpu.VMEM((pixels, channels), flat.dtype),
            pltpu.VMEM((taps, channels, width), weight.dtype),
            pltpu.VMEM(shape, flat.dtype),
            pltpu.VMEM((2, edge, width), jnp.bfloat16),
            pltpu.SemaphoreType.DMA,
            pltpu.SemaphoreType.DMA((3,)),
            pltpu.SemaphoreType.DMA((bands,)),
            pltpu.SemaphoreType.DMA((2,)),
        ],
        compiler_params=pltpu.CompilerParams(vmem_limit_bytes=VMEM_WHOLE),
        cost_estimate=pl.CostEstimate(
            flops=12 * edge * channels * width,
            bytes_accessed=12 * channels * width + 6 * pixels * channels,
            transcendentals=0,
        ),
        name="prepare",
    )(flat, weight)


def pass_on_kernel(x_ref, after_ref, out_ref):
    del x_ref, after_ref, out_ref


def pass_on(x, after):
    hbm = pl.BlockSpec(memory_space=pltpu.HBM)
    return pl.pallas_call(
        pass_on_kernel,
        in_specs=[hbm, pl.BlockSpec(memory_space=pl.ANY)],
        out_specs=hbm,
        out_shape=jax.ShapeDtypeStruct(x.shape, x.dtype),
        input_output_aliases={0: 0},
        name="pass_on",
    )(x, after)


def middle_kernel(columns, reach, x_ref, w_ref, after_ref, out_ref):
    del after_ref
    pixels, edge = x_ref.shape[0], reach * columns
    out_ref[...] = tap_row(x_ref[...], w_ref, 1, columns, reach)
    if pixels > edge:
        out_ref[edge:] += tap_row(x_ref[: pixels - edge], w_ref, 0, columns, reach)
        out_ref[: pixels - edge] += tap_row(x_ref[edge:], w_ref, 2, columns, reach)


def middle_taps(flat, weight, after, columns, reach):
    pixels, channels = flat.shape
    width = weight.shape[2]
    vmem = pl.BlockSpec(memory_space=pltpu.VMEM)
    return pl.pallas_call(
        functools.partial(middle_kernel, columns, reach),
        in_specs=[vmem, vmem, pl.BlockSpec(memory_space=pl.ANY)],
        out_shape=jax.ShapeDtypeStruct((pixels, width), jnp.float32),
        compiler_params=pltpu.CompilerParams(vmem_limit_bytes=VMEM_LIMIT),
        cost_estimate=pl.CostEstimate(
            flops=6 * pixels * channels * width,
            bytes_accessed=6 * channels * width + 2 * pixels * channels,
            transcendentals=0,
        ),
        name="middle_taps",
    )(flat, weight, after)


def pointwise_kernel(
    middle_ref, above_ref, below_ref, bias_ref, class_ref, label_ref, scale_ref, out_ref
):
    pixels, width = middle_ref.shape
    edge = above_ref.shape[0]
    above = above_ref[...].astype(jnp.float32)
    below = below_ref[...].astype(jnp.float32)
    if pixels > edge:
        none = jnp.zeros((pixels - edge, width), jnp.float32)
        above = jnp.concatenate([above, none], axis=0)
        below = jnp.concatenate([none, below], axis=0)
    preact = middle_ref[...] + above + below + bias_ref[...]
    sigmoid_z = jax.nn.sigmoid(preact)
    hidden = (preact * sigmoid_z).astype(jnp.bfloat16)
    classes = class_ref[...]
    logits = lax.dot_general(
        hidden, classes, (((1,), (1,)), ((), ())), preferred_element_type=jnp.float32
    )
    exponent = jnp.exp(logits)
    chances = exponent / jnp.sum(exponent, axis=1, keepdims=True)
    index = lax.broadcasted_iota(jnp.int32, chances.shape, 1)
    onehot = jnp.where(label_ref[...] == index, 1.0, 0.0)
    grad_logits = scale_ref[...].astype(jnp.float32) * (chances - onehot)
    wide = classes.astype(jnp.float32)
    hidden_grad = sum(
        grad_logits[:, k : k + 1] * wide[k : k + 1] for k in range(classes.shape[0])
    )
    gradient = hidden_grad * sigmoid_z * (1.0 + preact * (1.0 - sigmoid_z))
    out_ref[...] = gradient.astype(out_ref.dtype)


def pointwise(middle, above, below, bias, classes, labels, scale):
    pixels, width = middle.shape
    return pl.pallas_call(
        pointwise_kernel,
        out_shape=jax.ShapeDtypeStruct((pixels, width), jnp.bfloat16),
        compiler_params=pltpu.CompilerParams(vmem_limit_bytes=VMEM_LIMIT),
        cost_estimate=pl.CostEstimate(
            flops=30 * pixels * width,
            bytes_accessed=10 * pixels * width,
            transcendentals=pixels * width,
        ),
        name="pointwise",
    )(middle, above, below, bias, classes, labels, scale)


def shifted_taps(gradient, columns, reach):
    wide = gradient.astype(jnp.float32)
    return jnp.concatenate(
        [shift_columns(wide, (1 - b) * reach, columns).astype(jnp.bfloat16) for b in range(3)],
        axis=1,
    )


def kernel_grad_kernel(columns, reach, x_ref, *refs):
    *g_refs, out_ref, taps = refs
    bands, pixels, _ = x_ref.shape
    width = g_refs[0].shape[1]
    total = bands * pixels
    edge = reach * columns
    band = lax.axis_index("space")
    for k, g_ref in enumerate(g_refs):
        first = lax.rem(band + bands - k, bands) * pixels
        taps[pl.ds(pl.multiple_of(first, 16), pixels)] = shifted_taps(g_ref[...], columns, reach)
    features = x_ref[...].reshape(total, x_ref.shape[2])
    for a in range(3):
        if a == 0:
            left, right = features[: total - edge], taps[edge:]
        elif a == 1:
            left, right = features, taps[...]
        else:
            left, right = features[edge:], taps[: total - edge]
        block = lax.dot_general(
            left, right, (((0,), (0,)), ((), ())), preferred_element_type=jnp.float32
        )
        out_ref[:, 3 * a * width : 3 * (a + 1) * width] = block.astype(out_ref.dtype)


def kernel_grad(features, gradients, columns, reach):
    bands, pixels, extra = features.shape
    width = gradients[0].shape[1]
    return pl.pallas_call(
        functools.partial(kernel_grad_kernel, columns, reach),
        out_shape=jax.ShapeDtypeStruct((extra, 9 * width), jnp.bfloat16),
        scratch_shapes=[pltpu.VMEM((bands * pixels, 3 * width), jnp.bfloat16)],
        compiler_params=pltpu.CompilerParams(vmem_limit_bytes=VMEM_LIMIT),
        cost_estimate=pl.CostEstimate(
            flops=18 * bands * pixels * extra * width,
            bytes_accessed=2 * bands * pixels * (width + extra) + 18 * extra * width,
            transcendentals=0,
        ),
        name="kernel_grad",
    )(features, *gradients)


def feature_grad_kernel(columns, reach, bands, own_ref, above_ref, below_ref, w_ref, out_ref):
    band = lax.axis_index("space")
    pixels, width = own_ref.shape
    edge = reach * columns
    own = own_ref[...]
    above = above_ref[pixels - edge :]
    below = below_ref[:edge]
    above = jnp.where(band > 0, above, jnp.zeros_like(above))
    below = jnp.where(band + 1 < bands, below, jnp.zeros_like(below))
    stack = shifted_taps(jnp.concatenate([above, own, below], axis=0), columns, reach)
    taps = jnp.concatenate(
        [stack[(2 - a) * edge : (2 - a) * edge + pixels] for a in range(3)], axis=1
    )
    weight = jnp.concatenate([w_ref[t] for t in range(9)], axis=1)
    out_ref[...] = lax.dot_general(
        taps, weight, (((1,), (1,)), ((), ())), preferred_element_type=jnp.float32
    )


def feature_grad(own, above, below, weight, columns, reach, bands):
    pixels, _ = own.shape
    taps, channels, width = weight.shape
    step = 256 if channels % 256 == 0 else channels
    whole = pl.BlockSpec((pixels, width), lambda i: (0, 0))
    return pl.pallas_call(
        functools.partial(feature_grad_kernel, columns, reach, bands),
        grid=(channels // step,),
        in_specs=[whole, whole, whole, pl.BlockSpec((taps, step, width), lambda i: (0, i, 0))],
        out_specs=pl.BlockSpec((pixels, step), lambda i: (0, i)),
        out_shape=jax.ShapeDtypeStruct((pixels, channels), jnp.float32),
        compiler_params=pltpu.CompilerParams(vmem_limit_bytes=VMEM_LIMIT),
        cost_estimate=pl.CostEstimate(
            flops=2 * pixels * taps * channels * width,
            bytes_accessed=2 * taps * channels * width + 4 * pixels * channels,
            transcendentals=0,
        ),
        name="feature_grad",
    )(own, above, below, weight)


def final_kernel(in_ref, out_ref):
    replicas, cover, lanes = in_ref.shape
    width = out_ref.shape[1]
    taps = lanes // width
    total = in_ref[0].astype(jnp.float32)
    for d in range(1, replicas):
        total += in_ref[d].astype(jnp.float32)
    total = total / replicas
    for t in range(taps):
        out_ref[pl.ds(t, cover, stride=taps), :] = total[:, t * width : (t + 1) * width]


def final(came, width):
    replicas, cover, lanes = came.shape
    return pl.pallas_call(
        final_kernel,
        out_shape=jax.ShapeDtypeStruct((cover * lanes // width, width), jnp.float32),
        compiler_params=pltpu.CompilerParams(vmem_limit_bytes=VMEM_LIMIT),
        name="final_sum",
    )(came)


def on_device(features, labels, pixel_weight, conv_weight, conv_bias, class_weight):
    image = features[0]
    band_rows, columns, channels = image.shape
    taps, width = conv_weight.shape[1:]
    pixels = band_rows * columns
    replicas = lax.axis_size("dp")
    bands = lax.axis_size("space")
    reach = DILATION_SIZE

    flat = image.reshape(pixels, channels)
    weight = conv_weight.transpose(1, 0, 2)
    block_rows, cover, picks, offsets = channel_plan(channels, taps, replicas, bands)
    even = block_rows % taps == 0
    down, up, *split = prepare(flat, weight, columns, reach, bands, replicas, cover, even)
    if not even:
        order = jnp.array([c for line in picks for c in line], jnp.int32)
        blocks = jnp.take(flat, order, axis=1).reshape(pixels, bands, replicas * cover)
        split = [blocks.transpose(1, 0, 2)]
    above = lax.ppermute(down, "space", [(i, i + 1) for i in range(bands - 1)])
    below = lax.ppermute(up, "space", [(i + 1, i) for i in range(bands - 1)])
    middle = middle_taps(flat, weight, up, columns, reach)
    whole = lax.all_to_all(pass_on(split[0], above), "space", 0, 0)

    gradient = pointwise(
        middle,
        above,
        below,
        conv_bias.reshape(1, width),
        class_weight.T,
        labels.reshape(pixels, 1),
        pixel_weight.reshape(pixels, 1),
    )
    gradients = [gradient] + [
        lax.ppermute(gradient, "space", [(i, (i + k) % bands) for i in range(bands)])
        for k in range(1, bands)
    ]
    partial_grad = kernel_grad(whole, gradients, columns, reach)
    came = lax.all_to_all(partial_grad.reshape(replicas, cover, taps * width), "dp", 0, 0)
    weight_grad = final(came, width)
    if not even:
        start = jnp.array(offsets)[lax.axis_index("space"), lax.axis_index("dp")]
        weight_grad = lax.dynamic_slice_in_dim(weight_grad, start, block_rows)

    grad = feature_grad(gradient, gradients[1 % bands], gradients[-1], weight, columns, reach, bands)
    return grad.reshape(1, band_rows, columns, channels), weight_grad


def solution(mesh):
    placed = (
        P("dp", "space", None, None),
        P("dp", "space", None),
        P("dp", "space", None),
        P(),
        P(),
        P(),
    )
    return jax.shard_map(
        on_device,
        mesh=mesh,
        in_specs=placed,
        out_specs=(P("dp", "space", None, None), P(("dp", "space"), None)),
        check_vma=False,
    )
```

```python
import functools

import jax
import jax.numpy as jnp
from jax import lax
from jax.experimental import pallas as pl
from jax.experimental.pallas import tpu as pltpu
from jax.sharding import PartitionSpec as P

DILATION_SIZE = 6
VMEM_LIMIT = 16 * 1024 * 1024
VMEM_WHOLE = 62 * 1024 * 1024


def channel_plan(channels, taps, replicas, bands):
    rows = channels * taps // (replicas * bands)
    starts = [[(d * bands + s) * rows // taps for d in range(replicas)] for s in range(bands)]
    offsets = [[(d * bands + s) * rows % taps for d in range(replicas)] for s in range(bands)]
    cover = max(-(-(off + rows) // taps) for line in offsets for off in line)
    picks = [
        [min(line[d] + k, channels - 1) for d in replica_order(replicas) for k in range(cover)]
        for line in starts
    ]
    return rows, cover, picks, offsets


def replica_order(replicas):
    if replicas % 2:
        return list(range(replicas))
    return list(range(0, replicas, 2)) + list(range(1, replicas, 2))


def shift_columns(array, by, columns):
    if by == 0:
        return array
    size = array.shape[0]
    column = lax.broadcasted_iota(jnp.int32, array.shape, 0) % columns + by
    moved = pltpu.roll(array, (-by) % size, 0)
    return jnp.where((column >= 0) & (column < columns), moved, 0.0)


def tap_row(x, w_ref, a, columns, reach):
    width = w_ref.shape[2]
    weight = jnp.concatenate([w_ref[3 * a + b] for b in range(3)], axis=1)
    product = jnp.dot(x, weight, preferred_element_type=jnp.float32)
    return sum(
        shift_columns(product[:, b * width : (b + 1) * width], (b - 1) * reach, columns)
        for b in range(3)
    )


def prepare_kernel(
    columns, reach, replicas, cover, x_hbm, w_hbm, *refs
):
    outs, (x_ref, w_ref, room, halo, x_sem, w_sems, out_sems, halo_sems) = refs[:-8], refs[-8:]
    down_hbm, up_hbm = outs[:2]
    pixels, edge = x_ref.shape[0], reach * columns
    load = pltpu.make_async_copy(x_hbm, x_ref, x_sem)
    load.start()
    rows = [0, 2]
    loads = [
        pltpu.make_async_copy(w_hbm.at[pl.ds(3 * a, 3)], w_ref.at[pl.ds(3 * a, 3)], w_sems.at[a])
        for a in rows
    ]
    for copy in loads:
        copy.start()
    load.wait()
    copies = []
    if len(outs) == 3:
        x = x_ref[...]
        bands = room.shape[0]
        for s in range(bands):
            room[s] = jnp.concatenate(
                [
                    x[:, (d * bands + s) * cover : (d * bands + s + 1) * cover]
                    for d in replica_order(replicas)
                ],
                axis=1,
            )
            copies.append(pltpu.make_async_copy(room.at[s], outs[2].at[s], out_sems.at[s]))
            copies[-1].start()
    for k, a in enumerate(rows):
        loads[k].wait()
        x = x_ref[pixels - edge :] if a == 0 else x_ref[:edge]
        halo[k] = tap_row(x, w_ref, a, columns, reach).astype(halo.dtype)
        copies.append(pltpu.make_async_copy(halo.at[k], (down_hbm, up_hbm)[k], halo_sems.at[k]))
        copies[-1].start()
    for copy in copies:
        copy.wait()


def prepare(flat, weight, columns, reach, bands, replicas, cover, blocks):
    pixels, channels = flat.shape
    taps, _, width = weight.shape
    edge = reach * columns
    hbm = pl.BlockSpec(memory_space=pltpu.HBM)
    shape = (bands, pixels, replicas * cover)
    out_shape = [jax.ShapeDtypeStruct((edge, width), jnp.bfloat16)] * 2
    if blocks:
        out_shape.append(jax.ShapeDtypeStruct(shape, flat.dtype))
    return pl.pallas_call(
        functools.partial(prepare_kernel, columns, reach, replicas, cover),
        in_specs=[hbm, hbm],
        out_specs=[hbm] * len(out_shape),
        out_shape=out_shape,
        scratch_shapes=[
            pltpu.VMEM((pixels, channels), flat.dtype),
            pltpu.VMEM((taps, channels, width), weight.dtype),
            pltpu.VMEM(shape, flat.dtype),
            pltpu.VMEM((2, edge, width), jnp.bfloat16),
            pltpu.SemaphoreType.DMA,
            pltpu.SemaphoreType.DMA((3,)),
            pltpu.SemaphoreType.DMA((bands,)),
            pltpu.SemaphoreType.DMA((2,)),
        ],
        compiler_params=pltpu.CompilerParams(vmem_limit_bytes=VMEM_WHOLE),
        cost_estimate=pl.CostEstimate(
            flops=12 * edge * channels * width,
            bytes_accessed=12 * channels * width + 6 * pixels * channels,
            transcendentals=0,
        ),
        name="prepare",
    )(flat, weight)


def pass_on_kernel(*refs):
    del refs


def pass_on(x, *after):
    hbm = pl.BlockSpec(memory_space=pltpu.HBM)
    return pl.pallas_call(
        pass_on_kernel,
        in_specs=[hbm] + [pl.BlockSpec(memory_space=pl.ANY)] * len(after),
        out_specs=hbm,
        out_shape=jax.ShapeDtypeStruct(x.shape, x.dtype),
        input_output_aliases={0: 0},
        name="pass_on",
    )(x, *after)


def middle_kernel(columns, reach, x_ref, w_ref, after_ref, out_ref):
    del after_ref
    pixels, edge = x_ref.shape[0], reach * columns
    out_ref[...] = tap_row(x_ref[...], w_ref, 1, columns, reach)
    if pixels > edge:
        out_ref[edge:] += tap_row(x_ref[: pixels - edge], w_ref, 0, columns, reach)
        out_ref[: pixels - edge] += tap_row(x_ref[edge:], w_ref, 2, columns, reach)


def middle_taps(flat, weight, after, columns, reach):
    pixels, channels = flat.shape
    width = weight.shape[2]
    vmem = pl.BlockSpec(memory_space=pltpu.VMEM)
    return pl.pallas_call(
        functools.partial(middle_kernel, columns, reach),
        in_specs=[vmem, vmem, pl.BlockSpec(memory_space=pl.ANY)],
        out_shape=jax.ShapeDtypeStruct((pixels, width), jnp.float32),
        compiler_params=pltpu.CompilerParams(vmem_limit_bytes=VMEM_LIMIT),
        cost_estimate=pl.CostEstimate(
            flops=6 * pixels * channels * width,
            bytes_accessed=6 * channels * width + 2 * pixels * channels,
            transcendentals=0,
        ),
        name="middle_taps",
    )(flat, weight, after)


def pointwise_kernel(
    middle_ref, above_ref, below_ref, bias_ref, class_ref, label_ref, scale_ref, out_ref
):
    pixels, width = middle_ref.shape
    edge = above_ref.shape[0]
    above = above_ref[...].astype(jnp.float32)
    below = below_ref[...].astype(jnp.float32)
    if pixels > edge:
        none = jnp.zeros((pixels - edge, width), jnp.float32)
        above = jnp.concatenate([above, none], axis=0)
        below = jnp.concatenate([none, below], axis=0)
    preact = middle_ref[...] + above + below + bias_ref[...]
    sigmoid_z = jax.nn.sigmoid(preact)
    hidden = (preact * sigmoid_z).astype(jnp.bfloat16)
    classes = class_ref[...]
    logits = lax.dot_general(
        hidden, classes, (((1,), (1,)), ((), ())), preferred_element_type=jnp.float32
    )
    exponent = jnp.exp(logits)
    chances = exponent / jnp.sum(exponent, axis=1, keepdims=True)
    index = lax.broadcasted_iota(jnp.int32, chances.shape, 1)
    onehot = jnp.where(label_ref[...] == index, 1.0, 0.0)
    grad_logits = scale_ref[...].astype(jnp.float32) * (chances - onehot)
    wide = classes.astype(jnp.float32)
    hidden_grad = sum(
        grad_logits[:, k : k + 1] * wide[k : k + 1] for k in range(classes.shape[0])
    )
    gradient = hidden_grad * sigmoid_z * (1.0 + preact * (1.0 - sigmoid_z))
    out_ref[...] = gradient.astype(out_ref.dtype)


def pointwise(middle, above, below, bias, classes, labels, scale):
    pixels, width = middle.shape
    return pl.pallas_call(
        pointwise_kernel,
        out_shape=jax.ShapeDtypeStruct((pixels, width), jnp.bfloat16),
        compiler_params=pltpu.CompilerParams(vmem_limit_bytes=VMEM_LIMIT),
        cost_estimate=pl.CostEstimate(
            flops=30 * pixels * width,
            bytes_accessed=10 * pixels * width,
            transcendentals=pixels * width,
        ),
        name="pointwise",
    )(middle, above, below, bias, classes, labels, scale)


def shifted_taps(gradient, columns, reach):
    wide = gradient.astype(jnp.float32)
    return jnp.concatenate(
        [shift_columns(wide, (1 - b) * reach, columns).astype(jnp.bfloat16) for b in range(3)],
        axis=1,
    )


def kernel_grad_kernel(columns, reach, parts, other, x_ref, *refs):
    *g_refs, out_ref, taps = refs
    bands, pixels, lanes = x_ref.shape
    width = g_refs[0].shape[1]
    total = bands * pixels
    edge = reach * columns
    extra = lanes // parts
    band = lax.axis_index("space")
    for k, g_ref in enumerate(g_refs):
        first = lax.rem(band + bands - k, bands) * pixels
        taps[pl.ds(pl.multiple_of(first, 16), pixels)] = shifted_taps(g_ref[...], columns, reach)
    part = lax.rem(lax.axis_index("dp") + other, parts)
    if extra % 128 == 0:
        features = x_ref[:, :, pl.ds(pl.multiple_of(part * extra, 128), extra)]
    else:
        features = x_ref[:, :, :extra]
        for k in range(1, parts):
            features = jnp.where(part == k, x_ref[:, :, k * extra : (k + 1) * extra], features)
    features = features.reshape(total, extra)
    for a in range(3):
        if a == 0:
            left, right = features[: total - edge], taps[edge:]
        elif a == 1:
            left, right = features, taps[...]
        else:
            left, right = features[edge:], taps[: total - edge]
        block = lax.dot_general(
            left, right, (((0,), (0,)), ((), ())), preferred_element_type=jnp.float32
        )
        out_ref[:, 3 * a * width : 3 * (a + 1) * width] = block.astype(out_ref.dtype)


def kernel_grad(features, gradients, columns, reach, parts, other, dtype):
    bands, pixels, lanes = features.shape
    extra = lanes // parts
    width = gradients[0].shape[1]
    return pl.pallas_call(
        functools.partial(kernel_grad_kernel, columns, reach, parts, other),
        out_shape=jax.ShapeDtypeStruct((extra, 9 * width), dtype),
        scratch_shapes=[pltpu.VMEM((bands * pixels, 3 * width), jnp.bfloat16)],
        compiler_params=pltpu.CompilerParams(vmem_limit_bytes=VMEM_LIMIT),
        cost_estimate=pl.CostEstimate(
            flops=18 * bands * pixels * extra * width,
            bytes_accessed=2 * bands * pixels * (width + extra) + 18 * extra * width,
            transcendentals=0,
        ),
        name="kernel_grad",
    )(features, *gradients)


def add_kernel(a_ref, b_ref, out_ref):
    out_ref[...] = (a_ref[...] + b_ref[...].astype(jnp.float32)).astype(out_ref.dtype)


def add_up(own, came):
    return pl.pallas_call(
        add_kernel,
        out_shape=jax.ShapeDtypeStruct(came.shape, came.dtype),
        compiler_params=pltpu.CompilerParams(vmem_limit_bytes=VMEM_LIMIT),
        name="add_up",
    )(own, came)


def feature_grad_kernel(columns, reach, bands, own_ref, above_ref, below_ref, w_ref, out_ref):
    band = lax.axis_index("space")
    pixels, width = own_ref.shape
    edge = reach * columns
    own = own_ref[...]
    above = above_ref[pixels - edge :]
    below = below_ref[:edge]
    above = jnp.where(band > 0, above, jnp.zeros_like(above))
    below = jnp.where(band + 1 < bands, below, jnp.zeros_like(below))
    stack = shifted_taps(jnp.concatenate([above, own, below], axis=0), columns, reach)
    taps = jnp.concatenate(
        [stack[(2 - a) * edge : (2 - a) * edge + pixels] for a in range(3)], axis=1
    )
    weight = jnp.concatenate([w_ref[t] for t in range(9)], axis=1)
    out_ref[...] = lax.dot_general(
        taps, weight, (((1,), (1,)), ((), ())), preferred_element_type=jnp.float32
    )


def feature_grad(own, above, below, weight, columns, reach, bands):
    pixels, _ = own.shape
    taps, channels, width = weight.shape
    step = 256 if channels % 256 == 0 else channels
    whole = pl.BlockSpec((pixels, width), lambda i: (0, 0))
    return pl.pallas_call(
        functools.partial(feature_grad_kernel, columns, reach, bands),
        grid=(channels // step,),
        in_specs=[whole, whole, whole, pl.BlockSpec((taps, step, width), lambda i: (0, i, 0))],
        out_specs=pl.BlockSpec((pixels, step), lambda i: (0, i)),
        out_shape=jax.ShapeDtypeStruct((pixels, channels), jnp.float32),
        compiler_params=pltpu.CompilerParams(vmem_limit_bytes=VMEM_LIMIT),
        cost_estimate=pl.CostEstimate(
            flops=2 * pixels * taps * channels * width,
            bytes_accessed=2 * taps * channels * width + 4 * pixels * channels,
            transcendentals=0,
        ),
        name="feature_grad",
    )(own, above, below, weight)


def final_kernel(replicas, in_ref, out_ref):
    blocks, cover, lanes = in_ref.shape
    width = out_ref.shape[1]
    taps = lanes // width
    total = in_ref[0].astype(jnp.float32)
    for d in range(1, blocks):
        total += in_ref[d].astype(jnp.float32)
    total = total / replicas
    for t in range(taps):
        out_ref[pl.ds(t, cover, stride=taps), :] = total[:, t * width : (t + 1) * width]


def final(came, width, replicas):
    _, cover, lanes = came.shape
    return pl.pallas_call(
        functools.partial(final_kernel, replicas),
        out_shape=jax.ShapeDtypeStruct((cover * lanes // width, width), jnp.float32),
        compiler_params=pltpu.CompilerParams(vmem_limit_bytes=VMEM_LIMIT),
        name="final_sum",
    )(came)


def on_device(features, labels, pixel_weight, conv_weight, conv_bias, class_weight):
    image = features[0]
    band_rows, columns, channels = image.shape
    taps, width = conv_weight.shape[1:]
    pixels = band_rows * columns
    replicas = lax.axis_size("dp")
    bands = lax.axis_size("space")
    reach = DILATION_SIZE

    flat = image.reshape(pixels, channels)
    weight = conv_weight.transpose(1, 0, 2)
    block_rows, cover, picks, offsets = channel_plan(channels, taps, replicas, bands)
    even = block_rows % taps == 0
    down, up, *split = prepare(flat, weight, columns, reach, bands, replicas, cover, even)
    if not even:
        order = jnp.array([c for line in picks for c in line], jnp.int32)
        blocks = jnp.take(flat, order, axis=1).reshape(pixels, bands, replicas * cover)
        split = [blocks.transpose(1, 0, 2)]
    above = lax.ppermute(down, "space", [(i, i + 1) for i in range(bands - 1)])
    below = lax.ppermute(up, "space", [(i + 1, i) for i in range(bands - 1)])
    middle = middle_taps(flat, weight, up, columns, reach)
    whole = lax.all_to_all(pass_on(split[0], above, below), "space", 0, 0)

    gradient = pointwise(
        middle,
        above,
        below,
        conv_bias.reshape(1, width),
        class_weight.T,
        labels.reshape(pixels, 1),
        pixel_weight.reshape(pixels, 1),
    )
    gradients = [gradient] + [
        lax.ppermute(gradient, "space", [(i, (i + k) % bands) for i in range(bands)])
        for k in range(1, bands)
    ]
    if replicas % 2 == 0:
        theirs = kernel_grad(whole, gradients, columns, reach, 2, 1, jnp.bfloat16)
        came = lax.ppermute(theirs, "dp", [(i, i ^ 1) for i in range(replicas)])
        own = kernel_grad(whole, gradients, columns, reach, 2, 0, jnp.float32)
        partial_grad = add_up(own, came)
        groups = [list(range(c, replicas, 2)) for c in range(2)]
    else:
        partial_grad = kernel_grad(whole, gradients, columns, reach, 1, 0, jnp.bfloat16)
        groups = None
    partial_grad = partial_grad.reshape(-1, cover, taps * width)
    came = lax.all_to_all(partial_grad, "dp", 0, 0, axis_index_groups=groups)
    weight_grad = final(came, width, replicas)
    if not even:
        start = jnp.array(offsets)[lax.axis_index("space"), lax.axis_index("dp")]
        weight_grad = lax.dynamic_slice_in_dim(weight_grad, start, block_rows)

    grad = feature_grad(gradient, gradients[1 % bands], gradients[-1], weight, columns, reach, bands)
    return grad.reshape(1, band_rows, columns, channels), weight_grad


def solution(mesh):
    placed = (
        P("dp", "space", None, None),
        P("dp", "space", None),
        P("dp", "space", None),
        P(),
        P(),
        P(),
    )
    return jax.shard_map(
        on_device,
        mesh=mesh,
        in_specs=placed,
        out_specs=(P("dp", "space", None, None), P(("dp", "space"), None)),
        check_vma=False,
    )
```

```python
import functools

import jax
import jax.numpy as jnp
from jax import lax
from jax.experimental import pallas as pl
from jax.experimental.pallas import tpu as pltpu
from jax.sharding import PartitionSpec as P

DILATION_SIZE = 6
VMEM_LIMIT = 16 * 1024 * 1024
VMEM_WHOLE = 62 * 1024 * 1024


def channel_plan(channels, taps, replicas, bands):
    rows = channels * taps // (replicas * bands)
    starts = [[(d * bands + s) * rows // taps for d in range(replicas)] for s in range(bands)]
    offsets = [[(d * bands + s) * rows % taps for d in range(replicas)] for s in range(bands)]
    cover = max(-(-(off + rows) // taps) for line in offsets for off in line)
    picks = [
        [min(line[d] + k, channels - 1) for d in replica_order(replicas) for k in range(cover)]
        for line in starts
    ]
    return rows, cover, picks, offsets


def replica_order(replicas):
    if replicas % 2:
        return list(range(replicas))
    return list(range(0, replicas, 2)) + list(range(1, replicas, 2))


def shift_columns(array, by, columns):
    if by == 0:
        return array
    size = array.shape[0]
    column = lax.broadcasted_iota(jnp.int32, array.shape, 0) % columns + by
    moved = pltpu.roll(array, (-by) % size, 0)
    return jnp.where((column >= 0) & (column < columns), moved, 0.0)


def tap_row(x, w_ref, a, columns, reach):
    width = w_ref.shape[2]
    weight = jnp.concatenate([w_ref[3 * a + b] for b in range(3)], axis=1)
    product = jnp.dot(x, weight, preferred_element_type=jnp.float32)
    return sum(
        shift_columns(product[:, b * width : (b + 1) * width], (b - 1) * reach, columns)
        for b in range(3)
    )


def load_kernel(replicas, cover, x_hbm, w_hbm, *refs):
    x_ref, w_ref, *outs = refs[: len(refs) - 4]
    room, x_sem, w_sem, out_sems = refs[len(refs) - 4 :]
    x_load = pltpu.make_async_copy(x_hbm, x_ref, x_sem)
    w_load = pltpu.make_async_copy(w_hbm, w_ref, w_sem)
    x_load.start()
    w_load.start()
    x_load.wait()
    copies = []
    if outs:
        parts, bands, _, lanes = room.shape
        x = x_ref[...]
        order = replica_order(replicas)
        for p in range(parts):
            for s in range(bands):
                blocks = order[p * (replicas // parts) : (p + 1) * (replicas // parts)]
                room[p, s] = jnp.concatenate(
                    [x[:, (d * bands + s) * cover : (d * bands + s + 1) * cover] for d in blocks],
                    axis=1,
                )
        for k, out in enumerate(outs):
            part = lax.rem(lax.axis_index("dp") + parts - 1 - k, parts)
            copies.append(pltpu.make_async_copy(room.at[part], out, out_sems.at[k]))
            copies[-1].start()
    w_load.wait()
    for copy in copies:
        copy.wait()


def load(flat, weight, bands, replicas, cover, parts, blocks):
    pixels, channels = flat.shape
    hbm = pl.BlockSpec(memory_space=pltpu.HBM)
    vmem = pl.BlockSpec(memory_space=pltpu.VMEM)
    shape = (bands, pixels, replicas // parts * cover)
    count = parts if blocks else 0
    return pl.pallas_call(
        functools.partial(load_kernel, replicas, cover),
        in_specs=[hbm, hbm],
        out_specs=[vmem, vmem] + [hbm] * count,
        out_shape=[
            pltpu.VMEM(flat.shape, flat.dtype),
            pltpu.VMEM(weight.shape, weight.dtype),
        ]
        + [pltpu.HBM(shape, flat.dtype)] * count,
        scratch_shapes=[
            pltpu.VMEM((parts,) + shape, flat.dtype),
            pltpu.SemaphoreType.DMA,
            pltpu.SemaphoreType.DMA,
            pltpu.SemaphoreType.DMA((parts,)),
        ],
        compiler_params=pltpu.CompilerParams(vmem_limit_bytes=VMEM_LIMIT),
        cost_estimate=pl.CostEstimate(
            flops=0,
            bytes_accessed=2 * weight.size + 4 * pixels * channels,
            transcendentals=0,
        ),
        name="load",
    )(
        pltpu.with_memory_space_constraint(flat, pltpu.HBM),
        pltpu.with_memory_space_constraint(weight, pltpu.HBM),
    )


def halo_kernel(columns, reach, x_ref, w_ref, down_ref, up_ref):
    pixels, edge = x_ref.shape[0], reach * columns
    down_ref[...] = tap_row(x_ref[pixels - edge :], w_ref, 0, columns, reach).astype(down_ref.dtype)
    up_ref[...] = tap_row(x_ref[:edge], w_ref, 2, columns, reach).astype(up_ref.dtype)


def halo(flat, weight, columns, reach):
    _, channels = flat.shape
    width = weight.shape[2]
    edge = reach * columns
    return pl.pallas_call(
        functools.partial(halo_kernel, columns, reach),
        out_shape=[jax.ShapeDtypeStruct((edge, width), jnp.bfloat16)] * 2,
        compiler_params=pltpu.CompilerParams(vmem_limit_bytes=VMEM_LIMIT),
        cost_estimate=pl.CostEstimate(
            flops=12 * edge * channels * width,
            bytes_accessed=12 * channels * width + 2 * edge * channels,
            transcendentals=0,
        ),
        name="halo",
    )(flat, weight)


def pass_on_kernel(*refs):
    del refs


def pass_on(x, *after):
    hbm = pl.BlockSpec(memory_space=pltpu.HBM)
    return pl.pallas_call(
        pass_on_kernel,
        in_specs=[hbm] + [pl.BlockSpec(memory_space=pltpu.VMEM)] * len(after),
        out_specs=hbm,
        out_shape=pltpu.HBM(x.shape, x.dtype),
        input_output_aliases={0: 0},
        compiler_params=pltpu.CompilerParams(vmem_limit_bytes=VMEM_LIMIT),
        name="pass_on",
    )(pltpu.with_memory_space_constraint(x, pltpu.HBM), *after)


def middle_kernel(columns, reach, x_ref, w_ref, after_ref, out_ref):
    del after_ref
    pixels, edge = x_ref.shape[0], reach * columns
    out_ref[...] = tap_row(x_ref[...], w_ref, 1, columns, reach)
    if pixels > edge:
        out_ref[edge:] += tap_row(x_ref[: pixels - edge], w_ref, 0, columns, reach)
        out_ref[: pixels - edge] += tap_row(x_ref[edge:], w_ref, 2, columns, reach)


def middle_taps(flat, weight, after, columns, reach):
    pixels, channels = flat.shape
    width = weight.shape[2]
    vmem = pl.BlockSpec(memory_space=pltpu.VMEM)
    return pl.pallas_call(
        functools.partial(middle_kernel, columns, reach),
        in_specs=[vmem, vmem, vmem],
        out_shape=jax.ShapeDtypeStruct((pixels, width), jnp.float32),
        compiler_params=pltpu.CompilerParams(vmem_limit_bytes=VMEM_LIMIT),
        cost_estimate=pl.CostEstimate(
            flops=6 * pixels * channels * width,
            bytes_accessed=6 * channels * width + 2 * pixels * channels,
            transcendentals=0,
        ),
        name="middle_taps",
    )(flat, weight, after)


def pointwise_kernel(
    middle_ref, above_ref, below_ref, bias_ref, class_ref, label_ref, scale_ref, out_ref
):
    pixels, width = middle_ref.shape
    edge = above_ref.shape[0]
    above = above_ref[...].astype(jnp.float32)
    below = below_ref[...].astype(jnp.float32)
    if pixels > edge:
        none = jnp.zeros((pixels - edge, width), jnp.float32)
        above = jnp.concatenate([above, none], axis=0)
        below = jnp.concatenate([none, below], axis=0)
    preact = middle_ref[...] + above + below + bias_ref[...]
    sigmoid_z = jax.nn.sigmoid(preact)
    hidden = (preact * sigmoid_z).astype(jnp.bfloat16)
    classes = class_ref[...]
    logits = lax.dot_general(
        hidden, classes, (((1,), (1,)), ((), ())), preferred_element_type=jnp.float32
    )
    exponent = jnp.exp(logits)
    chances = exponent / jnp.sum(exponent, axis=1, keepdims=True)
    index = lax.broadcasted_iota(jnp.int32, chances.shape, 1)
    onehot = jnp.where(label_ref[...] == index, 1.0, 0.0)
    grad_logits = scale_ref[...].astype(jnp.float32) * (chances - onehot)
    wide = classes.astype(jnp.float32)
    hidden_grad = sum(
        grad_logits[:, k : k + 1] * wide[k : k + 1] for k in range(classes.shape[0])
    )
    gradient = hidden_grad * sigmoid_z * (1.0 + preact * (1.0 - sigmoid_z))
    out_ref[...] = gradient.astype(out_ref.dtype)


def pointwise(middle, above, below, bias, classes, labels, scale):
    pixels, width = middle.shape
    return pl.pallas_call(
        pointwise_kernel,
        out_shape=jax.ShapeDtypeStruct((pixels, width), jnp.bfloat16),
        compiler_params=pltpu.CompilerParams(vmem_limit_bytes=VMEM_LIMIT),
        cost_estimate=pl.CostEstimate(
            flops=30 * pixels * width,
            bytes_accessed=10 * pixels * width,
            transcendentals=pixels * width,
        ),
        name="pointwise",
    )(middle, above, below, bias, classes, labels, scale)


def shifted_taps(gradient, columns, reach):
    wide = gradient.astype(jnp.float32)
    return jnp.concatenate(
        [shift_columns(wide, (1 - b) * reach, columns).astype(jnp.bfloat16) for b in range(3)],
        axis=1,
    )


def kernel_grad_kernel(columns, reach, x_ref, *refs):
    *g_refs, out_ref, taps = refs
    bands, pixels, extra = x_ref.shape
    width = g_refs[0].shape[1]
    total = bands * pixels
    edge = reach * columns
    band = lax.axis_index("space")
    for k, g_ref in enumerate(g_refs):
        first = lax.rem(band + bands - k, bands) * pixels
        taps[pl.ds(pl.multiple_of(first, 16), pixels)] = shifted_taps(g_ref[...], columns, reach)
    features = x_ref[...].reshape(total, extra)
    for a in range(3):
        if a == 0:
            left, right = features[: total - edge], taps[edge:]
        elif a == 1:
            left, right = features, taps[...]
        else:
            left, right = features[edge:], taps[: total - edge]
        block = lax.dot_general(
            left, right, (((0,), (0,)), ((), ())), preferred_element_type=jnp.float32
        )
        out_ref[:, 3 * a * width : 3 * (a + 1) * width] = block.astype(out_ref.dtype)


def kernel_grad(features, gradients, columns, reach, dtype):
    bands, pixels, extra = features.shape
    width = gradients[0].shape[1]
    return pl.pallas_call(
        functools.partial(kernel_grad_kernel, columns, reach),
        out_shape=jax.ShapeDtypeStruct((extra, 9 * width), dtype),
        scratch_shapes=[pltpu.VMEM((bands * pixels, 3 * width), jnp.bfloat16)],
        compiler_params=pltpu.CompilerParams(vmem_limit_bytes=VMEM_LIMIT),
        cost_estimate=pl.CostEstimate(
            flops=18 * bands * pixels * extra * width,
            bytes_accessed=2 * bands * pixels * (width + extra) + 18 * extra * width,
            transcendentals=0,
        ),
        name="kernel_grad",
    )(features, *gradients)


def partner(i, k, count):
    return i ^ k if count & (count - 1) == 0 else (i + k) % count


def split_kernel(parts, terms, *refs):
    ins, outs = refs[:terms], refs[terms:]
    count = len(outs)
    cover = outs[0].shape[0]
    me = lax.axis_index("dp") // parts
    for k, out in enumerate(outs):
        if count == 1:
            rows = pl.ds(0, cover)
        else:
            block = jnp.bitwise_xor(me, k) if count & (count - 1) == 0 else lax.rem(me + k, count)
            rows = pl.ds(pl.multiple_of(block * cover, cover), cover)
        total = ins[0][rows, :].astype(jnp.float32)
        for ref in ins[1:]:
            total += ref[rows, :].astype(jnp.float32)
        out[...] = total.astype(out.dtype)


def split_up(terms, parts, count):
    rows, lanes = terms[0].shape
    return pl.pallas_call(
        functools.partial(split_kernel, parts, len(terms)),
        out_shape=[jax.ShapeDtypeStruct((rows // count, lanes), jnp.bfloat16)] * count,
        compiler_params=pltpu.CompilerParams(vmem_limit_bytes=VMEM_LIMIT),
        name="split_up",
    )(*terms)


def final_kernel(replicas, *refs):
    *ins, out_ref = refs
    cover, lanes = ins[0].shape
    width = out_ref.shape[1]
    taps = lanes // width
    total = ins[0][...].astype(jnp.float32)
    for ref in ins[1:]:
        total += ref[...].astype(jnp.float32)
    total = total / replicas
    for t in range(taps):
        out_ref[pl.ds(t, cover, stride=taps), :] = total[:, t * width : (t + 1) * width]


def final(blocks, width, replicas):
    cover, lanes = blocks[0].shape
    return pl.pallas_call(
        functools.partial(final_kernel, replicas),
        out_shape=jax.ShapeDtypeStruct((cover * lanes // width, width), jnp.float32),
        compiler_params=pltpu.CompilerParams(vmem_limit_bytes=VMEM_LIMIT),
        name="final_sum",
    )(*blocks)


def feature_grad_kernel(columns, reach, bands, own_ref, above_ref, below_ref, w_ref, out_ref):
    band = lax.axis_index("space")
    pixels, width = own_ref.shape
    edge = reach * columns
    own = own_ref[...]
    above = above_ref[pixels - edge :]
    below = below_ref[:edge]
    above = jnp.where(band > 0, above, jnp.zeros_like(above))
    below = jnp.where(band + 1 < bands, below, jnp.zeros_like(below))
    stack = shifted_taps(jnp.concatenate([above, own, below], axis=0), columns, reach)
    taps = jnp.concatenate(
        [stack[(2 - a) * edge : (2 - a) * edge + pixels] for a in range(3)], axis=1
    )
    weight = jnp.concatenate([w_ref[t] for t in range(9)], axis=1)
    out_ref[...] = lax.dot_general(
        taps, weight, (((1,), (1,)), ((), ())), preferred_element_type=jnp.float32
    )


def feature_grad(own, above, below, weight, columns, reach, bands):
    pixels, _ = own.shape
    taps, channels, width = weight.shape
    step = 256 if channels % 256 == 0 else channels
    whole = pl.BlockSpec((pixels, width), lambda i: (0, 0))
    return pl.pallas_call(
        functools.partial(feature_grad_kernel, columns, reach, bands),
        grid=(channels // step,),
        in_specs=[whole, whole, whole, pl.BlockSpec((taps, step, width), lambda i: (0, i, 0))],
        out_specs=pl.BlockSpec((pixels, step), lambda i: (0, i)),
        out_shape=jax.ShapeDtypeStruct((pixels, channels), jnp.float32),
        compiler_params=pltpu.CompilerParams(vmem_limit_bytes=VMEM_LIMIT),
        cost_estimate=pl.CostEstimate(
            flops=2 * pixels * taps * channels * width,
            bytes_accessed=2 * taps * channels * width + 4 * pixels * channels,
            transcendentals=0,
        ),
        name="feature_grad",
    )(own, above, below, weight)


def on_device(features, labels, pixel_weight, conv_weight, conv_bias, class_weight):
    image = features[0]
    band_rows, columns, channels = image.shape
    taps, width = conv_weight.shape[1:]
    pixels = band_rows * columns
    replicas = lax.axis_size("dp")
    bands = lax.axis_size("space")
    reach = DILATION_SIZE

    flat = image.reshape(pixels, channels)
    weight = conv_weight.transpose(1, 0, 2)
    block_rows, cover, picks, offsets = channel_plan(channels, taps, replicas, bands)
    even = block_rows % taps == 0
    parts = 2 if replicas % 2 == 0 else 1
    count = replicas // parts
    flat, weight, *split = load(flat, weight, bands, replicas, cover, parts, even)
    if not even:
        order = jnp.array([c for line in picks for c in line], jnp.int32)
        blocks = jnp.take(flat, order, axis=1).reshape(pixels, bands, parts, count * cover)
        blocks = blocks.transpose(2, 1, 0, 3)
        me = lax.axis_index("dp")
        split = [
            lax.dynamic_index_in_dim(blocks, (me + parts - 1 - k) % parts, keepdims=False)
            for k in range(parts)
        ]
    whole = [lax.all_to_all(split[0], "space", 0, 0)]
    down, up = halo(flat, weight, columns, reach)
    above = lax.ppermute(down, "space", [(i, i + 1) for i in range(bands - 1)])
    below = lax.ppermute(up, "space", [(i + 1, i) for i in range(bands - 1)])
    middle = middle_taps(flat, weight, up, columns, reach)
    for blocks in split[1:]:
        held = pass_on(blocks, above, below, middle, whole[0])
        whole.append(lax.all_to_all(held, "space", 0, 0))

    gradient = pointwise(
        middle,
        above,
        below,
        conv_bias.reshape(1, width),
        class_weight.T,
        labels.reshape(pixels, 1),
        pixel_weight.reshape(pixels, 1),
    )
    gradients = [gradient] + [
        lax.ppermute(gradient, "space", [(i, (i + k) % bands) for i in range(bands)])
        for k in range(1, bands)
    ]
    terms = [kernel_grad(whole[-1], gradients, columns, reach, jnp.float32)]
    if parts == 2:
        theirs = kernel_grad(whole[0], gradients, columns, reach, jnp.bfloat16)
        terms.append(lax.ppermute(theirs, "dp", [(i, i ^ 1) for i in range(replicas)]))
    if cover % 16 == 0 and count <= 8:
        blocks = split_up(terms, parts, count)
        came = [blocks[0]]
        for k in range(1, count):
            pairs = [(i, parts * partner(i // parts, k, count) + i % parts) for i in range(replicas)]
            came.append(lax.ppermute(blocks[k], "dp", pairs))
    else:
        blocks = split_up(terms, parts, 1)[0].reshape(count, cover, taps * width)
        groups = [list(range(c, replicas, parts)) for c in range(parts)]
        came = list(lax.all_to_all(blocks, "dp", 0, 0, axis_index_groups=groups))
    weight_grad = final(came, width, replicas)
    if not even:
        start = jnp.array(offsets)[lax.axis_index("space"), lax.axis_index("dp")]
        weight_grad = lax.dynamic_slice_in_dim(weight_grad, start, block_rows)

    grad = feature_grad(gradient, gradients[1 % bands], gradients[-1], weight, columns, reach, bands)
    return grad.reshape(1, band_rows, columns, channels), weight_grad


def solution(mesh):
    placed = (
        P("dp", "space", None, None),
        P("dp", "space", None),
        P("dp", "space", None),
        P(),
        P(),
        P(),
    )
    return jax.shard_map(
        on_device,
        mesh=mesh,
        in_specs=placed,
        out_specs=(P("dp", "space", None, None), P(("dp", "space"), None)),
        check_vma=False,
    )
```

```python
import functools

import jax
import jax.numpy as jnp
from jax import lax
from jax.experimental import pallas as pl
from jax.experimental.pallas import tpu as pltpu
from jax.sharding import PartitionSpec as P

DILATION_SIZE = 6
VMEM_LIMIT = 16 * 1024 * 1024
VMEM_WHOLE = 62 * 1024 * 1024


def channel_plan(channels, taps, replicas, bands):
    rows = channels * taps // (replicas * bands)
    starts = [[(d * bands + s) * rows // taps for d in range(replicas)] for s in range(bands)]
    offsets = [[(d * bands + s) * rows % taps for d in range(replicas)] for s in range(bands)]
    cover = max(-(-(off + rows) // taps) for line in offsets for off in line)
    picks = [
        [min(line[d] + k, channels - 1) for d in replica_order(replicas) for k in range(cover)]
        for line in starts
    ]
    return rows, cover, picks, offsets


def replica_order(replicas):
    if replicas % 2:
        return list(range(replicas))
    return list(range(0, replicas, 2)) + list(range(1, replicas, 2))


def shift_columns(array, by, columns):
    if by == 0:
        return array
    size = array.shape[0]
    column = lax.broadcasted_iota(jnp.int32, array.shape, 0) % columns + by
    moved = pltpu.roll(array, (-by) % size, 0)
    return jnp.where((column >= 0) & (column < columns), moved, 0.0)


def tap_row(x, w_ref, a, columns, reach):
    width = w_ref.shape[2]
    weight = jnp.concatenate([w_ref[3 * a + b] for b in range(3)], axis=1)
    product = jnp.dot(x, weight, preferred_element_type=jnp.float32)
    return sum(
        shift_columns(product[:, b * width : (b + 1) * width], (b - 1) * reach, columns)
        for b in range(3)
    )


def load_kernel(replicas, cover, x_hbm, w_hbm, x_ref, w_ref, *refs):
    *outs, room, x_sem, w_sem, out_sems = refs
    x_load = pltpu.make_async_copy(x_hbm, x_ref, x_sem)
    w_load = pltpu.make_async_copy(w_hbm, w_ref, w_sem)
    x_load.start()
    w_load.start()
    x_load.wait()
    copies = []
    for out in outs:
        bands = room.shape[0]
        x = x_ref[...]
        for s in range(bands):
            room[s] = jnp.concatenate(
                [
                    x[:, (d * bands + s) * cover : (d * bands + s + 1) * cover]
                    for d in replica_order(replicas)
                ],
                axis=1,
            )
            copies.append(pltpu.make_async_copy(room.at[s], out.at[s], out_sems.at[s]))
            copies[-1].start()
    w_load.wait()
    for copy in copies:
        copy.wait()


def load(flat, weight, bands, replicas, cover, blocks):
    pixels, channels = flat.shape
    hbm = pl.BlockSpec(memory_space=pltpu.HBM)
    vmem = pl.BlockSpec(memory_space=pltpu.VMEM)
    shape = (bands, pixels, replicas * cover)
    count = 1 if blocks else 0
    return pl.pallas_call(
        functools.partial(load_kernel, replicas, cover),
        in_specs=[hbm, hbm],
        out_specs=[vmem, vmem] + [hbm] * count,
        out_shape=[
            pltpu.VMEM(flat.shape, flat.dtype),
            pltpu.VMEM(weight.shape, weight.dtype),
        ]
        + [pltpu.HBM(shape, flat.dtype)] * count,
        scratch_shapes=[
            pltpu.VMEM(shape, flat.dtype),
            pltpu.SemaphoreType.DMA,
            pltpu.SemaphoreType.DMA,
            pltpu.SemaphoreType.DMA((bands,)),
        ],
        compiler_params=pltpu.CompilerParams(vmem_limit_bytes=VMEM_LIMIT),
        cost_estimate=pl.CostEstimate(
            flops=0,
            bytes_accessed=2 * weight.size + 4 * pixels * channels,
            transcendentals=0,
        ),
        name="load",
    )(
        pltpu.with_memory_space_constraint(flat, pltpu.HBM),
        pltpu.with_memory_space_constraint(weight, pltpu.HBM),
    )


def halo_kernel(columns, reach, x_ref, w_ref, down_ref, up_ref):
    pixels, edge = x_ref.shape[0], reach * columns
    down_ref[...] = tap_row(x_ref[pixels - edge :], w_ref, 0, columns, reach).astype(down_ref.dtype)
    up_ref[...] = tap_row(x_ref[:edge], w_ref, 2, columns, reach).astype(up_ref.dtype)


def halo(flat, weight, columns, reach):
    _, channels = flat.shape
    width = weight.shape[2]
    edge = reach * columns
    return pl.pallas_call(
        functools.partial(halo_kernel, columns, reach),
        out_shape=[jax.ShapeDtypeStruct((edge, width), jnp.bfloat16)] * 2,
        compiler_params=pltpu.CompilerParams(vmem_limit_bytes=VMEM_LIMIT),
        cost_estimate=pl.CostEstimate(
            flops=12 * edge * channels * width,
            bytes_accessed=12 * channels * width + 2 * edge * channels,
            transcendentals=0,
        ),
        name="halo",
    )(flat, weight)


def middle_kernel(columns, reach, x_ref, w_ref, after_ref, out_ref):
    del after_ref
    pixels, edge = x_ref.shape[0], reach * columns
    out_ref[...] = tap_row(x_ref[...], w_ref, 1, columns, reach)
    if pixels > edge:
        out_ref[edge:] += tap_row(x_ref[: pixels - edge], w_ref, 0, columns, reach)
        out_ref[: pixels - edge] += tap_row(x_ref[edge:], w_ref, 2, columns, reach)


def middle_taps(flat, weight, after, columns, reach):
    pixels, channels = flat.shape
    width = weight.shape[2]
    vmem = pl.BlockSpec(memory_space=pltpu.VMEM)
    return pl.pallas_call(
        functools.partial(middle_kernel, columns, reach),
        in_specs=[vmem, vmem, vmem],
        out_shape=jax.ShapeDtypeStruct((pixels, width), jnp.float32),
        compiler_params=pltpu.CompilerParams(vmem_limit_bytes=VMEM_LIMIT),
        cost_estimate=pl.CostEstimate(
            flops=6 * pixels * channels * width,
            bytes_accessed=6 * channels * width + 2 * pixels * channels,
            transcendentals=0,
        ),
        name="middle_taps",
    )(flat, weight, after)


def pointwise_kernel(
    middle_ref, above_ref, below_ref, bias_ref, class_ref, label_ref, scale_ref, after_ref, out_ref
):
    del after_ref
    pixels, width = middle_ref.shape
    edge = above_ref.shape[0]
    above = above_ref[...].astype(jnp.float32)
    below = below_ref[...].astype(jnp.float32)
    if pixels > edge:
        none = jnp.zeros((pixels - edge, width), jnp.float32)
        above = jnp.concatenate([above, none], axis=0)
        below = jnp.concatenate([none, below], axis=0)
    preact = middle_ref[...] + above + below + bias_ref[...]
    sigmoid_z = jax.nn.sigmoid(preact)
    hidden = (preact * sigmoid_z).astype(jnp.bfloat16)
    classes = class_ref[...]
    logits = lax.dot_general(
        hidden, classes, (((1,), (1,)), ((), ())), preferred_element_type=jnp.float32
    )
    exponent = jnp.exp(logits)
    chances = exponent / jnp.sum(exponent, axis=1, keepdims=True)
    index = lax.broadcasted_iota(jnp.int32, chances.shape, 1)
    onehot = jnp.where(label_ref[...] == index, 1.0, 0.0)
    grad_logits = scale_ref[...].astype(jnp.float32) * (chances - onehot)
    wide = classes.astype(jnp.float32)
    hidden_grad = sum(
        grad_logits[:, k : k + 1] * wide[k : k + 1] for k in range(classes.shape[0])
    )
    gradient = hidden_grad * sigmoid_z * (1.0 + preact * (1.0 - sigmoid_z))
    out_ref[...] = gradient.astype(out_ref.dtype)


def pointwise(middle, above, below, bias, classes, labels, scale, after):
    pixels, width = middle.shape
    vmem = pl.BlockSpec(memory_space=pltpu.VMEM)
    return pl.pallas_call(
        pointwise_kernel,
        in_specs=[vmem] * 7 + [pl.BlockSpec(memory_space=pl.ANY)],
        out_shape=jax.ShapeDtypeStruct((pixels, width), jnp.bfloat16),
        compiler_params=pltpu.CompilerParams(vmem_limit_bytes=VMEM_LIMIT),
        cost_estimate=pl.CostEstimate(
            flops=30 * pixels * width,
            bytes_accessed=10 * pixels * width,
            transcendentals=pixels * width,
        ),
        name="pointwise",
    )(middle, above, below, bias, classes, labels, scale, after)


def shifted_taps(gradient, columns, reach):
    wide = gradient.astype(jnp.float32)
    return jnp.concatenate(
        [shift_columns(wide, (1 - b) * reach, columns).astype(jnp.bfloat16) for b in range(3)],
        axis=1,
    )


def kernel_grad_kernel(columns, reach, parts, other, x_ref, *refs):
    *g_refs, out_ref, taps = refs
    bands, pixels, lanes = x_ref.shape
    width = g_refs[0].shape[1]
    total = bands * pixels
    edge = reach * columns
    extra = lanes // parts
    band = lax.axis_index("space")
    for k, g_ref in enumerate(g_refs):
        first = lax.rem(band + bands - k, bands) * pixels
        taps[pl.ds(pl.multiple_of(first, 16), pixels)] = shifted_taps(g_ref[...], columns, reach)
    part = lax.rem(lax.axis_index("dp") + other, parts)
    if extra % 128 == 0:
        features = x_ref[:, :, pl.ds(pl.multiple_of(part * extra, 128), extra)]
    else:
        features = x_ref[:, :, :extra]
        for k in range(1, parts):
            features = jnp.where(part == k, x_ref[:, :, k * extra : (k + 1) * extra], features)
    features = features.reshape(total, extra)
    for a in range(3):
        if a == 0:
            left, right = features[: total - edge], taps[edge:]
        elif a == 1:
            left, right = features, taps[...]
        else:
            left, right = features[edge:], taps[: total - edge]
        block = lax.dot_general(
            left, right, (((0,), (0,)), ((), ())), preferred_element_type=jnp.float32
        )
        out_ref[:, 3 * a * width : 3 * (a + 1) * width] = block.astype(out_ref.dtype)


def kernel_grad(features, gradients, columns, reach, parts, other, dtype):
    bands, pixels, lanes = features.shape
    extra = lanes // parts
    width = gradients[0].shape[1]
    return pl.pallas_call(
        functools.partial(kernel_grad_kernel, columns, reach, parts, other),
        out_shape=jax.ShapeDtypeStruct((extra, 9 * width), dtype),
        scratch_shapes=[pltpu.VMEM((bands * pixels, 3 * width), jnp.bfloat16)],
        compiler_params=pltpu.CompilerParams(vmem_limit_bytes=VMEM_LIMIT),
        cost_estimate=pl.CostEstimate(
            flops=18 * bands * pixels * extra * width,
            bytes_accessed=2 * bands * pixels * (width + extra) + 18 * extra * width,
            transcendentals=0,
        ),
        name="kernel_grad",
    )(features, *gradients)


def partner(i, k, count):
    return i ^ k if count & (count - 1) == 0 else (i + k) % count


def split_kernel(parts, terms, *refs):
    ins, outs = refs[:terms], refs[terms:]
    count = len(outs)
    cover = outs[0].shape[0]
    me = lax.axis_index("dp") // parts
    for k, out in enumerate(outs):
        if count == 1:
            rows = pl.ds(0, cover)
        else:
            block = jnp.bitwise_xor(me, k) if count & (count - 1) == 0 else lax.rem(me + k, count)
            rows = pl.ds(pl.multiple_of(block * cover, cover), cover)
        total = ins[0][rows, :].astype(jnp.float32)
        for ref in ins[1:]:
            total += ref[rows, :].astype(jnp.float32)
        out[...] = total.astype(out.dtype)


def split_up(terms, parts, count):
    rows, lanes = terms[0].shape
    return pl.pallas_call(
        functools.partial(split_kernel, parts, len(terms)),
        out_shape=[jax.ShapeDtypeStruct((rows // count, lanes), jnp.bfloat16)] * count,
        compiler_params=pltpu.CompilerParams(vmem_limit_bytes=VMEM_LIMIT),
        name="split_up",
    )(*terms)


def final_kernel(replicas, *refs):
    *ins, out_ref = refs
    cover, lanes = ins[0].shape
    width = out_ref.shape[1]
    taps = lanes // width
    total = ins[0][...].astype(jnp.float32)
    for ref in ins[1:]:
        total += ref[...].astype(jnp.float32)
    total = total / replicas
    for t in range(taps):
        out_ref[pl.ds(t, cover, stride=taps), :] = total[:, t * width : (t + 1) * width]


def final(blocks, width, replicas):
    cover, lanes = blocks[0].shape
    return pl.pallas_call(
        functools.partial(final_kernel, replicas),
        out_shape=jax.ShapeDtypeStruct((cover * lanes // width, width), jnp.float32),
        compiler_params=pltpu.CompilerParams(vmem_limit_bytes=VMEM_LIMIT),
        name="final_sum",
    )(*blocks)


def feature_grad_kernel(columns, reach, bands, own_ref, above_ref, below_ref, w_ref, out_ref):
    band = lax.axis_index("space")
    pixels, width = own_ref.shape
    edge = reach * columns
    own = own_ref[...]
    above = above_ref[pixels - edge :]
    below = below_ref[:edge]
    above = jnp.where(band > 0, above, jnp.zeros_like(above))
    below = jnp.where(band + 1 < bands, below, jnp.zeros_like(below))
    stack = shifted_taps(jnp.concatenate([above, own, below], axis=0), columns, reach)
    taps = jnp.concatenate(
        [stack[(2 - a) * edge : (2 - a) * edge + pixels] for a in range(3)], axis=1
    )
    weight = jnp.concatenate([w_ref[t] for t in range(9)], axis=1)
    out_ref[...] = lax.dot_general(
        taps, weight, (((1,), (1,)), ((), ())), preferred_element_type=jnp.float32
    )


def feature_grad(own, above, below, weight, columns, reach, bands):
    pixels, _ = own.shape
    taps, channels, width = weight.shape
    step = 256 if channels % 256 == 0 else channels
    whole = pl.BlockSpec((pixels, width), lambda i: (0, 0))
    return pl.pallas_call(
        functools.partial(feature_grad_kernel, columns, reach, bands),
        grid=(channels // step,),
        in_specs=[whole, whole, whole, pl.BlockSpec((taps, step, width), lambda i: (0, i, 0))],
        out_specs=pl.BlockSpec((pixels, step), lambda i: (0, i)),
        out_shape=jax.ShapeDtypeStruct((pixels, channels), jnp.float32),
        compiler_params=pltpu.CompilerParams(vmem_limit_bytes=VMEM_LIMIT),
        cost_estimate=pl.CostEstimate(
            flops=2 * pixels * taps * channels * width,
            bytes_accessed=2 * taps * channels * width + 4 * pixels * channels,
            transcendentals=0,
        ),
        name="feature_grad",
    )(own, above, below, weight)


def on_device(features, labels, pixel_weight, conv_weight, conv_bias, class_weight):
    image = features[0]
    band_rows, columns, channels = image.shape
    taps, width = conv_weight.shape[1:]
    pixels = band_rows * columns
    replicas = lax.axis_size("dp")
    bands = lax.axis_size("space")
    reach = DILATION_SIZE

    flat = image.reshape(pixels, channels)
    weight = conv_weight.transpose(1, 0, 2)
    block_rows, cover, picks, offsets = channel_plan(channels, taps, replicas, bands)
    even = block_rows % taps == 0
    parts = 2 if replicas % 2 == 0 else 1
    count = replicas // parts
    flat, weight, *split = load(flat, weight, bands, replicas, cover, even)
    if not even:
        order = jnp.array([c for line in picks for c in line], jnp.int32)
        blocks = jnp.take(flat, order, axis=1).reshape(pixels, bands, replicas * cover)
        split = [blocks.transpose(1, 0, 2)]
    whole = lax.all_to_all(split[0], "space", 0, 0)
    down, up = halo(flat, weight, columns, reach)
    above = lax.ppermute(down, "space", [(i, i + 1) for i in range(bands - 1)])
    below = lax.ppermute(up, "space", [(i + 1, i) for i in range(bands - 1)])
    middle = middle_taps(flat, weight, up, columns, reach)

    gradient = pointwise(
        middle,
        above,
        below,
        conv_bias.reshape(1, width),
        class_weight.T,
        labels.reshape(pixels, 1),
        pixel_weight.reshape(pixels, 1),
        whole,
    )
    gradients = [gradient] + [
        lax.ppermute(gradient, "space", [(i, (i + k) % bands) for i in range(bands)])
        for k in range(1, bands)
    ]
    terms = [kernel_grad(whole, gradients, columns, reach, parts, 0, jnp.float32)]
    if parts == 2:
        theirs = kernel_grad(whole, gradients, columns, reach, parts, 1, jnp.bfloat16)
        terms.append(lax.ppermute(theirs, "dp", [(i, i ^ 1) for i in range(replicas)]))
    if cover % 16 == 0 and count <= 8:
        blocks = split_up(terms, parts, count)
        came = [blocks[0]]
        for k in range(1, count):
            pairs = [(i, parts * partner(i // parts, k, count) + i % parts) for i in range(replicas)]
            came.append(lax.ppermute(blocks[k], "dp", pairs))
    else:
        blocks = split_up(terms, parts, 1)[0].reshape(count, cover, taps * width)
        groups = [list(range(c, replicas, parts)) for c in range(parts)]
        came = list(lax.all_to_all(blocks, "dp", 0, 0, axis_index_groups=groups))
    weight_grad = final(came, width, replicas)
    if not even:
        start = jnp.array(offsets)[lax.axis_index("space"), lax.axis_index("dp")]
        weight_grad = lax.dynamic_slice_in_dim(weight_grad, start, block_rows)

    grad = feature_grad(gradient, gradients[1 % bands], gradients[-1], weight, columns, reach, bands)
    return grad.reshape(1, band_rows, columns, channels), weight_grad


def solution(mesh):
    placed = (
        P("dp", "space", None, None),
        P("dp", "space", None),
        P("dp", "space", None),
        P(),
        P(),
        P(),
    )
    return jax.shard_map(
        on_device,
        mesh=mesh,
        in_specs=placed,
        out_specs=(P("dp", "space", None, None), P(("dp", "space"), None)),
        check_vma=False,
    )
```

```python
import functools

import jax
import jax.numpy as jnp
from jax import lax
from jax.experimental import pallas as pl
from jax.experimental.pallas import tpu as pltpu
from jax.sharding import PartitionSpec as P

DILATION_SIZE = 6
VMEM_LIMIT = 16 * 1024 * 1024
VMEM_WHOLE = 62 * 1024 * 1024


def channel_plan(channels, taps, replicas, bands):
    rows = channels * taps // (replicas * bands)
    starts = [[(d * bands + s) * rows // taps for d in range(replicas)] for s in range(bands)]
    offsets = [[(d * bands + s) * rows % taps for d in range(replicas)] for s in range(bands)]
    cover = max(-(-(off + rows) // taps) for line in offsets for off in line)
    picks = [
        [min(line[d] + k, channels - 1) for d in replica_order(replicas) for k in range(cover)]
        for line in starts
    ]
    return rows, cover, picks, offsets


def replica_order(replicas):
    if replicas % 2:
        return list(range(replicas))
    return list(range(0, replicas, 2)) + list(range(1, replicas, 2))


def shift_columns(array, by, columns):
    if by == 0:
        return array
    size = array.shape[0]
    column = lax.broadcasted_iota(jnp.int32, array.shape, 0) % columns + by
    moved = pltpu.roll(array, (-by) % size, 0)
    return jnp.where((column >= 0) & (column < columns), moved, 0.0)


def tap_row(x, w_ref, a, columns, reach):
    width = w_ref.shape[2]
    weight = jnp.concatenate([w_ref[3 * a + b] for b in range(3)], axis=1)
    product = jnp.dot(x, weight, preferred_element_type=jnp.float32)
    return sum(
        shift_columns(product[:, b * width : (b + 1) * width], (b - 1) * reach, columns)
        for b in range(3)
    )


def forward_kernel(columns, reach, replicas, cover, x_hbm, w_hbm, *refs):
    w_ref, down_ref, up_ref, own_ref, *outs, x_ref, room, x_sem, w_sems, out_sems = refs
    pixels, edge = x_ref.shape[0], reach * columns
    x_load = pltpu.make_async_copy(x_hbm, x_ref, x_sem)
    x_load.start()
    w_loads = {}
    for a in (0, 2, 1):
        rows = pl.ds(3 * a, 3)
        w_loads[a] = pltpu.make_async_copy(w_hbm.at[rows], w_ref.at[rows], w_sems.at[a])
        w_loads[a].start()
    x_load.wait()
    x = x_ref[...]
    copies = []
    for out in outs:
        bands = room.shape[0]
        for s in range(bands):
            room[s] = jnp.concatenate(
                [
                    x[:, (d * bands + s) * cover : (d * bands + s + 1) * cover]
                    for d in replica_order(replicas)
                ],
                axis=1,
            )
            copies.append(pltpu.make_async_copy(room.at[s], out.at[s], out_sems.at[s]))
            copies[-1].start()
    w_loads[0].wait()
    part = tap_row(x, w_ref, 0, columns, reach)
    down_ref[...] = part[pixels - edge :].astype(down_ref.dtype)
    if pixels > edge:
        none = jnp.zeros((edge, part.shape[1]), jnp.float32)
        own_ref[...] = jnp.concatenate([none, part[: pixels - edge]], axis=0)
    w_loads[2].wait()
    part = tap_row(x, w_ref, 2, columns, reach)
    up_ref[...] = part[:edge].astype(up_ref.dtype)
    if pixels > edge:
        own_ref[: pixels - edge] += part[edge:]
    w_loads[1].wait()
    part = tap_row(x, w_ref, 1, columns, reach)
    if pixels > edge:
        own_ref[...] += part
    else:
        own_ref[...] = part
    for copy in copies:
        copy.wait()


def forward(flat, weight, columns, reach, bands, replicas, cover, blocks):
    pixels, channels = flat.shape
    taps, _, width = weight.shape
    edge = reach * columns
    hbm = pl.BlockSpec(memory_space=pltpu.HBM)
    vmem = pl.BlockSpec(memory_space=pltpu.VMEM)
    shape = (bands, pixels, replicas * cover)
    count = 1 if blocks else 0
    return pl.pallas_call(
        functools.partial(forward_kernel, columns, reach, replicas, cover),
        in_specs=[hbm, hbm],
        out_specs=[vmem] * 4 + [hbm] * count,
        out_shape=[
            pltpu.VMEM(weight.shape, weight.dtype),
            pltpu.VMEM((edge, width), jnp.bfloat16),
            pltpu.VMEM((edge, width), jnp.bfloat16),
            pltpu.VMEM((pixels, width), jnp.float32),
        ]
        + [pltpu.HBM(shape, flat.dtype)] * count,
        scratch_shapes=[
            pltpu.VMEM(flat.shape, flat.dtype),
            pltpu.VMEM(shape, flat.dtype),
            pltpu.SemaphoreType.DMA,
            pltpu.SemaphoreType.DMA((3,)),
            pltpu.SemaphoreType.DMA((bands,)),
        ],
        compiler_params=pltpu.CompilerParams(vmem_limit_bytes=VMEM_LIMIT),
        cost_estimate=pl.CostEstimate(
            flops=2 * pixels * channels * taps * width,
            bytes_accessed=2 * weight.size + 4 * pixels * channels,
            transcendentals=0,
        ),
        name="forward",
    )(
        pltpu.with_memory_space_constraint(flat, pltpu.HBM),
        pltpu.with_memory_space_constraint(weight, pltpu.HBM),
    )


def pass_on_kernel(*refs):
    del refs


def pass_on(x, *after):
    hbm = pl.BlockSpec(memory_space=pltpu.HBM)
    return pl.pallas_call(
        pass_on_kernel,
        in_specs=[hbm] + [pl.BlockSpec(memory_space=pltpu.VMEM)] * len(after),
        out_specs=hbm,
        out_shape=pltpu.HBM(x.shape, x.dtype),
        input_output_aliases={0: 0},
        compiler_params=pltpu.CompilerParams(vmem_limit_bytes=VMEM_LIMIT),
        name="pass_on",
    )(pltpu.with_memory_space_constraint(x, pltpu.HBM), *after)


def as_column(rows_ref):
    values = rows_ref[...].astype(jnp.float32)
    rows, columns = values.shape
    shape = (columns, columns)
    same = lax.broadcasted_iota(jnp.int32, shape, 0) == lax.broadcasted_iota(jnp.int32, shape, 1)
    return jnp.concatenate(
        [
            jnp.sum(jnp.where(same, values[r : r + 1], 0.0), axis=1, keepdims=True)
            for r in range(rows)
        ],
        axis=0,
    )


def pointwise_kernel(
    middle_ref, above_ref, below_ref, bias_ref, class_ref, label_ref, scale_ref, out_ref
):
    pixels, width = middle_ref.shape
    edge = above_ref.shape[0]
    above = above_ref[...].astype(jnp.float32)
    below = below_ref[...].astype(jnp.float32)
    if pixels > edge:
        none = jnp.zeros((pixels - edge, width), jnp.float32)
        above = jnp.concatenate([above, none], axis=0)
        below = jnp.concatenate([none, below], axis=0)
    preact = middle_ref[...] + above + below + bias_ref[...]
    sigmoid_z = jax.nn.sigmoid(preact)
    hidden = (preact * sigmoid_z).astype(jnp.bfloat16)
    classes = class_ref[...]
    logits = lax.dot_general(
        hidden, classes, (((1,), (1,)), ((), ())), preferred_element_type=jnp.float32
    )
    exponent = jnp.exp(logits)
    chances = exponent / jnp.sum(exponent, axis=1, keepdims=True)
    index = lax.broadcasted_iota(jnp.int32, chances.shape, 1).astype(jnp.float32)
    onehot = jnp.where(as_column(label_ref) == index, 1.0, 0.0)
    grad_logits = as_column(scale_ref) * (chances - onehot)
    wide = classes.astype(jnp.float32)
    hidden_grad = sum(
        grad_logits[:, k : k + 1] * wide[k : k + 1] for k in range(classes.shape[0])
    )
    gradient = hidden_grad * sigmoid_z * (1.0 + preact * (1.0 - sigmoid_z))
    out_ref[...] = gradient.astype(out_ref.dtype)


def pointwise(middle, above, below, bias, classes, labels, scale):
    pixels, width = middle.shape
    return pl.pallas_call(
        pointwise_kernel,
        out_shape=jax.ShapeDtypeStruct((pixels, width), jnp.bfloat16),
        compiler_params=pltpu.CompilerParams(vmem_limit_bytes=VMEM_LIMIT),
        cost_estimate=pl.CostEstimate(
            flops=30 * pixels * width,
            bytes_accessed=10 * pixels * width,
            transcendentals=pixels * width,
        ),
        name="pointwise",
    )(middle, above, below, bias, classes, labels, scale)


def shifted_taps(gradient, columns, reach):
    wide = gradient.astype(jnp.float32)
    return jnp.concatenate(
        [shift_columns(wide, (1 - b) * reach, columns).astype(jnp.bfloat16) for b in range(3)],
        axis=1,
    )


def kernel_grad_kernel(columns, reach, parts, other, x_ref, *refs):
    *g_refs, out_ref, taps = refs
    bands, pixels, lanes = x_ref.shape
    width = g_refs[0].shape[1]
    total = bands * pixels
    edge = reach * columns
    extra = lanes // parts
    band = lax.axis_index("space")
    for k, g_ref in enumerate(g_refs):
        first = lax.rem(band + bands - k, bands) * pixels
        taps[pl.ds(pl.multiple_of(first, 16), pixels)] = shifted_taps(g_ref[...], columns, reach)
    part = lax.rem(lax.axis_index("dp") + other, parts)
    if extra % 128 == 0:
        features = x_ref[:, :, pl.ds(pl.multiple_of(part * extra, 128), extra)]
    else:
        features = x_ref[:, :, :extra]
        for k in range(1, parts):
            features = jnp.where(part == k, x_ref[:, :, k * extra : (k + 1) * extra], features)
    features = features.reshape(total, extra)
    for a in range(3):
        if a == 0:
            left, right = features[: total - edge], taps[edge:]
        elif a == 1:
            left, right = features, taps[...]
        else:
            left, right = features[edge:], taps[: total - edge]
        block = lax.dot_general(
            left, right, (((0,), (0,)), ((), ())), preferred_element_type=jnp.float32
        )
        out_ref[:, 3 * a * width : 3 * (a + 1) * width] = block.astype(out_ref.dtype)


def kernel_grad(features, gradients, columns, reach, parts, other, dtype):
    bands, pixels, lanes = features.shape
    extra = lanes // parts
    width = gradients[0].shape[1]
    return pl.pallas_call(
        functools.partial(kernel_grad_kernel, columns, reach, parts, other),
        out_shape=jax.ShapeDtypeStruct((extra, 9 * width), dtype),
        scratch_shapes=[pltpu.VMEM((bands * pixels, 3 * width), jnp.bfloat16)],
        compiler_params=pltpu.CompilerParams(vmem_limit_bytes=VMEM_LIMIT),
        cost_estimate=pl.CostEstimate(
            flops=18 * bands * pixels * extra * width,
            bytes_accessed=2 * bands * pixels * (width + extra) + 18 * extra * width,
            transcendentals=0,
        ),
        name="kernel_grad",
    )(features, *gradients)


def partner(i, k, count):
    return i ^ k if count & (count - 1) == 0 else (i + k) % count


def split_kernel(parts, terms, *refs):
    ins, outs = refs[:terms], refs[terms:]
    count = len(outs)
    cover = outs[0].shape[0]
    me = lax.axis_index("dp") // parts
    for k, out in enumerate(outs):
        if count == 1:
            rows = pl.ds(0, cover)
        else:
            block = jnp.bitwise_xor(me, k) if count & (count - 1) == 0 else lax.rem(me + k, count)
            rows = pl.ds(pl.multiple_of(block * cover, cover), cover)
        total = ins[0][rows, :].astype(jnp.float32)
        for ref in ins[1:]:
            total += ref[rows, :].astype(jnp.float32)
        out[...] = total.astype(out.dtype)


def split_up(terms, parts, count):
    rows, lanes = terms[0].shape
    return pl.pallas_call(
        functools.partial(split_kernel, parts, len(terms)),
        out_shape=[jax.ShapeDtypeStruct((rows // count, lanes), jnp.bfloat16)] * count,
        compiler_params=pltpu.CompilerParams(vmem_limit_bytes=VMEM_LIMIT),
        name="split_up",
    )(*terms)


def final_kernel(replicas, *refs):
    *ins, out_ref = refs
    cover, lanes = ins[0].shape
    width = out_ref.shape[1]
    taps = lanes // width
    total = ins[0][...].astype(jnp.float32)
    for ref in ins[1:]:
        total += ref[...].astype(jnp.float32)
    total = total / replicas
    for t in range(taps):
        out_ref[pl.ds(t, cover, stride=taps), :] = total[:, t * width : (t + 1) * width]


def final(blocks, width, replicas):
    cover, lanes = blocks[0].shape
    return pl.pallas_call(
        functools.partial(final_kernel, replicas),
        out_shape=jax.ShapeDtypeStruct((cover * lanes // width, width), jnp.float32),
        compiler_params=pltpu.CompilerParams(vmem_limit_bytes=VMEM_LIMIT),
        name="final_sum",
    )(*blocks)


def feature_grad_kernel(columns, reach, bands, own_ref, above_ref, below_ref, w_ref, out_ref):
    band = lax.axis_index("space")
    pixels, width = own_ref.shape
    edge = reach * columns
    own = own_ref[...]
    above = above_ref[pixels - edge :]
    below = below_ref[:edge]
    above = jnp.where(band > 0, above, jnp.zeros_like(above))
    below = jnp.where(band + 1 < bands, below, jnp.zeros_like(below))
    stack = shifted_taps(jnp.concatenate([above, own, below], axis=0), columns, reach)
    taps = jnp.concatenate(
        [stack[(2 - a) * edge : (2 - a) * edge + pixels] for a in range(3)], axis=1
    )
    weight = jnp.concatenate([w_ref[t] for t in range(9)], axis=1)
    out_ref[...] = lax.dot_general(
        taps, weight, (((1,), (1,)), ((), ())), preferred_element_type=jnp.float32
    )


def feature_grad(own, above, below, weight, columns, reach, bands):
    pixels, _ = own.shape
    taps, channels, width = weight.shape
    step = 256 if channels % 256 == 0 else channels
    whole = pl.BlockSpec((pixels, width), lambda i: (0, 0))
    return pl.pallas_call(
        functools.partial(feature_grad_kernel, columns, reach, bands),
        grid=(channels // step,),
        in_specs=[whole, whole, whole, pl.BlockSpec((taps, step, width), lambda i: (0, i, 0))],
        out_specs=pl.BlockSpec((pixels, step), lambda i: (0, i)),
        out_shape=jax.ShapeDtypeStruct((pixels, channels), jnp.float32),
        compiler_params=pltpu.CompilerParams(vmem_limit_bytes=VMEM_LIMIT),
        cost_estimate=pl.CostEstimate(
            flops=2 * pixels * taps * channels * width,
            bytes_accessed=2 * taps * channels * width + 4 * pixels * channels,
            transcendentals=0,
        ),
        name="feature_grad",
    )(own, above, below, weight)


def on_device(features, labels, pixel_weight, conv_weight, conv_bias, class_weight):
    image = features[0]
    band_rows, columns, channels = image.shape
    taps, width = conv_weight.shape[1:]
    pixels = band_rows * columns
    replicas = lax.axis_size("dp")
    bands = lax.axis_size("space")
    reach = DILATION_SIZE

    flat = image.reshape(pixels, channels)
    weight = conv_weight.transpose(1, 0, 2)
    block_rows, cover, picks, offsets = channel_plan(channels, taps, replicas, bands)
    even = block_rows % taps == 0
    parts = 2 if replicas % 2 == 0 else 1
    count = replicas // parts
    weight, down, up, middle, *split = forward(
        flat, weight, columns, reach, bands, replicas, cover, even
    )
    if not even:
        order = jnp.array([c for line in picks for c in line], jnp.int32)
        blocks = jnp.take(flat, order, axis=1).reshape(pixels, bands, replicas * cover)
        split = [blocks.transpose(1, 0, 2)]
    above = lax.ppermute(down, "space", [(i, i + 1) for i in range(bands - 1)])
    below = lax.ppermute(up, "space", [(i + 1, i) for i in range(bands - 1)])
    whole = lax.all_to_all(pass_on(split[0], above), "space", 0, 0)

    gradient = pointwise(
        middle,
        above,
        below,
        conv_bias.reshape(1, width),
        class_weight.T,
        labels.reshape(band_rows, columns),
        pixel_weight.reshape(band_rows, columns),
    )
    gradients = [gradient] + [
        lax.ppermute(gradient, "space", [(i, (i + k) % bands) for i in range(bands)])
        for k in range(1, bands)
    ]
    terms = [kernel_grad(whole, gradients, columns, reach, parts, 0, jnp.float32)]
    if parts == 2:
        theirs = kernel_grad(whole, gradients, columns, reach, parts, 1, jnp.bfloat16)
        terms.append(lax.ppermute(theirs, "dp", [(i, i ^ 1) for i in range(replicas)]))
    if cover % 16 == 0 and count <= 8:
        blocks = split_up(terms, parts, count)
        came = [blocks[0]]
        for k in range(1, count):
            pairs = [(i, parts * partner(i // parts, k, count) + i % parts) for i in range(replicas)]
            came.append(lax.ppermute(blocks[k], "dp", pairs))
    else:
        blocks = split_up(terms, parts, 1)[0].reshape(count, cover, taps * width)
        groups = [list(range(c, replicas, parts)) for c in range(parts)]
        came = list(lax.all_to_all(blocks, "dp", 0, 0, axis_index_groups=groups))
    weight_grad = final(came, width, replicas)
    if not even:
        start = jnp.array(offsets)[lax.axis_index("space"), lax.axis_index("dp")]
        weight_grad = lax.dynamic_slice_in_dim(weight_grad, start, block_rows)

    grad = feature_grad(gradient, gradients[1 % bands], gradients[-1], weight, columns, reach, bands)
    return grad.reshape(1, band_rows, columns, channels), weight_grad


def solution(mesh):
    placed = (
        P("dp", "space", None, None),
        P("dp", "space", None),
        P("dp", "space", None),
        P(),
        P(),
        P(),
    )
    return jax.shard_map(
        on_device,
        mesh=mesh,
        in_specs=placed,
        out_specs=(P("dp", "space", None, None), P(("dp", "space"), None)),
        check_vma=False,
    )
```

```python
import functools

import jax
import jax.numpy as jnp
from jax import lax
from jax.experimental import pallas as pl
from jax.experimental.pallas import tpu as pltpu
from jax.sharding import PartitionSpec as P

DILATION_SIZE = 6
VMEM_LIMIT = 16 * 1024 * 1024
VMEM_WHOLE = 62 * 1024 * 1024


def channel_plan(channels, taps, replicas, bands):
    rows = channels * taps // (replicas * bands)
    starts = [[(d * bands + s) * rows // taps for d in range(replicas)] for s in range(bands)]
    offsets = [[(d * bands + s) * rows % taps for d in range(replicas)] for s in range(bands)]
    cover = max(-(-(off + rows) // taps) for line in offsets for off in line)
    picks = [
        [min(line[d] + k, channels - 1) for d in replica_order(replicas) for k in range(cover)]
        for line in starts
    ]
    return rows, cover, picks, offsets


def replica_order(replicas):
    if replicas % 2:
        return list(range(replicas))
    return list(range(0, replicas, 2)) + list(range(1, replicas, 2))


def shift_columns(array, by, columns):
    if by == 0:
        return array
    size = array.shape[0]
    column = lax.broadcasted_iota(jnp.int32, array.shape, 0) % columns + by
    moved = pltpu.roll(array, (-by) % size, 0)
    return jnp.where((column >= 0) & (column < columns), moved, 0.0)


def tap_row(x, w_ref, a, columns, reach):
    width = w_ref.shape[2]
    weight = jnp.concatenate([w_ref[3 * a + b] for b in range(3)], axis=1)
    product = jnp.dot(x, weight, preferred_element_type=jnp.float32)
    return sum(
        shift_columns(product[:, b * width : (b + 1) * width], (b - 1) * reach, columns)
        for b in range(3)
    )


def load_kernel(replicas, cover, x_hbm, w_hbm, x_ref, w_ref, *refs):
    *outs, room, x_sem, w_sem, out_sems = refs
    x_load = pltpu.make_async_copy(x_hbm, x_ref, x_sem)
    w_load = pltpu.make_async_copy(w_hbm, w_ref, w_sem)
    x_load.start()
    w_load.start()
    x_load.wait()
    copies = []
    for out in outs:
        bands = room.shape[0]
        x = x_ref[...]
        for s in range(bands):
            room[s] = jnp.concatenate(
                [
                    x[:, (d * bands + s) * cover : (d * bands + s + 1) * cover]
                    for d in replica_order(replicas)
                ],
                axis=1,
            )
            copies.append(pltpu.make_async_copy(room.at[s], out.at[s], out_sems.at[s]))
            copies[-1].start()
    w_load.wait()
    for copy in copies:
        copy.wait()


def load(flat, weight, bands, replicas, cover, blocks):
    pixels, channels = flat.shape
    hbm = pl.BlockSpec(memory_space=pltpu.HBM)
    vmem = pl.BlockSpec(memory_space=pltpu.VMEM)
    shape = (bands, pixels, replicas * cover)
    count = 1 if blocks else 0
    return pl.pallas_call(
        functools.partial(load_kernel, replicas, cover),
        in_specs=[hbm, hbm],
        out_specs=[vmem, vmem] + [hbm] * count,
        out_shape=[
            pltpu.VMEM(flat.shape, flat.dtype),
            pltpu.VMEM(weight.shape, weight.dtype),
        ]
        + [pltpu.HBM(shape, flat.dtype)] * count,
        scratch_shapes=[
            pltpu.VMEM(shape, flat.dtype),
            pltpu.SemaphoreType.DMA,
            pltpu.SemaphoreType.DMA,
            pltpu.SemaphoreType.DMA((bands,)),
        ],
        compiler_params=pltpu.CompilerParams(vmem_limit_bytes=VMEM_LIMIT),
        cost_estimate=pl.CostEstimate(
            flops=0,
            bytes_accessed=2 * weight.size + 4 * pixels * channels,
            transcendentals=0,
        ),
        name="load",
    )(
        pltpu.with_memory_space_constraint(flat, pltpu.HBM),
        pltpu.with_memory_space_constraint(weight, pltpu.HBM),
    )


def halo_kernel(columns, reach, x_ref, w_ref, down_ref, up_ref):
    pixels, edge = x_ref.shape[0], reach * columns
    down_ref[...] = tap_row(x_ref[pixels - edge :], w_ref, 0, columns, reach).astype(down_ref.dtype)
    up_ref[...] = tap_row(x_ref[:edge], w_ref, 2, columns, reach).astype(up_ref.dtype)


def halo(flat, weight, columns, reach):
    _, channels = flat.shape
    width = weight.shape[2]
    edge = reach * columns
    return pl.pallas_call(
        functools.partial(halo_kernel, columns, reach),
        out_shape=[pltpu.VMEM((edge, width), jnp.bfloat16)] * 2,
        compiler_params=pltpu.CompilerParams(vmem_limit_bytes=VMEM_LIMIT),
        cost_estimate=pl.CostEstimate(
            flops=12 * edge * channels * width,
            bytes_accessed=12 * channels * width + 2 * edge * channels,
            transcendentals=0,
        ),
        name="halo",
    )(flat, weight)


def middle_kernel(columns, reach, x_ref, w_ref, after_ref, out_ref):
    del after_ref
    pixels, edge = x_ref.shape[0], reach * columns
    out_ref[...] = tap_row(x_ref[...], w_ref, 1, columns, reach)
    if pixels > edge:
        out_ref[edge:] += tap_row(x_ref[: pixels - edge], w_ref, 0, columns, reach)
        out_ref[: pixels - edge] += tap_row(x_ref[edge:], w_ref, 2, columns, reach)


def middle_taps(flat, weight, after, columns, reach):
    pixels, channels = flat.shape
    width = weight.shape[2]
    vmem = pl.BlockSpec(memory_space=pltpu.VMEM)
    return pl.pallas_call(
        functools.partial(middle_kernel, columns, reach),
        in_specs=[vmem, vmem, vmem],
        out_shape=pltpu.VMEM((pixels, width), jnp.float32),
        compiler_params=pltpu.CompilerParams(vmem_limit_bytes=VMEM_LIMIT),
        cost_estimate=pl.CostEstimate(
            flops=6 * pixels * channels * width,
            bytes_accessed=6 * channels * width + 2 * pixels * channels,
            transcendentals=0,
        ),
        name="middle_taps",
    )(flat, weight, after)


def as_column(rows_ref):
    values = rows_ref[...].astype(jnp.float32)
    rows, columns = values.shape
    shape = (columns, columns)
    same = lax.broadcasted_iota(jnp.int32, shape, 0) == lax.broadcasted_iota(jnp.int32, shape, 1)
    return jnp.concatenate(
        [
            jnp.sum(jnp.where(same, values[r : r + 1], 0.0), axis=1, keepdims=True)
            for r in range(rows)
        ],
        axis=0,
    )


def pointwise_kernel(
    middle_ref, above_ref, below_ref, bias_ref, class_ref, label_ref, scale_ref, out_ref
):
    pixels, width = middle_ref.shape
    edge = above_ref.shape[0]
    above = above_ref[...].astype(jnp.float32)
    below = below_ref[...].astype(jnp.float32)
    if pixels > edge:
        none = jnp.zeros((pixels - edge, width), jnp.float32)
        above = jnp.concatenate([above, none], axis=0)
        below = jnp.concatenate([none, below], axis=0)
    preact = middle_ref[...] + above + below + bias_ref[...]
    sigmoid_z = jax.nn.sigmoid(preact)
    hidden = (preact * sigmoid_z).astype(jnp.bfloat16)
    classes = class_ref[...]
    logits = lax.dot_general(
        hidden, classes, (((1,), (1,)), ((), ())), preferred_element_type=jnp.float32
    )
    exponent = jnp.exp(logits)
    chances = exponent / jnp.sum(exponent, axis=1, keepdims=True)
    index = lax.broadcasted_iota(jnp.int32, chances.shape, 1).astype(jnp.float32)
    onehot = jnp.where(as_column(label_ref) == index, 1.0, 0.0)
    grad_logits = as_column(scale_ref) * (chances - onehot)
    wide = classes.astype(jnp.float32)
    hidden_grad = sum(
        grad_logits[:, k : k + 1] * wide[k : k + 1] for k in range(classes.shape[0])
    )
    gradient = hidden_grad * sigmoid_z * (1.0 + preact * (1.0 - sigmoid_z))
    out_ref[...] = gradient.astype(out_ref.dtype)


def pointwise(middle, above, below, bias, classes, labels, scale):
    pixels, width = middle.shape
    return pl.pallas_call(
        pointwise_kernel,
        out_shape=jax.ShapeDtypeStruct((pixels, width), jnp.bfloat16),
        compiler_params=pltpu.CompilerParams(vmem_limit_bytes=VMEM_LIMIT),
        cost_estimate=pl.CostEstimate(
            flops=30 * pixels * width,
            bytes_accessed=10 * pixels * width,
            transcendentals=pixels * width,
        ),
        name="pointwise",
    )(middle, above, below, bias, classes, labels, scale)


def shifted_taps(gradient, columns, reach):
    wide = gradient.astype(jnp.float32)
    return jnp.concatenate(
        [shift_columns(wide, (1 - b) * reach, columns).astype(jnp.bfloat16) for b in range(3)],
        axis=1,
    )


def kernel_grad_kernel(columns, reach, parts, other, x_ref, *refs):
    *g_refs, out_ref, taps = refs
    bands, pixels, lanes = x_ref.shape
    width = g_refs[0].shape[1]
    total = bands * pixels
    edge = reach * columns
    extra = lanes // parts
    band = lax.axis_index("space")
    for k, g_ref in enumerate(g_refs):
        first = lax.rem(band + bands - k, bands) * pixels
        taps[pl.ds(pl.multiple_of(first, 16), pixels)] = shifted_taps(g_ref[...], columns, reach)
    part = lax.rem(lax.axis_index("dp") + other, parts)
    if extra % 128 == 0:
        features = x_ref[:, :, pl.ds(pl.multiple_of(part * extra, 128), extra)]
    else:
        features = x_ref[:, :, :extra]
        for k in range(1, parts):
            features = jnp.where(part == k, x_ref[:, :, k * extra : (k + 1) * extra], features)
    features = features.reshape(total, extra)
    for a in range(3):
        if a == 0:
            left, right = features[: total - edge], taps[edge:]
        elif a == 1:
            left, right = features, taps[...]
        else:
            left, right = features[edge:], taps[: total - edge]
        block = lax.dot_general(
            left, right, (((0,), (0,)), ((), ())), preferred_element_type=jnp.float32
        )
        out_ref[:, 3 * a * width : 3 * (a + 1) * width] = block.astype(out_ref.dtype)


def kernel_grad(features, gradients, columns, reach, parts, other, dtype):
    bands, pixels, lanes = features.shape
    extra = lanes // parts
    width = gradients[0].shape[1]
    return pl.pallas_call(
        functools.partial(kernel_grad_kernel, columns, reach, parts, other),
        out_shape=jax.ShapeDtypeStruct((extra, 9 * width), dtype),
        scratch_shapes=[pltpu.VMEM((bands * pixels, 3 * width), jnp.bfloat16)],
        compiler_params=pltpu.CompilerParams(vmem_limit_bytes=VMEM_LIMIT),
        cost_estimate=pl.CostEstimate(
            flops=18 * bands * pixels * extra * width,
            bytes_accessed=2 * bands * pixels * (width + extra) + 18 * extra * width,
            transcendentals=0,
        ),
        name="kernel_grad",
    )(features, *gradients)


def partner(i, k, count):
    return i ^ k if count & (count - 1) == 0 else (i + k) % count


def split_kernel(parts, terms, *refs):
    ins, outs = refs[:terms], refs[terms:]
    count = len(outs)
    cover = outs[0].shape[0]
    me = lax.axis_index("dp") // parts
    for k, out in enumerate(outs):
        if count == 1:
            rows = pl.ds(0, cover)
        else:
            block = jnp.bitwise_xor(me, k) if count & (count - 1) == 0 else lax.rem(me + k, count)
            rows = pl.ds(pl.multiple_of(block * cover, cover), cover)
        total = ins[0][rows, :].astype(jnp.float32)
        for ref in ins[1:]:
            total += ref[rows, :].astype(jnp.float32)
        out[...] = total.astype(out.dtype)


def split_up(terms, parts, count):
    rows, lanes = terms[0].shape
    return pl.pallas_call(
        functools.partial(split_kernel, parts, len(terms)),
        out_shape=[jax.ShapeDtypeStruct((rows // count, lanes), jnp.bfloat16)] * count,
        compiler_params=pltpu.CompilerParams(vmem_limit_bytes=VMEM_LIMIT),
        name="split_up",
    )(*terms)


def final_kernel(replicas, *refs):
    *ins, out_ref = refs
    cover, lanes = ins[0].shape
    width = out_ref.shape[1]
    taps = lanes // width
    total = ins[0][...].astype(jnp.float32)
    for ref in ins[1:]:
        total += ref[...].astype(jnp.float32)
    total = total / replicas
    for t in range(taps):
        out_ref[pl.ds(t, cover, stride=taps), :] = total[:, t * width : (t + 1) * width]


def final(blocks, width, replicas):
    cover, lanes = blocks[0].shape
    return pl.pallas_call(
        functools.partial(final_kernel, replicas),
        out_shape=jax.ShapeDtypeStruct((cover * lanes // width, width), jnp.float32),
        compiler_params=pltpu.CompilerParams(vmem_limit_bytes=VMEM_LIMIT),
        name="final_sum",
    )(*blocks)


def feature_grad_kernel(columns, reach, bands, own_ref, above_ref, below_ref, w_ref, out_ref):
    band = lax.axis_index("space")
    pixels, width = own_ref.shape
    edge = reach * columns
    own = own_ref[...]
    above = above_ref[pixels - edge :]
    below = below_ref[:edge]
    above = jnp.where(band > 0, above, jnp.zeros_like(above))
    below = jnp.where(band + 1 < bands, below, jnp.zeros_like(below))
    stack = shifted_taps(jnp.concatenate([above, own, below], axis=0), columns, reach)
    taps = jnp.concatenate(
        [stack[(2 - a) * edge : (2 - a) * edge + pixels] for a in range(3)], axis=1
    )
    weight = jnp.concatenate([w_ref[t] for t in range(9)], axis=1)
    out_ref[...] = lax.dot_general(
        taps, weight, (((1,), (1,)), ((), ())), preferred_element_type=jnp.float32
    )


def feature_grad(own, above, below, weight, columns, reach, bands):
    pixels, _ = own.shape
    taps, channels, width = weight.shape
    step = 256 if channels % 256 == 0 else channels
    whole = pl.BlockSpec((pixels, width), lambda i: (0, 0))
    return pl.pallas_call(
        functools.partial(feature_grad_kernel, columns, reach, bands),
        grid=(channels // step,),
        in_specs=[whole, whole, whole, pl.BlockSpec((taps, step, width), lambda i: (0, i, 0))],
        out_specs=pl.BlockSpec((pixels, step), lambda i: (0, i)),
        out_shape=jax.ShapeDtypeStruct((pixels, channels), jnp.float32),
        compiler_params=pltpu.CompilerParams(vmem_limit_bytes=VMEM_LIMIT),
        cost_estimate=pl.CostEstimate(
            flops=2 * pixels * taps * channels * width,
            bytes_accessed=2 * taps * channels * width + 4 * pixels * channels,
            transcendentals=0,
        ),
        name="feature_grad",
    )(own, above, below, weight)


def on_device(features, labels, pixel_weight, conv_weight, conv_bias, class_weight):
    image = features[0]
    band_rows, columns, channels = image.shape
    taps, width = conv_weight.shape[1:]
    pixels = band_rows * columns
    replicas = lax.axis_size("dp")
    bands = lax.axis_size("space")
    reach = DILATION_SIZE

    flat = image.reshape(pixels, channels)
    weight = conv_weight.transpose(1, 0, 2)
    block_rows, cover, picks, offsets = channel_plan(channels, taps, replicas, bands)
    even = block_rows % taps == 0
    parts = 2 if replicas % 2 == 0 else 1
    count = replicas // parts
    flat, weight, *split = load(flat, weight, bands, replicas, cover, even)
    if not even:
        order = jnp.array([c for line in picks for c in line], jnp.int32)
        blocks = jnp.take(flat, order, axis=1).reshape(pixels, bands, replicas * cover)
        split = [blocks.transpose(1, 0, 2)]
    whole = lax.all_to_all(split[0], "space", 0, 0)
    down, up = halo(flat, weight, columns, reach)
    above = lax.ppermute(down, "space", [(i, i + 1) for i in range(bands - 1)])
    below = lax.ppermute(up, "space", [(i + 1, i) for i in range(bands - 1)])
    middle = middle_taps(flat, weight, up, columns, reach)

    gradient = pointwise(
        middle,
        above,
        below,
        conv_bias.reshape(1, width),
        class_weight.T,
        labels.reshape(band_rows, columns),
        pixel_weight.reshape(band_rows, columns),
    )
    gradients = [gradient] + [
        lax.ppermute(gradient, "space", [(i, (i + k) % bands) for i in range(bands)])
        for k in range(1, bands)
    ]
    terms = [kernel_grad(whole, gradients, columns, reach, parts, 0, jnp.float32)]
    if parts == 2:
        theirs = kernel_grad(whole, gradients, columns, reach, parts, 1, jnp.bfloat16)
        terms.append(lax.ppermute(theirs, "dp", [(i, i ^ 1) for i in range(replicas)]))
    if cover % 16 == 0 and count <= 8:
        blocks = split_up(terms, parts, count)
        came = [blocks[0]]
        for k in reversed(range(1, count)):
            pairs = [(i, parts * partner(i // parts, k, count) + i % parts) for i in range(replicas)]
            came.append(lax.ppermute(blocks[k], "dp", pairs))
    else:
        blocks = split_up(terms, parts, 1)[0].reshape(count, cover, taps * width)
        groups = [list(range(c, replicas, parts)) for c in range(parts)]
        came = list(lax.all_to_all(blocks, "dp", 0, 0, axis_index_groups=groups))
    weight_grad = final(came, width, replicas)
    if not even:
        start = jnp.array(offsets)[lax.axis_index("space"), lax.axis_index("dp")]
        weight_grad = lax.dynamic_slice_in_dim(weight_grad, start, block_rows)

    grad = feature_grad(gradient, gradients[1 % bands], gradients[-1], weight, columns, reach, bands)
    return grad.reshape(1, band_rows, columns, channels), weight_grad


def solution(mesh):
    placed = (
        P("dp", "space", None, None),
        P("dp", "space", None),
        P("dp", "space", None),
        P(),
        P(),
        P(),
    )
    return jax.shard_map(
        on_device,
        mesh=mesh,
        in_specs=placed,
        out_specs=(P("dp", "space", None, None), P(("dp", "space"), None)),
        check_vma=False,
    )
```

```python
import functools

import jax
import jax.numpy as jnp
from jax import lax
from jax.experimental import pallas as pl
from jax.experimental.pallas import tpu as pltpu
from jax.sharding import PartitionSpec as P

DILATION_SIZE = 6
VMEM_LIMIT = 16 * 1024 * 1024
VMEM_WHOLE = 62 * 1024 * 1024


def channel_plan(channels, taps, replicas, bands):
    rows = channels * taps // (replicas * bands)
    starts = [[(d * bands + s) * rows // taps for d in range(replicas)] for s in range(bands)]
    offsets = [[(d * bands + s) * rows % taps for d in range(replicas)] for s in range(bands)]
    cover = max(-(-(off + rows) // taps) for line in offsets for off in line)
    picks = [
        [min(line[d] + k, channels - 1) for d in replica_order(replicas) for k in range(cover)]
        for line in starts
    ]
    return rows, cover, picks, offsets


def replica_order(replicas):
    if replicas % 2:
        return list(range(replicas))
    return list(range(0, replicas, 2)) + list(range(1, replicas, 2))


def shift_columns(array, by, columns):
    if by == 0:
        return array
    size = array.shape[0]
    column = lax.broadcasted_iota(jnp.int32, array.shape, 0) % columns + by
    moved = pltpu.roll(array, (-by) % size, 0)
    return jnp.where((column >= 0) & (column < columns), moved, 0.0)


def tap_row(x, w_ref, a, columns, reach):
    width = w_ref.shape[2]
    weight = jnp.concatenate([w_ref[3 * a + b] for b in range(3)], axis=1)
    product = jnp.dot(x, weight, preferred_element_type=jnp.float32)
    return sum(
        shift_columns(product[:, b * width : (b + 1) * width], (b - 1) * reach, columns)
        for b in range(3)
    )


def load_kernel(replicas, cover, x_hbm, w_hbm, x_ref, w_ref, *refs):
    *outs, room, x_sem, w_sem, out_sems = refs
    x_load = pltpu.make_async_copy(x_hbm, x_ref, x_sem)
    w_load = pltpu.make_async_copy(w_hbm, w_ref, w_sem)
    x_load.start()
    w_load.start()
    x_load.wait()
    copies = []
    for out in outs:
        bands = room.shape[0]
        x = x_ref[...]
        for s in range(bands):
            room[s] = jnp.concatenate(
                [
                    x[:, (d * bands + s) * cover : (d * bands + s + 1) * cover]
                    for d in replica_order(replicas)
                ],
                axis=1,
            )
            copies.append(pltpu.make_async_copy(room.at[s], out.at[s], out_sems.at[s]))
            copies[-1].start()
    w_load.wait()
    for copy in copies:
        copy.wait()


def load(flat, weight, bands, replicas, cover, blocks):
    pixels, channels = flat.shape
    hbm = pl.BlockSpec(memory_space=pltpu.HBM)
    vmem = pl.BlockSpec(memory_space=pltpu.VMEM)
    shape = (bands, pixels, replicas * cover)
    count = 1 if blocks else 0
    return pl.pallas_call(
        functools.partial(load_kernel, replicas, cover),
        in_specs=[hbm, hbm],
        out_specs=[vmem, vmem] + [hbm] * count,
        out_shape=[
            pltpu.VMEM(flat.shape, flat.dtype),
            pltpu.VMEM(weight.shape, weight.dtype),
        ]
        + [pltpu.HBM(shape, flat.dtype)] * count,
        scratch_shapes=[
            pltpu.VMEM(shape, flat.dtype),
            pltpu.SemaphoreType.DMA,
            pltpu.SemaphoreType.DMA,
            pltpu.SemaphoreType.DMA((bands,)),
        ],
        compiler_params=pltpu.CompilerParams(vmem_limit_bytes=VMEM_LIMIT),
        cost_estimate=pl.CostEstimate(
            flops=0,
            bytes_accessed=2 * weight.size + 4 * pixels * channels,
            transcendentals=0,
        ),
        name="load",
    )(
        pltpu.with_memory_space_constraint(flat, pltpu.HBM),
        pltpu.with_memory_space_constraint(weight, pltpu.HBM),
    )


def halo_kernel(columns, reach, x_ref, w_ref, down_ref, up_ref):
    pixels, edge = x_ref.shape[0], reach * columns
    width = w_ref.shape[2]
    if pixels > edge:
        down = tap_row(x_ref[pixels - edge :], w_ref, 0, columns, reach)
        up = tap_row(x_ref[:edge], w_ref, 2, columns, reach)
    else:
        weight = jnp.concatenate([w_ref[t] for t in (0, 1, 2, 6, 7, 8)], axis=1)
        product = jnp.dot(x_ref[...], weight, preferred_element_type=jnp.float32)
        down, up = [
            sum(
                shift_columns(
                    product[:, (3 * k + b) * width : (3 * k + b + 1) * width], (b - 1) * reach, columns
                )
                for b in range(3)
            )
            for k in range(2)
        ]
    down_ref[...] = down.astype(down_ref.dtype)
    up_ref[...] = up.astype(up_ref.dtype)


def halo(flat, weight, columns, reach):
    _, channels = flat.shape
    width = weight.shape[2]
    edge = reach * columns
    return pl.pallas_call(
        functools.partial(halo_kernel, columns, reach),
        out_shape=[pltpu.VMEM((edge, width), jnp.bfloat16)] * 2,
        compiler_params=pltpu.CompilerParams(vmem_limit_bytes=VMEM_LIMIT),
        cost_estimate=pl.CostEstimate(
            flops=12 * edge * channels * width,
            bytes_accessed=12 * channels * width + 2 * edge * channels,
            transcendentals=0,
        ),
        name="halo",
    )(flat, weight)


def middle_kernel(columns, reach, x_ref, w_ref, after_ref, out_ref):
    del after_ref
    pixels, edge = x_ref.shape[0], reach * columns
    out_ref[...] = tap_row(x_ref[...], w_ref, 1, columns, reach)
    if pixels > edge:
        out_ref[edge:] += tap_row(x_ref[: pixels - edge], w_ref, 0, columns, reach)
        out_ref[: pixels - edge] += tap_row(x_ref[edge:], w_ref, 2, columns, reach)


def middle_taps(flat, weight, after, columns, reach):
    pixels, channels = flat.shape
    width = weight.shape[2]
    vmem = pl.BlockSpec(memory_space=pltpu.VMEM)
    return pl.pallas_call(
        functools.partial(middle_kernel, columns, reach),
        in_specs=[vmem, vmem, vmem],
        out_shape=pltpu.VMEM((pixels, width), jnp.float32),
        compiler_params=pltpu.CompilerParams(vmem_limit_bytes=VMEM_LIMIT),
        cost_estimate=pl.CostEstimate(
            flops=6 * pixels * channels * width,
            bytes_accessed=6 * channels * width + 2 * pixels * channels,
            transcendentals=0,
        ),
        name="middle_taps",
    )(flat, weight, after)


def as_column(rows_ref):
    values = rows_ref[...].astype(jnp.float32)
    rows, columns = values.shape
    shape = (columns, columns)
    same = lax.broadcasted_iota(jnp.int32, shape, 0) == lax.broadcasted_iota(jnp.int32, shape, 1)
    return jnp.concatenate(
        [
            jnp.sum(jnp.where(same, values[r : r + 1], 0.0), axis=1, keepdims=True)
            for r in range(rows)
        ],
        axis=0,
    )


def pointwise_kernel(
    middle_ref, above_ref, below_ref, bias_ref, class_ref, label_ref, scale_ref, out_ref
):
    pixels, width = middle_ref.shape
    edge = above_ref.shape[0]
    above = above_ref[...].astype(jnp.float32)
    below = below_ref[...].astype(jnp.float32)
    if pixels > edge:
        none = jnp.zeros((pixels - edge, width), jnp.float32)
        above = jnp.concatenate([above, none], axis=0)
        below = jnp.concatenate([none, below], axis=0)
    preact = middle_ref[...] + above + below + bias_ref[...]
    sigmoid_z = jax.nn.sigmoid(preact)
    hidden = (preact * sigmoid_z).astype(jnp.bfloat16)
    classes = class_ref[...]
    logits = lax.dot_general(
        hidden, classes, (((1,), (1,)), ((), ())), preferred_element_type=jnp.float32
    )
    exponent = jnp.exp(logits)
    chances = exponent / jnp.sum(exponent, axis=1, keepdims=True)
    index = lax.broadcasted_iota(jnp.int32, chances.shape, 1).astype(jnp.float32)
    onehot = jnp.where(as_column(label_ref) == index, 1.0, 0.0)
    grad_logits = as_column(scale_ref) * (chances - onehot)
    wide = classes.astype(jnp.float32)
    hidden_grad = sum(
        grad_logits[:, k : k + 1] * wide[k : k + 1] for k in range(classes.shape[0])
    )
    gradient = hidden_grad * sigmoid_z * (1.0 + preact * (1.0 - sigmoid_z))
    out_ref[...] = gradient.astype(out_ref.dtype)


def pointwise(middle, above, below, bias, classes, labels, scale):
    pixels, width = middle.shape
    return pl.pallas_call(
        pointwise_kernel,
        out_shape=jax.ShapeDtypeStruct((pixels, width), jnp.bfloat16),
        compiler_params=pltpu.CompilerParams(vmem_limit_bytes=VMEM_LIMIT),
        cost_estimate=pl.CostEstimate(
            flops=30 * pixels * width,
            bytes_accessed=10 * pixels * width,
            transcendentals=pixels * width,
        ),
        name="pointwise",
    )(middle, above, below, bias, classes, labels, scale)


def shifted_taps(gradient, columns, reach):
    wide = gradient.astype(jnp.float32)
    return jnp.concatenate(
        [shift_columns(wide, (1 - b) * reach, columns).astype(jnp.bfloat16) for b in range(3)],
        axis=1,
    )


def kernel_grad_kernel(columns, reach, parts, others, distances, before, x_ref, *refs):
    count = len(distances)
    g_refs, sums, outs = refs[:count], refs[count : count + before], refs[count + before : -1]
    padded = refs[-1]
    bands, pixels, lanes = x_ref.shape
    width = g_refs[0].shape[1]
    total = bands * pixels
    edge = reach * columns
    extra = lanes // parts
    band = lax.axis_index("space")
    none = jnp.zeros((edge, padded.shape[1]), padded.dtype)
    padded[:edge] = none
    padded[edge + total :] = none
    shifted = [shifted_taps(g_ref[...], columns, reach) for g_ref in g_refs]
    for n, (other, out_ref) in enumerate(zip(others, outs)):
        part = lax.rem(lax.axis_index("dp") + other, parts)
        if extra % 128 == 0:
            features = x_ref[:, :, pl.ds(pl.multiple_of(part * extra, 128), extra)]
        else:
            features = x_ref[:, :, :extra]
            for k in range(1, parts):
                features = jnp.where(part == k, x_ref[:, :, k * extra : (k + 1) * extra], features)
        padded[edge : edge + total] = features.reshape(total, extra)
        for a in range(3):
            here = pl.ds(3 * a * width, 3 * width)
            grad = sums[n][:, here] if before else None
            for k, right in zip(distances, shifted):
                first = lax.rem(band + bands - k, bands) * pixels + a * edge
                left = padded[pl.ds(pl.multiple_of(first, 16), pixels)]
                term = lax.dot_general(
                    left, right, (((0,), (0,)), ((), ())), preferred_element_type=jnp.float32
                )
                grad = term if grad is None else grad + term
            out_ref[:, here] = grad.astype(out_ref.dtype)


def kernel_grad(features, gradients, sums, columns, reach, parts, others, dtype):
    bands, pixels, lanes = features.shape
    extra = lanes // parts
    distances = tuple(gradients)
    width = gradients[distances[0]].shape[1]
    work = len(others) * len(distances) * pixels * extra * width
    return pl.pallas_call(
        functools.partial(
            kernel_grad_kernel, columns, reach, parts, others, distances, len(sums)
        ),
        out_shape=[pltpu.VMEM((extra, 9 * width), dtype)] * len(others),
        scratch_shapes=[pltpu.VMEM((bands * pixels + 2 * reach * columns, extra), features.dtype)],
        compiler_params=pltpu.CompilerParams(vmem_limit_bytes=VMEM_LIMIT),
        cost_estimate=pl.CostEstimate(
            flops=18 * work, bytes_accessed=2 * bands * pixels * lanes, transcendentals=0
        ),
        name="kernel_grad",
    )(features, *gradients.values(), *sums)


def partner(i, k, count):
    return i ^ k if count & (count - 1) == 0 else (i + k) % count


def split_kernel(parts, terms, *refs):
    ins, outs = refs[:terms], refs[terms:]
    count = len(outs)
    cover = outs[0].shape[0]
    me = lax.axis_index("dp") // parts
    for k, out in enumerate(outs):
        if count == 1:
            rows = pl.ds(0, cover)
        else:
            block = jnp.bitwise_xor(me, k) if count & (count - 1) == 0 else lax.rem(me + k, count)
            rows = pl.ds(pl.multiple_of(block * cover, cover), cover)
        total = ins[0][rows, :].astype(jnp.float32)
        for ref in ins[1:]:
            total += ref[rows, :].astype(jnp.float32)
        out[...] = total.astype(out.dtype)


def split_up(terms, parts, count):
    rows, lanes = terms[0].shape
    return pl.pallas_call(
        functools.partial(split_kernel, parts, len(terms)),
        out_shape=[jax.ShapeDtypeStruct((rows // count, lanes), jnp.bfloat16)] * count,
        compiler_params=pltpu.CompilerParams(vmem_limit_bytes=VMEM_LIMIT),
        name="split_up",
    )(*terms)


def final_kernel(replicas, *refs):
    *ins, out_ref = refs
    cover, lanes = ins[0].shape
    width = out_ref.shape[1]
    taps = lanes // width
    total = ins[0][...].astype(jnp.float32)
    for ref in ins[1:]:
        total += ref[...].astype(jnp.float32)
    total = total / replicas
    for t in range(taps):
        out_ref[pl.ds(t, cover, stride=taps), :] = total[:, t * width : (t + 1) * width]


def final(blocks, width, replicas):
    cover, lanes = blocks[0].shape
    return pl.pallas_call(
        functools.partial(final_kernel, replicas),
        out_shape=jax.ShapeDtypeStruct((cover * lanes // width, width), jnp.float32),
        compiler_params=pltpu.CompilerParams(vmem_limit_bytes=VMEM_LIMIT),
        name="final_sum",
    )(*blocks)


def feature_grad_kernel(columns, reach, bands, own_ref, above_ref, below_ref, w_ref, out, room, sems):
    band = lax.axis_index("space")
    pixels, width = own_ref.shape
    edge = reach * columns
    own = own_ref[...]
    above = above_ref[pixels - edge :]
    below = below_ref[:edge]
    above = jnp.where(band > 0, above, jnp.zeros_like(above))
    below = jnp.where(band + 1 < bands, below, jnp.zeros_like(below))
    stack = shifted_taps(jnp.concatenate([above, own, below], axis=0), columns, reach)
    taps = jnp.concatenate(
        [stack[(2 - a) * edge : (2 - a) * edge + pixels] for a in range(3)], axis=1
    )
    steps, _, step = room.shape
    copies = []
    for n in range(steps):
        here = pl.ds(n * step, step)
        weight = jnp.concatenate([w_ref[t, here, :] for t in range(w_ref.shape[0])], axis=1)
        room[n] = lax.dot_general(
            taps, weight, (((1,), (1,)), ((), ())), preferred_element_type=jnp.float32
        )
        copies.append(pltpu.make_async_copy(room.at[n], out.at[:, here], sems.at[n]))
        copies[-1].start()
    for copy in copies:
        copy.wait()


def feature_grad(own, above, below, weight, columns, reach, bands):
    pixels, _ = own.shape
    taps, channels, width = weight.shape
    step = 256 if channels % 256 == 0 else channels
    vmem = pl.BlockSpec(memory_space=pltpu.VMEM)
    return pl.pallas_call(
        functools.partial(feature_grad_kernel, columns, reach, bands),
        in_specs=[vmem] * 4,
        out_specs=pl.BlockSpec(memory_space=pltpu.HBM),
        out_shape=pltpu.HBM((pixels, channels), jnp.float32),
        scratch_shapes=[
            pltpu.VMEM((channels // step, pixels, step), jnp.float32),
            pltpu.SemaphoreType.DMA((channels // step,)),
        ],
        compiler_params=pltpu.CompilerParams(vmem_limit_bytes=VMEM_LIMIT),
        cost_estimate=pl.CostEstimate(
            flops=2 * pixels * taps * channels * width,
            bytes_accessed=2 * taps * channels * width + 4 * pixels * channels,
            transcendentals=0,
        ),
        name="feature_grad",
    )(own, above, below, weight)


def on_device(features, labels, pixel_weight, conv_weight, conv_bias, class_weight):
    image = features[0]
    band_rows, columns, channels = image.shape
    taps, width = conv_weight.shape[1:]
    pixels = band_rows * columns
    replicas = lax.axis_size("dp")
    bands = lax.axis_size("space")
    reach = DILATION_SIZE

    flat = image.reshape(pixels, channels)
    weight = conv_weight.transpose(1, 0, 2)
    block_rows, cover, picks, offsets = channel_plan(channels, taps, replicas, bands)
    even = block_rows % taps == 0
    parts = 2 if replicas % 2 == 0 else 1
    count = replicas // parts
    flat, weight, *split = load(flat, weight, bands, replicas, cover, even)
    if not even:
        order = jnp.array([c for line in picks for c in line], jnp.int32)
        blocks = jnp.take(flat, order, axis=1).reshape(pixels, bands, replicas * cover)
        split = [blocks.transpose(1, 0, 2)]
    whole = lax.all_to_all(split[0], "space", 0, 0)
    down, up = halo(flat, weight, columns, reach)
    above = lax.ppermute(down, "space", [(i, i + 1) for i in range(bands - 1)])
    below = lax.ppermute(up, "space", [(i + 1, i) for i in range(bands - 1)])
    middle = middle_taps(flat, weight, up, columns, reach)

    gradient = pointwise(
        middle,
        above,
        below,
        conv_bias.reshape(1, width),
        class_weight.T,
        labels.reshape(band_rows, columns),
        pixel_weight.reshape(band_rows, columns),
    )
    gradients = [gradient] + [
        lax.ppermute(gradient, "space", [(i, (i + k) % bands) for i in range(bands)])
        for k in range(1, bands)
    ]
    late = bands // 2
    early = {k: g for k, g in enumerate(gradients) if k != late or bands == 1}
    others = (0, 1)[:parts]
    terms = kernel_grad(whole, early, [], columns, reach, parts, others, jnp.float32)
    if bands > 1:
        last = {late: gradients[late]}
        own, *theirs = terms
        terms = kernel_grad(whole, last, [own], columns, reach, parts, (0,), jnp.float32)
        terms += kernel_grad(whole, last, theirs, columns, reach, parts, (1,), jnp.bfloat16) if theirs else []
    if parts == 2:
        theirs = terms[1].astype(jnp.bfloat16)
        terms = [terms[0], lax.ppermute(theirs, "dp", [(i, i ^ 1) for i in range(replicas)])]
    if cover % 16 == 0 and count <= 8:
        blocks = split_up(terms, parts, count)
        came = [blocks[0]]
        for k in reversed(range(1, count)):
            pairs = [(i, parts * partner(i // parts, k, count) + i % parts) for i in range(replicas)]
            came.append(lax.ppermute(blocks[k], "dp", pairs))
    else:
        blocks = split_up(terms, parts, 1)[0].reshape(count, cover, taps * width)
        groups = [list(range(c, replicas, parts)) for c in range(parts)]
        came = list(lax.all_to_all(blocks, "dp", 0, 0, axis_index_groups=groups))
    weight_grad = final(came, width, replicas)
    if not even:
        start = jnp.array(offsets)[lax.axis_index("space"), lax.axis_index("dp")]
        weight_grad = lax.dynamic_slice_in_dim(weight_grad, start, block_rows)

    grad = feature_grad(gradient, gradients[1 % bands], gradients[-1], weight, columns, reach, bands)
    return grad.reshape(1, band_rows, columns, channels), weight_grad


def solution(mesh):
    placed = (
        P("dp", "space", None, None),
        P("dp", "space", None),
        P("dp", "space", None),
        P(),
        P(),
        P(),
    )
    return jax.shard_map(
        on_device,
        mesh=mesh,
        in_specs=placed,
        out_specs=(P("dp", "space", None, None), P(("dp", "space"), None)),
        check_vma=False,
    )
```

```python
import functools

import jax
import jax.numpy as jnp
from jax import lax
from jax.experimental import pallas as pl
from jax.experimental.pallas import tpu as pltpu
from jax.sharding import PartitionSpec as P

DILATION_SIZE = 6
VMEM_LIMIT = 16 * 1024 * 1024
VMEM_WHOLE = 62 * 1024 * 1024


def channel_plan(channels, taps, replicas, bands):
    rows = channels * taps // (replicas * bands)
    starts = [[(d * bands + s) * rows // taps for d in range(replicas)] for s in range(bands)]
    offsets = [[(d * bands + s) * rows % taps for d in range(replicas)] for s in range(bands)]
    cover = max(-(-(off + rows) // taps) for line in offsets for off in line)
    picks = [
        [min(line[d] + k, channels - 1) for d in replica_order(replicas) for k in range(cover)]
        for line in starts
    ]
    return rows, cover, picks, offsets


def replica_order(replicas):
    if replicas % 2:
        return list(range(replicas))
    return list(range(0, replicas, 2)) + list(range(1, replicas, 2))


def shift_columns(array, by, columns):
    if by == 0:
        return array
    size = array.shape[0]
    column = lax.broadcasted_iota(jnp.int32, array.shape, 0) % columns + by
    moved = pltpu.roll(array, (-by) % size, 0)
    return jnp.where((column >= 0) & (column < columns), moved, 0.0)


def tap_row(x, w_ref, a, columns, reach):
    width = w_ref.shape[2]
    weight = jnp.concatenate([w_ref[3 * a + b] for b in range(3)], axis=1)
    product = jnp.dot(x, weight, preferred_element_type=jnp.float32)
    return sum(
        shift_columns(product[:, b * width : (b + 1) * width], (b - 1) * reach, columns)
        for b in range(3)
    )


def load_kernel(replicas, cover, chunks, x_hbm, w_hbm, x_ref, w_ref, *refs):
    *outs, room, x_sems, w_sems, out_sems = refs
    rows = x_ref.shape[0] // chunks
    x_loads, w_loads, copies = [], [], []
    for n in range(chunks):
        here = pl.ds(n * rows, rows)
        x_loads.append(pltpu.make_async_copy(x_hbm.at[here], x_ref.at[here], x_sems.at[n]))
        x_loads[-1].start()
    for a in range(3):
        here = pl.ds(3 * a, 3)
        w_loads.append(pltpu.make_async_copy(w_hbm.at[here], w_ref.at[here], w_sems.at[a]))
        w_loads[-1].start()
    for n in range(chunks):
        x_loads[n].wait()
        here = pl.ds(n * rows, rows)
        for out in outs:
            bands = room.shape[0]
            x = x_ref[here]
            for s in range(bands):
                room[s, here] = jnp.concatenate(
                    [
                        x[:, (d * bands + s) * cover : (d * bands + s + 1) * cover]
                        for d in replica_order(replicas)
                    ],
                    axis=1,
                )
                copies.append(
                    pltpu.make_async_copy(room.at[s, here], out.at[s, here], out_sems.at[n, s])
                )
                copies[-1].start()
    for copy in w_loads + copies:
        copy.wait()


def load(flat, weight, bands, replicas, cover, blocks):
    pixels, channels = flat.shape
    hbm = pl.BlockSpec(memory_space=pltpu.HBM)
    vmem = pl.BlockSpec(memory_space=pltpu.VMEM)
    shape = (bands, pixels, replicas * cover)
    count = 1 if blocks else 0
    chunks = 4 if pixels % 64 == 0 else 1
    return pl.pallas_call(
        functools.partial(load_kernel, replicas, cover, chunks),
        in_specs=[hbm, hbm],
        out_specs=[vmem, vmem] + [hbm] * count,
        out_shape=[
            pltpu.VMEM(flat.shape, flat.dtype),
            pltpu.VMEM(weight.shape, weight.dtype),
        ]
        + [pltpu.HBM(shape, flat.dtype)] * count,
        scratch_shapes=[
            pltpu.VMEM(shape, flat.dtype),
            pltpu.SemaphoreType.DMA((chunks,)),
            pltpu.SemaphoreType.DMA((3,)),
            pltpu.SemaphoreType.DMA((chunks, bands)),
        ],
        compiler_params=pltpu.CompilerParams(vmem_limit_bytes=VMEM_LIMIT),
        cost_estimate=pl.CostEstimate(
            flops=0,
            bytes_accessed=2 * weight.size + 4 * pixels * channels,
            transcendentals=0,
        ),
        name="load",
    )(
        pltpu.with_memory_space_constraint(flat, pltpu.HBM),
        pltpu.with_memory_space_constraint(weight, pltpu.HBM),
    )


def halo_kernel(columns, reach, x_ref, w_ref, down_ref, up_ref):
    pixels, edge = x_ref.shape[0], reach * columns
    width = w_ref.shape[2]
    if pixels > edge:
        down = tap_row(x_ref[pixels - edge :], w_ref, 0, columns, reach)
        up = tap_row(x_ref[:edge], w_ref, 2, columns, reach)
    else:
        weight = jnp.concatenate([w_ref[t] for t in (0, 1, 2, 6, 7, 8)], axis=1)
        product = jnp.dot(x_ref[...], weight, preferred_element_type=jnp.float32)
        down, up = [
            sum(
                shift_columns(
                    product[:, (3 * k + b) * width : (3 * k + b + 1) * width], (b - 1) * reach, columns
                )
                for b in range(3)
            )
            for k in range(2)
        ]
    down_ref[...] = down.astype(down_ref.dtype)
    up_ref[...] = up.astype(up_ref.dtype)


def halo(flat, weight, columns, reach):
    _, channels = flat.shape
    width = weight.shape[2]
    edge = reach * columns
    return pl.pallas_call(
        functools.partial(halo_kernel, columns, reach),
        out_shape=[pltpu.VMEM((edge, width), jnp.bfloat16)] * 2,
        compiler_params=pltpu.CompilerParams(vmem_limit_bytes=VMEM_LIMIT),
        cost_estimate=pl.CostEstimate(
            flops=12 * edge * channels * width,
            bytes_accessed=12 * channels * width + 2 * edge * channels,
            transcendentals=0,
        ),
        name="halo",
    )(flat, weight)


def middle_kernel(columns, reach, x_ref, w_ref, after_ref, out_ref):
    del after_ref
    pixels, edge = x_ref.shape[0], reach * columns
    out_ref[...] = tap_row(x_ref[...], w_ref, 1, columns, reach)
    if pixels > edge:
        out_ref[edge:] += tap_row(x_ref[: pixels - edge], w_ref, 0, columns, reach)
        out_ref[: pixels - edge] += tap_row(x_ref[edge:], w_ref, 2, columns, reach)


def middle_taps(flat, weight, after, columns, reach):
    pixels, channels = flat.shape
    width = weight.shape[2]
    vmem = pl.BlockSpec(memory_space=pltpu.VMEM)
    return pl.pallas_call(
        functools.partial(middle_kernel, columns, reach),
        in_specs=[vmem, vmem, vmem],
        out_shape=pltpu.VMEM((pixels, width), jnp.float32),
        compiler_params=pltpu.CompilerParams(vmem_limit_bytes=VMEM_LIMIT),
        cost_estimate=pl.CostEstimate(
            flops=6 * pixels * channels * width,
            bytes_accessed=6 * channels * width + 2 * pixels * channels,
            transcendentals=0,
        ),
        name="middle_taps",
    )(flat, weight, after)


def as_column(rows_ref):
    values = rows_ref[...].astype(jnp.float32)
    rows, columns = values.shape
    shape = (columns, columns)
    same = lax.broadcasted_iota(jnp.int32, shape, 0) == lax.broadcasted_iota(jnp.int32, shape, 1)
    return jnp.concatenate(
        [
            jnp.sum(jnp.where(same, values[r : r + 1], 0.0), axis=1, keepdims=True)
            for r in range(rows)
        ],
        axis=0,
    )


def pointwise_kernel(
    middle_ref, above_ref, below_ref, bias_ref, class_ref, label_ref, scale_ref, out_ref
):
    pixels, width = middle_ref.shape
    edge = above_ref.shape[0]
    above = above_ref[...].astype(jnp.float32)
    below = below_ref[...].astype(jnp.float32)
    if pixels > edge:
        none = jnp.zeros((pixels - edge, width), jnp.float32)
        above = jnp.concatenate([above, none], axis=0)
        below = jnp.concatenate([none, below], axis=0)
    preact = middle_ref[...] + above + below + bias_ref[...]
    sigmoid_z = jax.nn.sigmoid(preact)
    hidden = (preact * sigmoid_z).astype(jnp.bfloat16)
    classes = class_ref[...]
    logits = lax.dot_general(
        hidden, classes, (((1,), (1,)), ((), ())), preferred_element_type=jnp.float32
    )
    exponent = jnp.exp(logits)
    chances = exponent / jnp.sum(exponent, axis=1, keepdims=True)
    index = lax.broadcasted_iota(jnp.int32, chances.shape, 1).astype(jnp.float32)
    onehot = jnp.where(as_column(label_ref) == index, 1.0, 0.0)
    grad_logits = as_column(scale_ref) * (chances - onehot)
    wide = classes.astype(jnp.float32)
    hidden_grad = sum(
        grad_logits[:, k : k + 1] * wide[k : k + 1] for k in range(classes.shape[0])
    )
    gradient = hidden_grad * sigmoid_z * (1.0 + preact * (1.0 - sigmoid_z))
    out_ref[...] = gradient.astype(out_ref.dtype)


def pointwise(middle, above, below, bias, classes, labels, scale):
    pixels, width = middle.shape
    return pl.pallas_call(
        pointwise_kernel,
        out_shape=jax.ShapeDtypeStruct((pixels, width), jnp.bfloat16),
        compiler_params=pltpu.CompilerParams(vmem_limit_bytes=VMEM_LIMIT),
        cost_estimate=pl.CostEstimate(
            flops=30 * pixels * width,
            bytes_accessed=10 * pixels * width,
            transcendentals=pixels * width,
        ),
        name="pointwise",
    )(middle, above, below, bias, classes, labels, scale)


def shifted_taps(gradient, columns, reach):
    wide = gradient.astype(jnp.float32)
    return jnp.concatenate(
        [shift_columns(wide, (1 - b) * reach, columns).astype(jnp.bfloat16) for b in range(3)],
        axis=1,
    )


def kernel_grad_kernel(columns, reach, parts, others, distances, before, x_ref, *refs):
    count = len(distances)
    g_refs, sums, outs = refs[:count], refs[count : count + before], refs[count + before : -1]
    padded = refs[-1]
    bands, pixels, lanes = x_ref.shape
    width = g_refs[0].shape[1]
    total = bands * pixels
    edge = reach * columns
    extra = lanes // parts
    band = lax.axis_index("space")
    none = jnp.zeros((edge, padded.shape[1]), padded.dtype)
    padded[:edge] = none
    padded[edge + total :] = none
    shifted = [shifted_taps(g_ref[...], columns, reach) for g_ref in g_refs]
    for n, (other, out_ref) in enumerate(zip(others, outs)):
        part = lax.rem(lax.axis_index("dp") + other, parts)
        if extra % 128 == 0:
            features = x_ref[:, :, pl.ds(pl.multiple_of(part * extra, 128), extra)]
        else:
            features = x_ref[:, :, :extra]
            for k in range(1, parts):
                features = jnp.where(part == k, x_ref[:, :, k * extra : (k + 1) * extra], features)
        padded[edge : edge + total] = features.reshape(total, extra)
        for a in range(3):
            here = pl.ds(3 * a * width, 3 * width)
            grad = sums[n][:, here] if before else None
            for k, right in zip(distances, shifted):
                first = lax.rem(band + bands - k, bands) * pixels + a * edge
                left = padded[pl.ds(pl.multiple_of(first, 16), pixels)]
                term = lax.dot_general(
                    left, right, (((0,), (0,)), ((), ())), preferred_element_type=jnp.float32
                )
                grad = term if grad is None else grad + term
            out_ref[:, here] = grad.astype(out_ref.dtype)


def kernel_grad(features, gradients, sums, columns, reach, parts, others, dtype):
    bands, pixels, lanes = features.shape
    extra = lanes // parts
    distances = tuple(gradients)
    width = gradients[distances[0]].shape[1]
    work = len(others) * len(distances) * pixels * extra * width
    return pl.pallas_call(
        functools.partial(
            kernel_grad_kernel, columns, reach, parts, others, distances, len(sums)
        ),
        out_shape=[pltpu.VMEM((extra, 9 * width), dtype)] * len(others),
        scratch_shapes=[pltpu.VMEM((bands * pixels + 2 * reach * columns, extra), features.dtype)],
        compiler_params=pltpu.CompilerParams(vmem_limit_bytes=VMEM_LIMIT),
        cost_estimate=pl.CostEstimate(
            flops=18 * work, bytes_accessed=2 * bands * pixels * lanes, transcendentals=0
        ),
        name="kernel_grad",
    )(features, *gradients.values(), *sums)


def partner(i, k, count):
    return i ^ k if count & (count - 1) == 0 else (i + k) % count


def split_kernel(parts, terms, *refs):
    ins, outs = refs[:terms], refs[terms:]
    count = len(outs)
    cover = outs[0].shape[0]
    me = lax.axis_index("dp") // parts
    for k, out in enumerate(outs):
        if count == 1:
            rows = pl.ds(0, cover)
        else:
            block = jnp.bitwise_xor(me, k) if count & (count - 1) == 0 else lax.rem(me + k, count)
            rows = pl.ds(pl.multiple_of(block * cover, cover), cover)
        total = ins[0][rows, :].astype(jnp.float32)
        for ref in ins[1:]:
            total += ref[rows, :].astype(jnp.float32)
        out[...] = total.astype(out.dtype)


def split_up(terms, parts, count):
    rows, lanes = terms[0].shape
    return pl.pallas_call(
        functools.partial(split_kernel, parts, len(terms)),
        out_shape=[jax.ShapeDtypeStruct((rows // count, lanes), jnp.bfloat16)] * count,
        compiler_params=pltpu.CompilerParams(vmem_limit_bytes=VMEM_LIMIT),
        name="split_up",
    )(*terms)


def final_kernel(replicas, chunks, *refs):
    *ins, out, room, sems = refs
    cover, lanes = ins[0].shape
    width = out.shape[1]
    taps = lanes // width
    step = cover // chunks
    copies = []
    for n in range(chunks):
        here = slice(n * step, (n + 1) * step)
        total = ins[0][here].astype(jnp.float32)
        for ref in ins[1:]:
            total += ref[here].astype(jnp.float32)
        total = total / replicas
        for t in range(taps):
            rows = pl.ds(n * step * taps + t, step, stride=taps)
            room[rows, :] = total[:, t * width : (t + 1) * width]
        rows = pl.ds(n * step * taps, step * taps)
        copies.append(pltpu.make_async_copy(room.at[rows], out.at[rows], sems.at[n]))
        copies[-1].start()
    for copy in copies:
        copy.wait()


def final(blocks, width, replicas):
    cover, lanes = blocks[0].shape
    chunks = 2 if cover % 32 == 0 else 1
    shape = (cover * lanes // width, width)
    return pl.pallas_call(
        functools.partial(final_kernel, replicas, chunks),
        out_specs=pl.BlockSpec(memory_space=pltpu.HBM),
        out_shape=pltpu.HBM(shape, jnp.float32),
        scratch_shapes=[pltpu.VMEM(shape, jnp.float32), pltpu.SemaphoreType.DMA((chunks,))],
        compiler_params=pltpu.CompilerParams(vmem_limit_bytes=VMEM_LIMIT),
        name="final_sum",
    )(*blocks)


def feature_grad_kernel(columns, reach, bands, own_ref, above_ref, below_ref, w_ref, out, room, sems):
    band = lax.axis_index("space")
    pixels, width = own_ref.shape
    edge = reach * columns
    own = own_ref[...]
    above = above_ref[pixels - edge :]
    below = below_ref[:edge]
    above = jnp.where(band > 0, above, jnp.zeros_like(above))
    below = jnp.where(band + 1 < bands, below, jnp.zeros_like(below))
    stack = shifted_taps(jnp.concatenate([above, own, below], axis=0), columns, reach)
    taps = jnp.concatenate(
        [stack[(2 - a) * edge : (2 - a) * edge + pixels] for a in range(3)], axis=1
    )
    steps, _, step = room.shape
    copies = []
    for n in range(steps):
        here = pl.ds(n * step, step)
        weight = jnp.concatenate([w_ref[t, here, :] for t in range(w_ref.shape[0])], axis=1)
        room[n] = lax.dot_general(
            taps, weight, (((1,), (1,)), ((), ())), preferred_element_type=jnp.float32
        )
        copies.append(pltpu.make_async_copy(room.at[n], out.at[:, here], sems.at[n]))
        copies[-1].start()
    for copy in copies:
        copy.wait()


def feature_grad(own, above, below, weight, columns, reach, bands):
    pixels, _ = own.shape
    taps, channels, width = weight.shape
    step = 256 if channels % 256 == 0 else channels
    vmem = pl.BlockSpec(memory_space=pltpu.VMEM)
    return pl.pallas_call(
        functools.partial(feature_grad_kernel, columns, reach, bands),
        in_specs=[vmem] * 4,
        out_specs=pl.BlockSpec(memory_space=pltpu.HBM),
        out_shape=pltpu.HBM((pixels, channels), jnp.float32),
        scratch_shapes=[
            pltpu.VMEM((channels // step, pixels, step), jnp.float32),
            pltpu.SemaphoreType.DMA((channels // step,)),
        ],
        compiler_params=pltpu.CompilerParams(vmem_limit_bytes=VMEM_LIMIT),
        cost_estimate=pl.CostEstimate(
            flops=2 * pixels * taps * channels * width,
            bytes_accessed=2 * taps * channels * width + 4 * pixels * channels,
            transcendentals=0,
        ),
        name="feature_grad",
    )(own, above, below, weight)


def on_device(features, labels, pixel_weight, conv_weight, conv_bias, class_weight):
    image = features[0]
    band_rows, columns, channels = image.shape
    taps, width = conv_weight.shape[1:]
    pixels = band_rows * columns
    replicas = lax.axis_size("dp")
    bands = lax.axis_size("space")
    reach = DILATION_SIZE

    flat = image.reshape(pixels, channels)
    weight = conv_weight.transpose(1, 0, 2)
    block_rows, cover, picks, offsets = channel_plan(channels, taps, replicas, bands)
    even = block_rows % taps == 0
    parts = 2 if replicas % 2 == 0 else 1
    count = replicas // parts
    flat, weight, *split = load(flat, weight, bands, replicas, cover, even)
    if not even:
        order = jnp.array([c for line in picks for c in line], jnp.int32)
        blocks = jnp.take(flat, order, axis=1).reshape(pixels, bands, replicas * cover)
        split = [blocks.transpose(1, 0, 2)]
    whole = lax.all_to_all(split[0], "space", 0, 0)
    down, up = halo(flat, weight, columns, reach)
    above = lax.ppermute(down, "space", [(i, i + 1) for i in range(bands - 1)])
    below = lax.ppermute(up, "space", [(i + 1, i) for i in range(bands - 1)])
    middle = middle_taps(flat, weight, up, columns, reach)

    gradient = pointwise(
        middle,
        above,
        below,
        conv_bias.reshape(1, width),
        class_weight.T,
        labels.reshape(band_rows, columns),
        pixel_weight.reshape(band_rows, columns),
    )
    gradients = [gradient] + [
        lax.ppermute(gradient, "space", [(i, (i + k) % bands) for i in range(bands)])
        for k in range(1, bands)
    ]
    late = bands // 2
    early = {k: g for k, g in enumerate(gradients) if k != late or bands == 1}
    others = (0, 1)[:parts]
    terms = kernel_grad(whole, early, [], columns, reach, parts, others, jnp.float32)
    if bands > 1:
        last = {late: gradients[late]}
        own, *theirs = terms
        terms = kernel_grad(whole, last, [own], columns, reach, parts, (0,), jnp.float32)
        terms += kernel_grad(whole, last, theirs, columns, reach, parts, (1,), jnp.bfloat16) if theirs else []
    if parts == 2:
        theirs = terms[1].astype(jnp.bfloat16)
        terms = [terms[0], lax.ppermute(theirs, "dp", [(i, i ^ 1) for i in range(replicas)])]
    if cover % 16 == 0 and count <= 8:
        blocks = split_up(terms, parts, count)
        came = [blocks[0]]
        for k in reversed(range(1, count)):
            pairs = [(i, parts * partner(i // parts, k, count) + i % parts) for i in range(replicas)]
            came.append(lax.ppermute(blocks[k], "dp", pairs))
    else:
        blocks = split_up(terms, parts, 1)[0].reshape(count, cover, taps * width)
        groups = [list(range(c, replicas, parts)) for c in range(parts)]
        came = list(lax.all_to_all(blocks, "dp", 0, 0, axis_index_groups=groups))
    weight_grad = final(came, width, replicas)
    if not even:
        start = jnp.array(offsets)[lax.axis_index("space"), lax.axis_index("dp")]
        weight_grad = lax.dynamic_slice_in_dim(weight_grad, start, block_rows)

    grad = feature_grad(gradient, gradients[1 % bands], gradients[-1], weight, columns, reach, bands)
    return grad.reshape(1, band_rows, columns, channels), weight_grad


def solution(mesh):
    placed = (
        P("dp", "space", None, None),
        P("dp", "space", None),
        P("dp", "space", None),
        P(),
        P(),
        P(),
    )
    return jax.shard_map(
        on_device,
        mesh=mesh,
        in_specs=placed,
        out_specs=(P("dp", "space", None, None), P(("dp", "space"), None)),
        check_vma=False,
    )
```

```python
import functools

import jax
import jax.numpy as jnp
from jax import lax
from jax.experimental import pallas as pl
from jax.experimental.pallas import tpu as pltpu
from jax.sharding import PartitionSpec as P

DILATION_SIZE = 6
VMEM_LIMIT = 16 * 1024 * 1024
VMEM_WHOLE = 62 * 1024 * 1024


def channel_plan(channels, taps, replicas, bands):
    rows = channels * taps // (replicas * bands)
    starts = [[(d * bands + s) * rows // taps for d in range(replicas)] for s in range(bands)]
    offsets = [[(d * bands + s) * rows % taps for d in range(replicas)] for s in range(bands)]
    cover = max(-(-(off + rows) // taps) for line in offsets for off in line)
    picks = [
        [min(line[d] + k, channels - 1) for d in replica_order(replicas) for k in range(cover)]
        for line in starts
    ]
    return rows, cover, picks, offsets


def replica_order(replicas):
    if replicas % 2:
        return list(range(replicas))
    return list(range(0, replicas, 2)) + list(range(1, replicas, 2))


def shift_columns(array, by, columns):
    if by == 0:
        return array
    size = array.shape[0]
    column = lax.broadcasted_iota(jnp.int32, array.shape, 0) % columns + by
    moved = pltpu.roll(array, (-by) % size, 0)
    return jnp.where((column >= 0) & (column < columns), moved, 0.0)


def tap_row(x, w_ref, a, columns, reach):
    width = w_ref.shape[2]
    weight = jnp.concatenate([w_ref[3 * a + b] for b in range(3)], axis=1)
    product = jnp.dot(x, weight, preferred_element_type=jnp.float32)
    return sum(
        shift_columns(product[:, b * width : (b + 1) * width], (b - 1) * reach, columns)
        for b in range(3)
    )


def load_kernel(replicas, cover, tail, x_hbm, w_hbm, x_ref, w_ref, *refs):
    *outs, room, x_sem, w_sem, out_sems = refs
    outs, tails = outs[:1], outs[1:]
    x_load = pltpu.make_async_copy(x_hbm, x_ref, x_sem)
    w_load = pltpu.make_async_copy(w_hbm, w_ref, w_sem)
    x_load.start()
    w_load.start()
    x_load.wait()
    copies = []
    for out in outs:
        bands = room.shape[0]
        x = x_ref[...]
        for s in range(bands):
            room[s] = jnp.concatenate(
                [
                    x[:, (d * bands + s) * cover : (d * bands + s + 1) * cover]
                    for d in replica_order(replicas)
                ],
                axis=1,
            )
            head = pl.ds(0, out.shape[1])
            copies.append(pltpu.make_async_copy(room.at[s, head], out.at[s], out_sems.at[s]))
            copies[-1].start()
            for tail_ref in tails:
                width = tail_ref.shape[2]
                for p in range(room.shape[2] // width):
                    block = room[s, out.shape[1] :, p * width : (p + 1) * width]
                    tail_ref[s, p * tail : (p + 1) * tail] = block
    w_load.wait()
    for copy in copies:
        copy.wait()


def load(flat, weight, bands, replicas, cover, blocks, tail):
    pixels, channels = flat.shape
    hbm = pl.BlockSpec(memory_space=pltpu.HBM)
    vmem = pl.BlockSpec(memory_space=pltpu.VMEM)
    shape = (bands, pixels, replicas * cover)
    width = weight.shape[2]
    count = 1 if blocks else 0
    tails = 1 if tail else 0
    return pl.pallas_call(
        functools.partial(load_kernel, replicas, cover, tail),
        in_specs=[hbm, hbm],
        out_specs=[vmem, vmem] + [hbm] * count + [vmem] * tails,
        out_shape=[
            pltpu.VMEM(flat.shape, flat.dtype),
            pltpu.VMEM(weight.shape, weight.dtype),
        ]
        + [pltpu.HBM((bands, pixels - tail, shape[2]), flat.dtype)] * count
        + [pltpu.VMEM((bands, shape[2] // width * tail, width), flat.dtype)] * tails,
        scratch_shapes=[
            pltpu.VMEM(shape, flat.dtype),
            pltpu.SemaphoreType.DMA,
            pltpu.SemaphoreType.DMA,
            pltpu.SemaphoreType.DMA((bands,)),
        ],
        compiler_params=pltpu.CompilerParams(vmem_limit_bytes=VMEM_LIMIT),
        cost_estimate=pl.CostEstimate(
            flops=0,
            bytes_accessed=2 * weight.size + 4 * pixels * channels,
            transcendentals=0,
        ),
        name="load",
    )(
        pltpu.with_memory_space_constraint(flat, pltpu.HBM),
        pltpu.with_memory_space_constraint(weight, pltpu.HBM),
    )


def halo_kernel(columns, reach, x_ref, w_ref, down_ref, up_ref):
    pixels, edge = x_ref.shape[0], reach * columns
    width = w_ref.shape[2]
    if pixels > edge:
        down = tap_row(x_ref[pixels - edge :], w_ref, 0, columns, reach)
        up = tap_row(x_ref[:edge], w_ref, 2, columns, reach)
    else:
        weight = jnp.concatenate([w_ref[t] for t in (0, 1, 2, 6, 7, 8)], axis=1)
        product = jnp.dot(x_ref[...], weight, preferred_element_type=jnp.float32)
        down, up = [
            sum(
                shift_columns(
                    product[:, (3 * k + b) * width : (3 * k + b + 1) * width], (b - 1) * reach, columns
                )
                for b in range(3)
            )
            for k in range(2)
        ]
    down_ref[...] = down.astype(down_ref.dtype)
    up_ref[...] = up.astype(up_ref.dtype)


def halo(flat, weight, columns, reach):
    _, channels = flat.shape
    width = weight.shape[2]
    edge = reach * columns
    return pl.pallas_call(
        functools.partial(halo_kernel, columns, reach),
        out_shape=[pltpu.VMEM((edge, width), jnp.bfloat16)] * 2,
        compiler_params=pltpu.CompilerParams(vmem_limit_bytes=VMEM_LIMIT),
        cost_estimate=pl.CostEstimate(
            flops=12 * edge * channels * width,
            bytes_accessed=12 * channels * width + 2 * edge * channels,
            transcendentals=0,
        ),
        name="halo",
    )(flat, weight)


def middle_kernel(columns, reach, x_ref, w_ref, after_ref, out_ref):
    del after_ref
    pixels, edge = x_ref.shape[0], reach * columns
    out_ref[...] = tap_row(x_ref[...], w_ref, 1, columns, reach)
    if pixels > edge:
        out_ref[edge:] += tap_row(x_ref[: pixels - edge], w_ref, 0, columns, reach)
        out_ref[: pixels - edge] += tap_row(x_ref[edge:], w_ref, 2, columns, reach)


def middle_taps(flat, weight, after, columns, reach):
    pixels, channels = flat.shape
    width = weight.shape[2]
    vmem = pl.BlockSpec(memory_space=pltpu.VMEM)
    return pl.pallas_call(
        functools.partial(middle_kernel, columns, reach),
        in_specs=[vmem, vmem, vmem],
        out_shape=pltpu.VMEM((pixels, width), jnp.float32),
        compiler_params=pltpu.CompilerParams(vmem_limit_bytes=VMEM_LIMIT),
        cost_estimate=pl.CostEstimate(
            flops=6 * pixels * channels * width,
            bytes_accessed=6 * channels * width + 2 * pixels * channels,
            transcendentals=0,
        ),
        name="middle_taps",
    )(flat, weight, after)


def as_column(rows_ref):
    values = rows_ref[...].astype(jnp.float32)
    rows, columns = values.shape
    shape = (columns, columns)
    same = lax.broadcasted_iota(jnp.int32, shape, 0) == lax.broadcasted_iota(jnp.int32, shape, 1)
    return jnp.concatenate(
        [
            jnp.sum(jnp.where(same, values[r : r + 1], 0.0), axis=1, keepdims=True)
            for r in range(rows)
        ],
        axis=0,
    )


def pointwise_kernel(
    extras, middle_ref, above_ref, below_ref, bias_ref, class_ref, label_ref, scale_ref, *refs
):
    pixels, width = middle_ref.shape
    edge = above_ref.shape[0]
    above = above_ref[...].astype(jnp.float32)
    below = below_ref[...].astype(jnp.float32)
    if pixels > edge:
        none = jnp.zeros((pixels - edge, width), jnp.float32)
        above = jnp.concatenate([above, none], axis=0)
        below = jnp.concatenate([none, below], axis=0)
    preact = middle_ref[...] + above + below + bias_ref[...]
    sigmoid_z = jax.nn.sigmoid(preact)
    hidden = (preact * sigmoid_z).astype(jnp.bfloat16)
    classes = class_ref[...]
    logits = lax.dot_general(
        hidden, classes, (((1,), (1,)), ((), ())), preferred_element_type=jnp.float32
    )
    exponent = jnp.exp(logits)
    chances = exponent / jnp.sum(exponent, axis=1, keepdims=True)
    index = lax.broadcasted_iota(jnp.int32, chances.shape, 1).astype(jnp.float32)
    onehot = jnp.where(as_column(label_ref) == index, 1.0, 0.0)
    grad_logits = as_column(scale_ref) * (chances - onehot)
    wide = classes.astype(jnp.float32)
    hidden_grad = sum(
        grad_logits[:, k : k + 1] * wide[k : k + 1] for k in range(classes.shape[0])
    )
    gradient = hidden_grad * sigmoid_z * (1.0 + preact * (1.0 - sigmoid_z))
    gradient = gradient.astype(jnp.bfloat16)
    tails, outs = refs[:extras], refs[extras:]
    band = lax.axis_index("space")
    bands = len(outs)
    outs[0][...] = gradient
    for k in range(1, bands):
        outs[k][:pixels] = gradient
        for tail_ref in tails:
            outs[k][pixels:] = tail_ref[lax.rem(band + k, bands)]


def pointwise(middle, above, below, bias, classes, labels, scale, bands, tails):
    pixels, width = middle.shape
    rows = pixels + sum(t.shape[1] for t in tails)
    shapes = [(pixels, width)] + [(rows, width)] * (bands - 1)
    return pl.pallas_call(
        functools.partial(pointwise_kernel, len(tails)),
        out_shape=[pltpu.VMEM(shape, jnp.bfloat16) for shape in shapes],
        compiler_params=pltpu.CompilerParams(vmem_limit_bytes=VMEM_LIMIT),
        cost_estimate=pl.CostEstimate(
            flops=30 * pixels * width,
            bytes_accessed=10 * pixels * width,
            transcendentals=pixels * width,
        ),
        name="pointwise",
    )(middle, above, below, bias, classes, labels, scale, *tails)


def shifted_taps(gradient, columns, reach):
    wide = gradient.astype(jnp.float32)
    return jnp.concatenate(
        [shift_columns(wide, (1 - b) * reach, columns).astype(jnp.bfloat16) for b in range(3)],
        axis=1,
    )


def kernel_grad_kernel(columns, reach, parts, others, here, late, before, tail, x_ref, *refs):
    bands, head, lanes = x_ref.shape
    g_refs, refs = refs[:bands], refs[bands:]
    tails, refs = refs[: 1 if tail else 0], refs[1 if tail else 0 :]
    sums, outs, padded = refs[:before], refs[before:-1], refs[-1]
    pixels, width = g_refs[0].shape
    total = bands * pixels
    edge = reach * columns
    extra = lanes // parts
    band = lax.axis_index("space")
    none = jnp.zeros((edge, extra), padded.dtype)
    padded[:edge] = none
    padded[edge + total :] = none
    shifted = {k: shifted_taps(g_refs[k][:pixels], columns, reach) for k in here}
    last = lax.rem(band + bands - late, bands)
    near = {}
    if tail and before:
        for a, k in ((0, (late - 1) % bands), (2, (late + 1) % bands)):
            rows = shifted_taps(g_refs[k][:pixels], columns, reach)[head:]
            there = (last + 1 < bands) if a == 0 else (last > 0)
            near[a] = jnp.where(there, rows, jnp.zeros_like(rows))
    for n, (other, out_ref) in enumerate(zip(others, outs)):
        part = lax.rem(lax.axis_index("dp") + other, parts)
        if extra % 128 == 0:
            features = x_ref[:, :, pl.ds(pl.multiple_of(part * extra, 128), extra)]
        else:
            features = x_ref[:, :, :extra]
            for k in range(1, parts):
                features = jnp.where(part == k, x_ref[:, :, k * extra : (k + 1) * extra], features)
        for s in range(bands):
            padded[edge + s * pixels : edge + s * pixels + head] = features[s]
        for tail_ref in tails:
            for k in range(bands):
                from_band = lax.rem(band + bands - k, bands)
                rows = pl.multiple_of(part * tail, 16)
                if k == late and not before:
                    block = jnp.zeros((tail, extra), padded.dtype)
                elif k:
                    block = g_refs[k][pl.ds(pixels + rows, tail)]
                else:
                    block = tail_ref[band, pl.ds(rows, tail)]
                start = pl.multiple_of(edge + from_band * pixels + head, 16)
                padded[pl.ds(start, tail)] = block
        for a in range(3):
            lane = pl.ds(3 * a * width, 3 * width)
            grad = sums[n][:, lane] if before else None
            pairs = []
            for k, right in shifted.items():
                first = lax.rem(band + bands - k, bands) * pixels + a * edge
                pairs.append((padded[pl.ds(pl.multiple_of(first, 16), pixels)], right))
            if a in near:
                start = pl.multiple_of(edge + last * pixels + head, 16)
                pairs.append((padded[pl.ds(start, tail)], near[a]))
            for left, right in pairs:
                term = lax.dot_general(
                    left, right, (((0,), (0,)), ((), ())), preferred_element_type=jnp.float32
                )
                grad = term if grad is None else grad + term
            out_ref[:, lane] = grad.astype(out_ref.dtype)


def kernel_grad(features, gradients, tails, sums, columns, reach, parts, others, late, dtype):
    bands, head, lanes = features.shape
    pixels, width = gradients[0].shape
    extra = lanes // parts
    here = [late] if sums else [k for k in range(bands) if k != late or bands == 1]
    work = len(others) * len(here) * pixels * extra * width
    given = list(gradients)
    if not sums and bands > 1:
        given[late] = gradients[0]
    return pl.pallas_call(
        functools.partial(
            kernel_grad_kernel, columns, reach, parts, others, here, late, len(sums), pixels - head
        ),
        out_shape=[pltpu.VMEM((extra, 9 * width), dtype)] * len(others),
        scratch_shapes=[pltpu.VMEM((bands * pixels + 2 * reach * columns, extra), features.dtype)],
        compiler_params=pltpu.CompilerParams(vmem_limit_bytes=VMEM_LIMIT),
        cost_estimate=pl.CostEstimate(
            flops=18 * work, bytes_accessed=2 * bands * pixels * lanes, transcendentals=0
        ),
        name="kernel_grad",
    )(features, *given, *tails, *sums)


def partner(i, k, count):
    return i ^ k if count & (count - 1) == 0 else (i + k) % count


def split_kernel(parts, terms, *refs):
    ins, outs = refs[:terms], refs[terms:]
    count = len(outs)
    cover = outs[0].shape[0]
    me = lax.axis_index("dp") // parts
    for k, out in enumerate(outs):
        if count == 1:
            rows = pl.ds(0, cover)
        else:
            block = jnp.bitwise_xor(me, k) if count & (count - 1) == 0 else lax.rem(me + k, count)
            rows = pl.ds(pl.multiple_of(block * cover, cover), cover)
        total = ins[0][rows, :].astype(jnp.float32)
        for ref in ins[1:]:
            total += ref[rows, :].astype(jnp.float32)
        out[...] = total.astype(out.dtype)


def split_up(terms, parts, count):
    rows, lanes = terms[0].shape
    return pl.pallas_call(
        functools.partial(split_kernel, parts, len(terms)),
        out_shape=[jax.ShapeDtypeStruct((rows // count, lanes), jnp.bfloat16)] * count,
        compiler_params=pltpu.CompilerParams(vmem_limit_bytes=VMEM_LIMIT),
        name="split_up",
    )(*terms)


def final_kernel(replicas, *refs):
    *ins, out_ref = refs
    cover, lanes = ins[0].shape
    width = out_ref.shape[1]
    taps = lanes // width
    total = ins[0][...].astype(jnp.float32)
    for ref in ins[1:]:
        total += ref[...].astype(jnp.float32)
    total = total / replicas
    for t in range(taps):
        out_ref[pl.ds(t, cover, stride=taps), :] = total[:, t * width : (t + 1) * width]


def final(blocks, width, replicas):
    cover, lanes = blocks[0].shape
    return pl.pallas_call(
        functools.partial(final_kernel, replicas),
        out_shape=jax.ShapeDtypeStruct((cover * lanes // width, width), jnp.float32),
        compiler_params=pltpu.CompilerParams(vmem_limit_bytes=VMEM_LIMIT),
        name="final_sum",
    )(*blocks)


def feature_grad_kernel(columns, reach, bands, own_ref, above_ref, below_ref, w_ref, out, room, sems):
    band = lax.axis_index("space")
    pixels, width = own_ref.shape
    edge = reach * columns
    own = own_ref[...]
    above = above_ref[pixels - edge : pixels]
    below = below_ref[:edge]
    above = jnp.where(band > 0, above, jnp.zeros_like(above))
    below = jnp.where(band + 1 < bands, below, jnp.zeros_like(below))
    stack = shifted_taps(jnp.concatenate([above, own, below], axis=0), columns, reach)
    taps = jnp.concatenate(
        [stack[(2 - a) * edge : (2 - a) * edge + pixels] for a in range(3)], axis=1
    )
    steps, _, step = room.shape
    copies = []
    for n in range(steps):
        here = pl.ds(n * step, step)
        weight = jnp.concatenate([w_ref[t, here, :] for t in range(w_ref.shape[0])], axis=1)
        room[n] = lax.dot_general(
            taps, weight, (((1,), (1,)), ((), ())), preferred_element_type=jnp.float32
        )
        copies.append(pltpu.make_async_copy(room.at[n], out.at[:, here], sems.at[n]))
        copies[-1].start()
    for copy in copies:
        copy.wait()


def feature_grad(own, above, below, weight, columns, reach, bands):
    pixels, _ = own.shape
    taps, channels, width = weight.shape
    step = 256 if channels % 256 == 0 else channels
    vmem = pl.BlockSpec(memory_space=pltpu.VMEM)
    return pl.pallas_call(
        functools.partial(feature_grad_kernel, columns, reach, bands),
        in_specs=[vmem] * 4,
        out_specs=pl.BlockSpec(memory_space=pltpu.HBM),
        out_shape=pltpu.HBM((pixels, channels), jnp.float32),
        scratch_shapes=[
            pltpu.VMEM((channels // step, pixels, step), jnp.float32),
            pltpu.SemaphoreType.DMA((channels // step,)),
        ],
        compiler_params=pltpu.CompilerParams(vmem_limit_bytes=VMEM_LIMIT),
        cost_estimate=pl.CostEstimate(
            flops=2 * pixels * taps * channels * width,
            bytes_accessed=2 * taps * channels * width + 4 * pixels * channels,
            transcendentals=0,
        ),
        name="feature_grad",
    )(own, above, below, weight)


def on_device(features, labels, pixel_weight, conv_weight, conv_bias, class_weight):
    image = features[0]
    band_rows, columns, channels = image.shape
    taps, width = conv_weight.shape[1:]
    pixels = band_rows * columns
    replicas = lax.axis_size("dp")
    bands = lax.axis_size("space")
    reach = DILATION_SIZE

    flat = image.reshape(pixels, channels)
    weight = conv_weight.transpose(1, 0, 2)
    block_rows, cover, picks, offsets = channel_plan(channels, taps, replicas, bands)
    even = block_rows % taps == 0
    parts = 2 if replicas % 2 == 0 else 1
    count = replicas // parts
    apart = even and bands > 1 and band_rows == reach and count * cover == width
    tail = pixels // 6 // 16 * 16 if apart else 0
    flat, weight, *split = load(flat, weight, bands, replicas, cover, even, tail)
    tails = split[1:]
    if not even:
        order = jnp.array([c for line in picks for c in line], jnp.int32)
        blocks = jnp.take(flat, order, axis=1).reshape(pixels, bands, replicas * cover)
        split = [blocks.transpose(1, 0, 2)]
    whole = lax.all_to_all(split[0], "space", 0, 0)
    down, up = halo(flat, weight, columns, reach)
    above = lax.ppermute(down, "space", [(i, i + 1) for i in range(bands - 1)])
    below = lax.ppermute(up, "space", [(i + 1, i) for i in range(bands - 1)])
    middle = middle_taps(flat, weight, up, columns, reach)

    gradient, *packed = pointwise(
        middle,
        above,
        below,
        conv_bias.reshape(1, width),
        class_weight.T,
        labels.reshape(band_rows, columns),
        pixel_weight.reshape(band_rows, columns),
        bands,
        tails,
    )
    gradients = [gradient] + [
        lax.ppermute(packed[k - 1], "space", [(i, (i + k) % bands) for i in range(bands)])
        for k in range(1, bands)
    ]
    late = bands // 2
    grads = functools.partial(kernel_grad, whole, gradients, tails)
    terms = grads([], columns, reach, parts, (0, 1)[:parts], late, jnp.float32)
    if bands > 1:
        own, *theirs = terms
        terms = grads([own], columns, reach, parts, (0,), late, jnp.float32)
        if theirs:
            terms += grads(theirs, columns, reach, parts, (1,), late, jnp.bfloat16)
    if parts == 2:
        theirs = terms[1].astype(jnp.bfloat16)
        terms = [terms[0], lax.ppermute(theirs, "dp", [(i, i ^ 1) for i in range(replicas)])]
    if cover % 16 == 0 and count <= 8:
        blocks = split_up(terms, parts, count)
        came = [blocks[0]]
        for k in reversed(range(1, count)):
            pairs = [(i, parts * partner(i // parts, k, count) + i % parts) for i in range(replicas)]
            came.append(lax.ppermute(blocks[k], "dp", pairs))
    else:
        blocks = split_up(terms, parts, 1)[0].reshape(count, cover, taps * width)
        groups = [list(range(c, replicas, parts)) for c in range(parts)]
        came = list(lax.all_to_all(blocks, "dp", 0, 0, axis_index_groups=groups))
    weight_grad = final(came, width, replicas)
    if not even:
        start = jnp.array(offsets)[lax.axis_index("space"), lax.axis_index("dp")]
        weight_grad = lax.dynamic_slice_in_dim(weight_grad, start, block_rows)

    grad = feature_grad(gradient, gradients[1 % bands], gradients[-1], weight, columns, reach, bands)
    return grad.reshape(1, band_rows, columns, channels), weight_grad


def solution(mesh):
    placed = (
        P("dp", "space", None, None),
        P("dp", "space", None),
        P("dp", "space", None),
        P(),
        P(),
        P(),
    )
    return jax.shard_map(
        on_device,
        mesh=mesh,
        in_specs=placed,
        out_specs=(P("dp", "space", None, None), P(("dp", "space"), None)),
        check_vma=False,
    )
```

```python
import functools

import jax
import jax.numpy as jnp
from jax import lax
from jax.experimental import pallas as pl
from jax.experimental.pallas import tpu as pltpu
from jax.sharding import PartitionSpec as P

DILATION_SIZE = 6
VMEM_LIMIT = 16 * 1024 * 1024
VMEM_WHOLE = 62 * 1024 * 1024


def channel_plan(channels, taps, replicas, bands):
    rows = channels * taps // (replicas * bands)
    starts = [[(d * bands + s) * rows // taps for d in range(replicas)] for s in range(bands)]
    offsets = [[(d * bands + s) * rows % taps for d in range(replicas)] for s in range(bands)]
    cover = max(-(-(off + rows) // taps) for line in offsets for off in line)
    picks = [
        [min(line[d] + k, channels - 1) for d in replica_order(replicas) for k in range(cover)]
        for line in starts
    ]
    return rows, cover, picks, offsets


def replica_order(replicas):
    if replicas % 2:
        return list(range(replicas))
    return list(range(0, replicas, 2)) + list(range(1, replicas, 2))


def shift_columns(array, by, columns):
    if by == 0:
        return array
    size = array.shape[0]
    column = lax.broadcasted_iota(jnp.int32, array.shape, 0) % columns + by
    moved = pltpu.roll(array, (-by) % size, 0)
    return jnp.where((column >= 0) & (column < columns), moved, 0.0)


def tap_row(x, w_ref, a, columns, reach):
    width = w_ref.shape[2]
    weight = jnp.concatenate([w_ref[3 * a + b] for b in range(3)], axis=1)
    product = jnp.dot(x, weight, preferred_element_type=jnp.float32)
    return sum(
        shift_columns(product[:, b * width : (b + 1) * width], (b - 1) * reach, columns)
        for b in range(3)
    )


def load_kernel(replicas, cover, x_hbm, w_hbm, x_ref, w_ref, *refs):
    *outs, room, x_sem, w_sem, out_sems = refs
    x_load = pltpu.make_async_copy(x_hbm, x_ref, x_sem)
    w_load = pltpu.make_async_copy(w_hbm, w_ref, w_sem)
    x_load.start()
    w_load.start()
    x_load.wait()
    copies = []
    for out in outs:
        bands = room.shape[0]
        x = x_ref[...]
        for s in range(bands):
            room[s] = jnp.concatenate(
                [
                    x[:, (d * bands + s) * cover : (d * bands + s + 1) * cover]
                    for d in replica_order(replicas)
                ],
                axis=1,
            )
            copies.append(pltpu.make_async_copy(room.at[s], out.at[s], out_sems.at[s]))
            copies[-1].start()
    w_load.wait()
    for copy in copies:
        copy.wait()


def load(flat, weight, bands, replicas, cover, blocks):
    pixels, channels = flat.shape
    hbm = pl.BlockSpec(memory_space=pltpu.HBM)
    vmem = pl.BlockSpec(memory_space=pltpu.VMEM)
    shape = (bands, pixels, replicas * cover)
    count = 1 if blocks else 0
    return pl.pallas_call(
        functools.partial(load_kernel, replicas, cover),
        in_specs=[hbm, hbm],
        out_specs=[vmem, vmem] + [hbm] * count,
        out_shape=[
            pltpu.VMEM(flat.shape, flat.dtype),
            pltpu.VMEM(weight.shape, weight.dtype),
        ]
        + [pltpu.HBM(shape, flat.dtype)] * count,
        scratch_shapes=[
            pltpu.VMEM(shape, flat.dtype),
            pltpu.SemaphoreType.DMA,
            pltpu.SemaphoreType.DMA,
            pltpu.SemaphoreType.DMA((bands,)),
        ],
        compiler_params=pltpu.CompilerParams(vmem_limit_bytes=VMEM_LIMIT),
        cost_estimate=pl.CostEstimate(
            flops=0,
            bytes_accessed=2 * weight.size + 4 * pixels * channels,
            transcendentals=0,
        ),
        name="load",
    )(
        pltpu.with_memory_space_constraint(flat, pltpu.HBM),
        pltpu.with_memory_space_constraint(weight, pltpu.HBM),
    )


def halo_sums(x_ref, w_ref, columns, reach):
    pixels, edge = x_ref.shape[0], reach * columns
    width = w_ref.shape[2]
    if pixels > edge:
        down = tap_row(x_ref[pixels - edge :], w_ref, 0, columns, reach)
        up = tap_row(x_ref[:edge], w_ref, 2, columns, reach)
        return down, up
    weight = jnp.concatenate([w_ref[t] for t in (0, 1, 2, 6, 7, 8)], axis=1)
    product = jnp.dot(x_ref[...], weight, preferred_element_type=jnp.float32)
    return [
        sum(
            shift_columns(
                product[:, (3 * k + b) * width : (3 * k + b + 1) * width], (b - 1) * reach, columns
            )
            for b in range(3)
        )
        for k in range(2)
    ]


def lay_out_kernel(columns, reach, replicas, cover, x_hbm, w_hbm, x_ref, w_ref, *refs):
    *blocks, room, x_sem, w_sems = refs
    bands = len(blocks)
    band = lax.axis_index("space")
    lanes = room.shape[2]
    x_load = pltpu.make_async_copy(x_hbm, x_ref, x_sem)
    x_load.start()
    w_loads = []
    for n, (t, size) in enumerate(((0, 3), (6, 3), (3, 3))):
        here = pl.ds(t, size)
        w_loads.append(pltpu.make_async_copy(w_hbm.at[here], w_ref.at[here], w_sems.at[n]))
        w_loads[-1].start()
    x_load.wait()
    x = x_ref[...]
    for s in range(bands):
        room[s] = jnp.concatenate(
            [
                x[:, (d * bands + s) * cover : (d * bands + s + 1) * cover]
                for d in replica_order(replicas)
            ],
            axis=1,
        )
    for k, block in enumerate(blocks):
        block[:, :lanes] = room[jnp.bitwise_xor(band, k)]
    w_loads[0].wait()
    w_loads[1].wait()
    down, up = halo_sums(x_ref, w_ref, columns, reach)
    blocks[1][:, lanes:] = jnp.where(lax.rem(band, 2) == 0, down, up).astype(x.dtype)
    blocks[3][:, lanes:] = jnp.where(band < 2, down, up).astype(x.dtype)
    w_loads[2].wait()


def lay_out(flat, weight, columns, reach, bands, replicas, cover):
    pixels, channels = flat.shape
    width = weight.shape[2]
    hbm = pl.BlockSpec(memory_space=pltpu.HBM)
    vmem = pl.BlockSpec(memory_space=pltpu.VMEM)
    lanes = replicas * cover
    shapes = [(pixels, lanes + (width if k % 2 else 0)) for k in range(bands)]
    return pl.pallas_call(
        functools.partial(lay_out_kernel, columns, reach, replicas, cover),
        in_specs=[hbm, hbm],
        out_specs=[vmem] * (2 + bands),
        out_shape=[
            pltpu.VMEM(flat.shape, flat.dtype),
            pltpu.VMEM(weight.shape, weight.dtype),
        ]
        + [pltpu.VMEM(shape, flat.dtype) for shape in shapes],
        scratch_shapes=[
            pltpu.VMEM((bands, pixels, lanes), flat.dtype),
            pltpu.SemaphoreType.DMA,
            pltpu.SemaphoreType.DMA((3,)),
        ],
        compiler_params=pltpu.CompilerParams(vmem_limit_bytes=VMEM_LIMIT),
        cost_estimate=pl.CostEstimate(
            flops=12 * pixels * channels * width,
            bytes_accessed=2 * weight.size + 4 * pixels * channels,
            transcendentals=0,
        ),
        name="lay_out",
    )(
        pltpu.with_memory_space_constraint(flat, pltpu.HBM),
        pltpu.with_memory_space_constraint(weight, pltpu.HBM),
    )


def halo_kernel(columns, reach, x_ref, w_ref, down_ref, up_ref):
    down, up = halo_sums(x_ref, w_ref, columns, reach)
    down_ref[...] = down.astype(down_ref.dtype)
    up_ref[...] = up.astype(up_ref.dtype)


def halo(flat, weight, columns, reach):
    _, channels = flat.shape
    width = weight.shape[2]
    edge = reach * columns
    return pl.pallas_call(
        functools.partial(halo_kernel, columns, reach),
        out_shape=[pltpu.VMEM((edge, width), jnp.bfloat16)] * 2,
        compiler_params=pltpu.CompilerParams(vmem_limit_bytes=VMEM_LIMIT),
        cost_estimate=pl.CostEstimate(
            flops=12 * edge * channels * width,
            bytes_accessed=12 * channels * width + 2 * edge * channels,
            transcendentals=0,
        ),
        name="halo",
    )(flat, weight)


def middle_kernel(columns, reach, x_ref, w_ref, after_ref, out_ref):
    del after_ref
    pixels, edge = x_ref.shape[0], reach * columns
    out_ref[...] = tap_row(x_ref[...], w_ref, 1, columns, reach)
    if pixels > edge:
        out_ref[edge:] += tap_row(x_ref[: pixels - edge], w_ref, 0, columns, reach)
        out_ref[: pixels - edge] += tap_row(x_ref[edge:], w_ref, 2, columns, reach)


def middle_taps(flat, weight, after, columns, reach):
    pixels, channels = flat.shape
    width = weight.shape[2]
    vmem = pl.BlockSpec(memory_space=pltpu.VMEM)
    return pl.pallas_call(
        functools.partial(middle_kernel, columns, reach),
        in_specs=[vmem, vmem, vmem],
        out_shape=pltpu.VMEM((pixels, width), jnp.float32),
        compiler_params=pltpu.CompilerParams(vmem_limit_bytes=VMEM_LIMIT),
        cost_estimate=pl.CostEstimate(
            flops=6 * pixels * channels * width,
            bytes_accessed=6 * channels * width + 2 * pixels * channels,
            transcendentals=0,
        ),
        name="middle_taps",
    )(flat, weight, after)


def as_column(rows_ref):
    values = rows_ref[...].astype(jnp.float32)
    rows, columns = values.shape
    shape = (columns, columns)
    same = lax.broadcasted_iota(jnp.int32, shape, 0) == lax.broadcasted_iota(jnp.int32, shape, 1)
    return jnp.concatenate(
        [
            jnp.sum(jnp.where(same, values[r : r + 1], 0.0), axis=1, keepdims=True)
            for r in range(rows)
        ],
        axis=0,
    )


def pointwise_kernel(
    paired, middle_ref, above_ref, below_ref, bias_ref, class_ref, label_ref, scale_ref, out_ref
):
    pixels, width = middle_ref.shape
    edge = above_ref.shape[0]
    above = above_ref[:, above_ref.shape[1] - width :].astype(jnp.float32)
    below = below_ref[:, below_ref.shape[1] - width :].astype(jnp.float32)
    if paired:
        band = lax.axis_index("space")
        below = jnp.where((band == 1) | (band == 2), below, 0.0)
    if pixels > edge:
        none = jnp.zeros((pixels - edge, width), jnp.float32)
        above = jnp.concatenate([above, none], axis=0)
        below = jnp.concatenate([none, below], axis=0)
    preact = middle_ref[...] + above + below + bias_ref[...]
    sigmoid_z = jax.nn.sigmoid(preact)
    hidden = (preact * sigmoid_z).astype(jnp.bfloat16)
    classes = class_ref[...]
    logits = lax.dot_general(
        hidden, classes, (((1,), (1,)), ((), ())), preferred_element_type=jnp.float32
    )
    exponent = jnp.exp(logits)
    chances = exponent / jnp.sum(exponent, axis=1, keepdims=True)
    index = lax.broadcasted_iota(jnp.int32, chances.shape, 1).astype(jnp.float32)
    onehot = jnp.where(as_column(label_ref) == index, 1.0, 0.0)
    grad_logits = as_column(scale_ref) * (chances - onehot)
    wide = classes.astype(jnp.float32)
    hidden_grad = sum(
        grad_logits[:, k : k + 1] * wide[k : k + 1] for k in range(classes.shape[0])
    )
    gradient = hidden_grad * sigmoid_z * (1.0 + preact * (1.0 - sigmoid_z))
    out_ref[...] = gradient.astype(out_ref.dtype)


def pointwise(middle, above, below, bias, classes, labels, scale, paired):
    pixels, width = middle.shape
    return pl.pallas_call(
        functools.partial(pointwise_kernel, paired),
        out_shape=jax.ShapeDtypeStruct((pixels, width), jnp.bfloat16),
        compiler_params=pltpu.CompilerParams(vmem_limit_bytes=VMEM_LIMIT),
        cost_estimate=pl.CostEstimate(
            flops=30 * pixels * width,
            bytes_accessed=10 * pixels * width,
            transcendentals=pixels * width,
        ),
        name="pointwise",
    )(middle, above, below, bias, classes, labels, scale)


def shifted_taps(gradient, columns, reach):
    wide = gradient.astype(jnp.float32)
    return jnp.concatenate(
        [shift_columns(wide, (1 - b) * reach, columns).astype(jnp.bfloat16) for b in range(3)],
        axis=1,
    )


def kernel_grad_kernel(columns, reach, parts, others, distances, before, given, lanes, *refs):
    x_refs, refs = refs[:given], refs[given:]
    count = len(distances)
    g_refs, sums, outs = refs[:count], refs[count : count + before], refs[count + before : -1]
    padded = refs[-1]
    pixels, width = g_refs[0].shape
    total = padded.shape[1] - 2 * reach * columns
    bands = total // pixels
    edge = reach * columns
    extra = lanes // parts
    band = lax.axis_index("space")
    slots = given > 1
    shifted = [shifted_taps(g_ref[...], columns, reach) for g_ref in g_refs]
    for n, (other, out_ref) in enumerate(zip(others, outs)):
        part = lax.rem(lax.axis_index("dp") + other, parts)
        for k, x_ref in enumerate(x_refs):
            if extra % 128 == 0:
                features = x_ref[..., pl.ds(pl.multiple_of(part * extra, 128), extra)]
            else:
                features = x_ref[..., :extra]
                for j in range(1, parts):
                    other_part = x_ref[..., j * extra : (j + 1) * extra]
                    features = jnp.where(part == j, other_part, features)
            if slots:
                padded[n, k * pixels : (k + 1) * pixels] = features
            else:
                padded[n, edge : edge + total] = features.reshape(total, extra)
        if slots:
            padded[n, total : total + pixels] = jnp.zeros((pixels, extra), padded.dtype)
        else:
            padded[n, :edge] = jnp.zeros((edge, extra), padded.dtype)
            padded[n, edge + total :] = jnp.zeros((edge, extra), padded.dtype)
        for a in range(3):
            here = pl.ds(3 * a * width, 3 * width)
            grad = sums[n][:, here] if before else None
            for k, right in zip(distances, shifted):
                from_band = lax.rem(band + bands - k, bands)
                if slots:
                    row = from_band + (a - 1)
                    inside = (row >= 0) & (row < bands)
                    slot = jnp.bitwise_xor(band, jnp.clip(row, 0, bands - 1))
                    first = jnp.where(inside, slot, bands) * pixels
                else:
                    first = from_band * pixels + a * edge
                left = padded[n, pl.ds(pl.multiple_of(first, 16), pixels)]
                term = lax.dot_general(
                    left, right, (((0,), (0,)), ((), ())), preferred_element_type=jnp.float32
                )
                grad = term if grad is None else grad + term
            out_ref[:, here] = grad.astype(out_ref.dtype)


def kernel_grad(features, gradients, sums, columns, reach, parts, others, dtype, bands, lanes):
    distances = tuple(gradients)
    pixels, width = gradients[distances[0]].shape
    extra = lanes // parts
    work = len(others) * len(distances) * pixels * extra * width
    return pl.pallas_call(
        functools.partial(
            kernel_grad_kernel,
            columns,
            reach,
            parts,
            others,
            distances,
            len(sums),
            len(features),
            lanes,
        ),
        out_shape=[pltpu.VMEM((extra, 9 * width), dtype)] * len(others),
        scratch_shapes=[pltpu.VMEM((len(others), bands * pixels + 2 * reach * columns, extra), jnp.bfloat16)],
        compiler_params=pltpu.CompilerParams(vmem_limit_bytes=VMEM_LIMIT),
        cost_estimate=pl.CostEstimate(
            flops=18 * work, bytes_accessed=2 * bands * pixels * lanes, transcendentals=0
        ),
        name="kernel_grad",
    )(*features, *gradients.values(), *sums)


def partner(i, k, count):
    return i ^ k if count & (count - 1) == 0 else (i + k) % count


def split_kernel(parts, terms, *refs):
    ins, outs = refs[:terms], refs[terms:]
    count = len(outs)
    cover = outs[0].shape[0]
    me = lax.axis_index("dp") // parts
    for k, out in enumerate(outs):
        if count == 1:
            rows = pl.ds(0, cover)
        else:
            block = jnp.bitwise_xor(me, k) if count & (count - 1) == 0 else lax.rem(me + k, count)
            rows = pl.ds(pl.multiple_of(block * cover, cover), cover)
        total = ins[0][rows, :].astype(jnp.float32)
        for ref in ins[1:]:
            total += ref[rows, :].astype(jnp.float32)
        out[...] = total.astype(out.dtype)


def split_up(terms, parts, count):
    rows, lanes = terms[0].shape
    return pl.pallas_call(
        functools.partial(split_kernel, parts, len(terms)),
        out_shape=[jax.ShapeDtypeStruct((rows // count, lanes), jnp.bfloat16)] * count,
        compiler_params=pltpu.CompilerParams(vmem_limit_bytes=VMEM_LIMIT),
        name="split_up",
    )(*terms)


def final_kernel(replicas, *refs):
    *ins, out_ref = refs
    cover, lanes = ins[0].shape
    width = out_ref.shape[1]
    taps = lanes // width
    total = ins[0][...].astype(jnp.float32)
    for ref in ins[1:]:
        total += ref[...].astype(jnp.float32)
    total = total / replicas
    for t in range(taps):
        out_ref[pl.ds(t, cover, stride=taps), :] = total[:, t * width : (t + 1) * width]


def final(blocks, width, replicas):
    cover, lanes = blocks[0].shape
    return pl.pallas_call(
        functools.partial(final_kernel, replicas),
        out_shape=jax.ShapeDtypeStruct((cover * lanes // width, width), jnp.float32),
        compiler_params=pltpu.CompilerParams(vmem_limit_bytes=VMEM_LIMIT),
        name="final_sum",
    )(*blocks)


def feature_grad_kernel(columns, reach, bands, own_ref, above_ref, below_ref, w_ref, out, room, sems):
    band = lax.axis_index("space")
    pixels, width = own_ref.shape
    edge = reach * columns
    own = own_ref[...]
    above = above_ref[pixels - edge :]
    below = below_ref[:edge]
    above = jnp.where(band > 0, above, jnp.zeros_like(above))
    below = jnp.where(band + 1 < bands, below, jnp.zeros_like(below))
    stack = shifted_taps(jnp.concatenate([above, own, below], axis=0), columns, reach)
    taps = jnp.concatenate(
        [stack[(2 - a) * edge : (2 - a) * edge + pixels] for a in range(3)], axis=1
    )
    steps, _, step = room.shape
    copies = []
    for n in range(steps):
        here = pl.ds(n * step, step)
        weight = jnp.concatenate([w_ref[t, here, :] for t in range(w_ref.shape[0])], axis=1)
        room[n] = lax.dot_general(
            taps, weight, (((1,), (1,)), ((), ())), preferred_element_type=jnp.float32
        )
        copies.append(pltpu.make_async_copy(room.at[n], out.at[:, here], sems.at[n]))
        copies[-1].start()
    for copy in copies:
        copy.wait()


def feature_grad(own, above, below, weight, columns, reach, bands):
    pixels, _ = own.shape
    taps, channels, width = weight.shape
    step = 256 if channels % 256 == 0 else channels
    vmem = pl.BlockSpec(memory_space=pltpu.VMEM)
    return pl.pallas_call(
        functools.partial(feature_grad_kernel, columns, reach, bands),
        in_specs=[vmem] * 4,
        out_specs=pl.BlockSpec(memory_space=pltpu.HBM),
        out_shape=pltpu.HBM((pixels, channels), jnp.float32),
        scratch_shapes=[
            pltpu.VMEM((channels // step, pixels, step), jnp.float32),
            pltpu.SemaphoreType.DMA((channels // step,)),
        ],
        compiler_params=pltpu.CompilerParams(vmem_limit_bytes=VMEM_LIMIT),
        cost_estimate=pl.CostEstimate(
            flops=2 * pixels * taps * channels * width,
            bytes_accessed=2 * taps * channels * width + 4 * pixels * channels,
            transcendentals=0,
        ),
        name="feature_grad",
    )(own, above, below, weight)


def on_device(features, labels, pixel_weight, conv_weight, conv_bias, class_weight):
    image = features[0]
    band_rows, columns, channels = image.shape
    taps, width = conv_weight.shape[1:]
    pixels = band_rows * columns
    replicas = lax.axis_size("dp")
    bands = lax.axis_size("space")
    reach = DILATION_SIZE

    flat = image.reshape(pixels, channels)
    weight = conv_weight.transpose(1, 0, 2)
    block_rows, cover, picks, offsets = channel_plan(channels, taps, replicas, bands)
    even = block_rows % taps == 0
    parts = 2 if replicas % 2 == 0 else 1
    count = replicas // parts
    paired = bands == 4 and band_rows == reach and even
    if paired:
        flat, weight, own, *blocks = lay_out(flat, weight, columns, reach, bands, replicas, cover)
        whole = [own] + [
            lax.ppermute(block, "space", [(i, i ^ k) for i in range(bands)])
            for k, block in enumerate(blocks, 1)
        ]
        above, below, after = whole[1], whole[3], blocks[0]
    else:
        flat, weight, *split = load(flat, weight, bands, replicas, cover, even)
        if not even:
            order = jnp.array([c for line in picks for c in line], jnp.int32)
            split = jnp.take(flat, order, axis=1).reshape(pixels, bands, replicas * cover)
            split = [split.transpose(1, 0, 2)]
        whole = [lax.all_to_all(split[0], "space", 0, 0)]
        down, up = halo(flat, weight, columns, reach)
        above = lax.ppermute(down, "space", [(i, i + 1) for i in range(bands - 1)])
        below = lax.ppermute(up, "space", [(i + 1, i) for i in range(bands - 1)])
        after = up
    middle = middle_taps(flat, weight, after, columns, reach)

    gradient = pointwise(
        middle,
        above,
        below,
        conv_bias.reshape(1, width),
        class_weight.T,
        labels.reshape(band_rows, columns),
        pixel_weight.reshape(band_rows, columns),
        paired,
    )
    gradients = [gradient] + [
        lax.ppermute(gradient, "space", [(i, (i + k) % bands) for i in range(bands)])
        for k in range(1, bands)
    ]
    late = bands // 2
    early = {k: g for k, g in enumerate(gradients) if k != late or bands == 1}
    others = (0, 1)[:parts]
    size = (bands, replicas * cover)
    terms = kernel_grad(whole, early, [], columns, reach, parts, others, jnp.float32, *size)
    if bands > 1:
        last = {late: gradients[late]}
        own, *theirs = terms
        terms = kernel_grad(whole, last, [own], columns, reach, parts, (0,), jnp.float32, *size)
        if theirs:
            terms += kernel_grad(whole, last, theirs, columns, reach, parts, (1,), jnp.bfloat16, *size)
    if parts == 2:
        theirs = terms[1].astype(jnp.bfloat16)
        terms = [terms[0], lax.ppermute(theirs, "dp", [(i, i ^ 1) for i in range(replicas)])]
    if cover % 16 == 0 and count <= 8:
        blocks = split_up(terms, parts, count)
        came = [blocks[0]]
        for k in reversed(range(1, count)):
            pairs = [(i, parts * partner(i // parts, k, count) + i % parts) for i in range(replicas)]
            came.append(lax.ppermute(blocks[k], "dp", pairs))
    else:
        blocks = split_up(terms, parts, 1)[0].reshape(count, cover, taps * width)
        groups = [list(range(c, replicas, parts)) for c in range(parts)]
        came = list(lax.all_to_all(blocks, "dp", 0, 0, axis_index_groups=groups))
    weight_grad = final(came, width, replicas)
    if not even:
        start = jnp.array(offsets)[lax.axis_index("space"), lax.axis_index("dp")]
        weight_grad = lax.dynamic_slice_in_dim(weight_grad, start, block_rows)

    grad = feature_grad(gradient, gradients[1 % bands], gradients[-1], weight, columns, reach, bands)
    return grad.reshape(1, band_rows, columns, channels), weight_grad


def solution(mesh):
    placed = (
        P("dp", "space", None, None),
        P("dp", "space", None),
        P("dp", "space", None),
        P(),
        P(),
        P(),
    )
    return jax.shard_map(
        on_device,
        mesh=mesh,
        in_specs=placed,
        out_specs=(P("dp", "space", None, None), P(("dp", "space"), None)),
        check_vma=False,
    )
```

```python
import functools

import jax
import jax.numpy as jnp
from jax import lax
from jax.experimental import pallas as pl
from jax.experimental.pallas import tpu as pltpu
from jax.sharding import PartitionSpec as P

DILATION_SIZE = 6
VMEM_LIMIT = 16 * 1024 * 1024
VMEM_WHOLE = 62 * 1024 * 1024


def channel_plan(channels, taps, replicas, bands):
    rows = channels * taps // (replicas * bands)
    starts = [[(d * bands + s) * rows // taps for d in range(replicas)] for s in range(bands)]
    offsets = [[(d * bands + s) * rows % taps for d in range(replicas)] for s in range(bands)]
    cover = max(-(-(off + rows) // taps) for line in offsets for off in line)
    picks = [
        [min(line[d] + k, channels - 1) for d in replica_order(replicas) for k in range(cover)]
        for line in starts
    ]
    return rows, cover, picks, offsets


def replica_order(replicas):
    if replicas % 2:
        return list(range(replicas))
    return list(range(0, replicas, 2)) + list(range(1, replicas, 2))


def shift_columns(array, by, columns):
    if by == 0:
        return array
    size = array.shape[0]
    column = lax.broadcasted_iota(jnp.int32, array.shape, 0) % columns + by
    moved = pltpu.roll(array, (-by) % size, 0)
    return jnp.where((column >= 0) & (column < columns), moved, 0.0)


def tap_row(x, w_ref, a, columns, reach):
    width = w_ref.shape[2]
    weight = jnp.concatenate([w_ref[3 * a + b] for b in range(3)], axis=1)
    product = jnp.dot(x, weight, preferred_element_type=jnp.float32)
    return sum(
        shift_columns(product[:, b * width : (b + 1) * width], (b - 1) * reach, columns)
        for b in range(3)
    )


def load_kernel(replicas, cover, x_hbm, w_hbm, x_ref, w_ref, *refs):
    *outs, room, x_sem, w_sem, out_sems = refs
    x_load = pltpu.make_async_copy(x_hbm, x_ref, x_sem)
    w_load = pltpu.make_async_copy(w_hbm, w_ref, w_sem)
    x_load.start()
    w_load.start()
    x_load.wait()
    copies = []
    for out in outs:
        bands = room.shape[0]
        x = x_ref[...]
        for s in range(bands):
            room[s] = jnp.concatenate(
                [
                    x[:, (d * bands + s) * cover : (d * bands + s + 1) * cover]
                    for d in replica_order(replicas)
                ],
                axis=1,
            )
            copies.append(pltpu.make_async_copy(room.at[s], out.at[s], out_sems.at[s]))
            copies[-1].start()
    w_load.wait()
    for copy in copies:
        copy.wait()


def load(flat, weight, bands, replicas, cover, blocks):
    pixels, channels = flat.shape
    hbm = pl.BlockSpec(memory_space=pltpu.HBM)
    vmem = pl.BlockSpec(memory_space=pltpu.VMEM)
    shape = (bands, pixels, replicas * cover)
    count = 1 if blocks else 0
    return pl.pallas_call(
        functools.partial(load_kernel, replicas, cover),
        in_specs=[hbm, hbm],
        out_specs=[vmem, vmem] + [hbm] * count,
        out_shape=[
            pltpu.VMEM(flat.shape, flat.dtype),
            pltpu.VMEM(weight.shape, weight.dtype),
        ]
        + [pltpu.HBM(shape, flat.dtype)] * count,
        scratch_shapes=[
            pltpu.VMEM(shape, flat.dtype),
            pltpu.SemaphoreType.DMA,
            pltpu.SemaphoreType.DMA,
            pltpu.SemaphoreType.DMA((bands,)),
        ],
        compiler_params=pltpu.CompilerParams(vmem_limit_bytes=VMEM_LIMIT),
        cost_estimate=pl.CostEstimate(
            flops=0,
            bytes_accessed=2 * weight.size + 4 * pixels * channels,
            transcendentals=0,
        ),
        name="load",
    )(
        pltpu.with_memory_space_constraint(flat, pltpu.HBM),
        pltpu.with_memory_space_constraint(weight, pltpu.HBM),
    )


def halo_sums(x_ref, w_ref, columns, reach):
    pixels, edge = x_ref.shape[0], reach * columns
    width = w_ref.shape[2]
    if pixels > edge:
        down = tap_row(x_ref[pixels - edge :], w_ref, 0, columns, reach)
        up = tap_row(x_ref[:edge], w_ref, 2, columns, reach)
        return down, up
    weight = jnp.concatenate([w_ref[t] for t in (0, 1, 2, 6, 7, 8)], axis=1)
    product = jnp.dot(x_ref[...], weight, preferred_element_type=jnp.float32)
    return [
        sum(
            shift_columns(
                product[:, (3 * k + b) * width : (3 * k + b + 1) * width], (b - 1) * reach, columns
            )
            for b in range(3)
        )
        for k in range(2)
    ]


def lay_out_kernel(columns, reach, replicas, cover, x_hbm, w_hbm, x_ref, w_ref, *refs):
    *blocks, sums_ref, room, x_sem, w_sems = refs
    bands = len(blocks)
    band = lax.axis_index("space")
    lanes = room.shape[2]
    x_load = pltpu.make_async_copy(x_hbm, x_ref, x_sem)
    x_load.start()
    w_loads = []
    for n, (t, size) in enumerate(((0, 3), (6, 3), (3, 3))):
        here = pl.ds(t, size)
        w_loads.append(pltpu.make_async_copy(w_hbm.at[here], w_ref.at[here], w_sems.at[n]))
        w_loads[-1].start()
    x_load.wait()
    x = x_ref[...]
    for s in range(bands):
        room[s] = jnp.concatenate(
            [
                x[:, (d * bands + s) * cover : (d * bands + s + 1) * cover]
                for d in replica_order(replicas)
            ],
            axis=1,
        )
    for k, block in enumerate(blocks):
        block[:, :lanes] = room[jnp.bitwise_xor(band, k)]
    w_loads[0].wait()
    w_loads[1].wait()
    down, up = halo_sums(x_ref, w_ref, columns, reach)
    sums_ref[...] = jnp.where(band < 2, down, up).astype(x.dtype)
    blocks[1][:, lanes:] = jnp.where(lax.rem(band, 2) == 0, down, up).astype(x.dtype)
    w_loads[2].wait()


def lay_out(flat, weight, columns, reach, bands, replicas, cover):
    pixels, channels = flat.shape
    width = weight.shape[2]
    hbm = pl.BlockSpec(memory_space=pltpu.HBM)
    vmem = pl.BlockSpec(memory_space=pltpu.VMEM)
    lanes = replicas * cover
    shapes = [(pixels, lanes + (width if k == 1 else 0)) for k in range(bands)] + [(pixels, width)]
    return pl.pallas_call(
        functools.partial(lay_out_kernel, columns, reach, replicas, cover),
        in_specs=[hbm, hbm],
        out_specs=[vmem] * (3 + bands),
        out_shape=[
            pltpu.VMEM(flat.shape, flat.dtype),
            pltpu.VMEM(weight.shape, weight.dtype),
        ]
        + [pltpu.VMEM(shape, flat.dtype) for shape in shapes],
        scratch_shapes=[
            pltpu.VMEM((bands, pixels, lanes), flat.dtype),
            pltpu.SemaphoreType.DMA,
            pltpu.SemaphoreType.DMA((3,)),
        ],
        compiler_params=pltpu.CompilerParams(vmem_limit_bytes=VMEM_LIMIT),
        cost_estimate=pl.CostEstimate(
            flops=12 * pixels * channels * width,
            bytes_accessed=2 * weight.size + 4 * pixels * channels,
            transcendentals=0,
        ),
        name="lay_out",
    )(
        pltpu.with_memory_space_constraint(flat, pltpu.HBM),
        pltpu.with_memory_space_constraint(weight, pltpu.HBM),
    )


def halo_kernel(columns, reach, x_ref, w_ref, down_ref, up_ref):
    down, up = halo_sums(x_ref, w_ref, columns, reach)
    down_ref[...] = down.astype(down_ref.dtype)
    up_ref[...] = up.astype(up_ref.dtype)


def halo(flat, weight, columns, reach):
    _, channels = flat.shape
    width = weight.shape[2]
    edge = reach * columns
    return pl.pallas_call(
        functools.partial(halo_kernel, columns, reach),
        out_shape=[pltpu.VMEM((edge, width), jnp.bfloat16)] * 2,
        compiler_params=pltpu.CompilerParams(vmem_limit_bytes=VMEM_LIMIT),
        cost_estimate=pl.CostEstimate(
            flops=12 * edge * channels * width,
            bytes_accessed=12 * channels * width + 2 * edge * channels,
            transcendentals=0,
        ),
        name="halo",
    )(flat, weight)


def middle_kernel(columns, reach, x_ref, w_ref, after_ref, out_ref):
    del after_ref
    pixels, edge = x_ref.shape[0], reach * columns
    out_ref[...] = tap_row(x_ref[...], w_ref, 1, columns, reach)
    if pixels > edge:
        out_ref[edge:] += tap_row(x_ref[: pixels - edge], w_ref, 0, columns, reach)
        out_ref[: pixels - edge] += tap_row(x_ref[edge:], w_ref, 2, columns, reach)


def middle_taps(flat, weight, after, columns, reach):
    pixels, channels = flat.shape
    width = weight.shape[2]
    vmem = pl.BlockSpec(memory_space=pltpu.VMEM)
    return pl.pallas_call(
        functools.partial(middle_kernel, columns, reach),
        in_specs=[vmem, vmem, vmem],
        out_shape=pltpu.VMEM((pixels, width), jnp.float32),
        compiler_params=pltpu.CompilerParams(vmem_limit_bytes=VMEM_LIMIT),
        cost_estimate=pl.CostEstimate(
            flops=6 * pixels * channels * width,
            bytes_accessed=6 * channels * width + 2 * pixels * channels,
            transcendentals=0,
        ),
        name="middle_taps",
    )(flat, weight, after)


def as_column(rows_ref):
    values = rows_ref[...].astype(jnp.float32)
    rows, columns = values.shape
    shape = (columns, columns)
    same = lax.broadcasted_iota(jnp.int32, shape, 0) == lax.broadcasted_iota(jnp.int32, shape, 1)
    return jnp.concatenate(
        [
            jnp.sum(jnp.where(same, values[r : r + 1], 0.0), axis=1, keepdims=True)
            for r in range(rows)
        ],
        axis=0,
    )


def pointwise_kernel(
    middle_ref, above_ref, below_ref, bias_ref, class_ref, label_ref, scale_ref, out_ref
):
    pixels, width = middle_ref.shape
    edge = above_ref.shape[0]
    above = above_ref[:, above_ref.shape[1] - width :].astype(jnp.float32)
    below = below_ref[:, below_ref.shape[1] - width :].astype(jnp.float32)
    if pixels > edge:
        none = jnp.zeros((pixels - edge, width), jnp.float32)
        above = jnp.concatenate([above, none], axis=0)
        below = jnp.concatenate([none, below], axis=0)
    preact = middle_ref[...] + above + below + bias_ref[...]
    sigmoid_z = jax.nn.sigmoid(preact)
    hidden = (preact * sigmoid_z).astype(jnp.bfloat16)
    classes = class_ref[...]
    logits = lax.dot_general(
        hidden, classes, (((1,), (1,)), ((), ())), preferred_element_type=jnp.float32
    )
    exponent = jnp.exp(logits)
    chances = exponent / jnp.sum(exponent, axis=1, keepdims=True)
    index = lax.broadcasted_iota(jnp.int32, chances.shape, 1).astype(jnp.float32)
    onehot = jnp.where(as_column(label_ref) == index, 1.0, 0.0)
    grad_logits = as_column(scale_ref) * (chances - onehot)
    wide = classes.astype(jnp.float32)
    hidden_grad = sum(
        grad_logits[:, k : k + 1] * wide[k : k + 1] for k in range(classes.shape[0])
    )
    gradient = hidden_grad * sigmoid_z * (1.0 + preact * (1.0 - sigmoid_z))
    out_ref[...] = gradient.astype(out_ref.dtype)


def pointwise(middle, above, below, bias, classes, labels, scale):
    pixels, width = middle.shape
    return pl.pallas_call(
        pointwise_kernel,
        out_shape=jax.ShapeDtypeStruct((pixels, width), jnp.bfloat16),
        compiler_params=pltpu.CompilerParams(vmem_limit_bytes=VMEM_LIMIT),
        cost_estimate=pl.CostEstimate(
            flops=30 * pixels * width,
            bytes_accessed=10 * pixels * width,
            transcendentals=pixels * width,
        ),
        name="pointwise",
    )(middle, above, below, bias, classes, labels, scale)


def shifted_taps(gradient, columns, reach):
    wide = gradient.astype(jnp.float32)
    return jnp.concatenate(
        [shift_columns(wide, (1 - b) * reach, columns).astype(jnp.bfloat16) for b in range(3)],
        axis=1,
    )


def kernel_grad_kernel(columns, reach, parts, others, distances, before, given, lanes, *refs):
    x_refs, refs = refs[:given], refs[given:]
    count = len(distances)
    g_refs, sums, outs = refs[:count], refs[count : count + before], refs[count + before : -1]
    padded = refs[-1]
    pixels, width = g_refs[0].shape
    total = padded.shape[1] - 2 * reach * columns
    bands = total // pixels
    edge = reach * columns
    extra = lanes // parts
    band = lax.axis_index("space")
    slots = given > 1
    shifted = [shifted_taps(g_ref[...], columns, reach) for g_ref in g_refs]
    for n, (other, out_ref) in enumerate(zip(others, outs)):
        part = lax.rem(lax.axis_index("dp") + other, parts)
        for k, x_ref in enumerate(x_refs):
            if extra % 128 == 0:
                features = x_ref[..., pl.ds(pl.multiple_of(part * extra, 128), extra)]
            else:
                features = x_ref[..., :extra]
                for j in range(1, parts):
                    other_part = x_ref[..., j * extra : (j + 1) * extra]
                    features = jnp.where(part == j, other_part, features)
            if slots:
                padded[n, k * pixels : (k + 1) * pixels] = features
            else:
                padded[n, edge : edge + total] = features.reshape(total, extra)
        if slots:
            padded[n, total : total + pixels] = jnp.zeros((pixels, extra), padded.dtype)
        else:
            padded[n, :edge] = jnp.zeros((edge, extra), padded.dtype)
            padded[n, edge + total :] = jnp.zeros((edge, extra), padded.dtype)
        for a in range(3):
            here = pl.ds(3 * a * width, 3 * width)
            grad = sums[n][:, here] if before else None
            for k, right in zip(distances, shifted):
                from_band = lax.rem(band + bands - k, bands)
                if slots:
                    row = from_band + (a - 1)
                    inside = (row >= 0) & (row < bands)
                    slot = jnp.bitwise_xor(band, jnp.clip(row, 0, bands - 1))
                    first = jnp.where(inside, slot, bands) * pixels
                else:
                    first = from_band * pixels + a * edge
                left = padded[n, pl.ds(pl.multiple_of(first, 16), pixels)]
                term = lax.dot_general(
                    left, right, (((0,), (0,)), ((), ())), preferred_element_type=jnp.float32
                )
                grad = term if grad is None else grad + term
            out_ref[:, here] = grad.astype(out_ref.dtype)


def kernel_grad(features, gradients, sums, columns, reach, parts, others, dtype, bands, lanes):
    distances = tuple(gradients)
    pixels, width = gradients[distances[0]].shape
    extra = lanes // parts
    work = len(others) * len(distances) * pixels * extra * width
    return pl.pallas_call(
        functools.partial(
            kernel_grad_kernel,
            columns,
            reach,
            parts,
            others,
            distances,
            len(sums),
            len(features),
            lanes,
        ),
        out_shape=[pltpu.VMEM((extra, 9 * width), dtype)] * len(others),
        scratch_shapes=[pltpu.VMEM((len(others), bands * pixels + 2 * reach * columns, extra), jnp.bfloat16)],
        compiler_params=pltpu.CompilerParams(vmem_limit_bytes=VMEM_LIMIT),
        cost_estimate=pl.CostEstimate(
            flops=18 * work, bytes_accessed=2 * bands * pixels * lanes, transcendentals=0
        ),
        name="kernel_grad",
    )(*features, *gradients.values(), *sums)


def partner(i, k, count):
    return i ^ k if count & (count - 1) == 0 else (i + k) % count


def split_kernel(parts, terms, *refs):
    ins, outs = refs[:terms], refs[terms:]
    count = len(outs)
    cover = outs[0].shape[0]
    me = lax.axis_index("dp") // parts
    for k, out in enumerate(outs):
        if count == 1:
            rows = pl.ds(0, cover)
        else:
            block = jnp.bitwise_xor(me, k) if count & (count - 1) == 0 else lax.rem(me + k, count)
            rows = pl.ds(pl.multiple_of(block * cover, cover), cover)
        total = ins[0][rows, :].astype(jnp.float32)
        for ref in ins[1:]:
            total += ref[rows, :].astype(jnp.float32)
        out[...] = total.astype(out.dtype)


def split_up(terms, parts, count):
    rows, lanes = terms[0].shape
    return pl.pallas_call(
        functools.partial(split_kernel, parts, len(terms)),
        out_shape=[jax.ShapeDtypeStruct((rows // count, lanes), jnp.bfloat16)] * count,
        compiler_params=pltpu.CompilerParams(vmem_limit_bytes=VMEM_LIMIT),
        name="split_up",
    )(*terms)


def final_kernel(replicas, *refs):
    *ins, out_ref = refs
    cover, lanes = ins[0].shape
    width = out_ref.shape[1]
    taps = lanes // width
    total = ins[0][...].astype(jnp.float32)
    for ref in ins[1:]:
        total += ref[...].astype(jnp.float32)
    total = total / replicas
    for t in range(taps):
        out_ref[pl.ds(t, cover, stride=taps), :] = total[:, t * width : (t + 1) * width]


def final(blocks, width, replicas):
    cover, lanes = blocks[0].shape
    return pl.pallas_call(
        functools.partial(final_kernel, replicas),
        out_shape=jax.ShapeDtypeStruct((cover * lanes // width, width), jnp.float32),
        compiler_params=pltpu.CompilerParams(vmem_limit_bytes=VMEM_LIMIT),
        name="final_sum",
    )(*blocks)


def feature_grad_kernel(columns, reach, bands, own_ref, above_ref, below_ref, w_ref, out, room, sems):
    band = lax.axis_index("space")
    pixels, width = own_ref.shape
    edge = reach * columns
    own = own_ref[...]
    above = above_ref[pixels - edge :]
    below = below_ref[:edge]
    above = jnp.where(band > 0, above, jnp.zeros_like(above))
    below = jnp.where(band + 1 < bands, below, jnp.zeros_like(below))
    stack = shifted_taps(jnp.concatenate([above, own, below], axis=0), columns, reach)
    taps = jnp.concatenate(
        [stack[(2 - a) * edge : (2 - a) * edge + pixels] for a in range(3)], axis=1
    )
    steps, _, step = room.shape
    copies = []
    for n in range(steps):
        here = pl.ds(n * step, step)
        weight = jnp.concatenate([w_ref[t, here, :] for t in range(w_ref.shape[0])], axis=1)
        room[n] = lax.dot_general(
            taps, weight, (((1,), (1,)), ((), ())), preferred_element_type=jnp.float32
        )
        copies.append(pltpu.make_async_copy(room.at[n], out.at[:, here], sems.at[n]))
        copies[-1].start()
    for copy in copies:
        copy.wait()


def feature_grad(own, above, below, weight, columns, reach, bands):
    pixels, _ = own.shape
    taps, channels, width = weight.shape
    step = 256 if channels % 256 == 0 else channels
    vmem = pl.BlockSpec(memory_space=pltpu.VMEM)
    return pl.pallas_call(
        functools.partial(feature_grad_kernel, columns, reach, bands),
        in_specs=[vmem] * 4,
        out_specs=pl.BlockSpec(memory_space=pltpu.HBM),
        out_shape=pltpu.HBM((pixels, channels), jnp.float32),
        scratch_shapes=[
            pltpu.VMEM((channels // step, pixels, step), jnp.float32),
            pltpu.SemaphoreType.DMA((channels // step,)),
        ],
        compiler_params=pltpu.CompilerParams(vmem_limit_bytes=VMEM_LIMIT),
        cost_estimate=pl.CostEstimate(
            flops=2 * pixels * taps * channels * width,
            bytes_accessed=2 * taps * channels * width + 4 * pixels * channels,
            transcendentals=0,
        ),
        name="feature_grad",
    )(own, above, below, weight)


def on_device(features, labels, pixel_weight, conv_weight, conv_bias, class_weight):
    image = features[0]
    band_rows, columns, channels = image.shape
    taps, width = conv_weight.shape[1:]
    pixels = band_rows * columns
    replicas = lax.axis_size("dp")
    bands = lax.axis_size("space")
    reach = DILATION_SIZE

    flat = image.reshape(pixels, channels)
    weight = conv_weight.transpose(1, 0, 2)
    block_rows, cover, picks, offsets = channel_plan(channels, taps, replicas, bands)
    even = block_rows % taps == 0
    parts = 2 if replicas % 2 == 0 else 1
    count = replicas // parts
    paired = bands == 4 and band_rows == reach and even
    if paired:
        flat, weight, own, *blocks, sums = lay_out(
            flat, weight, columns, reach, bands, replicas, cover
        )
        below = lax.ppermute(sums, "space", [(1, 2), (2, 1)])
        whole = [own] + [
            lax.ppermute(block, "space", [(i, i ^ k) for i in range(bands)])
            for k, block in enumerate(blocks, 1)
        ]
        above, after = whole[1], sums
    else:
        flat, weight, *split = load(flat, weight, bands, replicas, cover, even)
        if not even:
            order = jnp.array([c for line in picks for c in line], jnp.int32)
            split = jnp.take(flat, order, axis=1).reshape(pixels, bands, replicas * cover)
            split = [split.transpose(1, 0, 2)]
        whole = [lax.all_to_all(split[0], "space", 0, 0)]
        down, up = halo(flat, weight, columns, reach)
        above = lax.ppermute(down, "space", [(i, i + 1) for i in range(bands - 1)])
        below = lax.ppermute(up, "space", [(i + 1, i) for i in range(bands - 1)])
        after = up
    middle = middle_taps(flat, weight, after, columns, reach)

    gradient = pointwise(
        middle,
        above,
        below,
        conv_bias.reshape(1, width),
        class_weight.T,
        labels.reshape(band_rows, columns),
        pixel_weight.reshape(band_rows, columns),
    )
    gradients = [gradient] + [
        lax.ppermute(gradient, "space", [(i, (i + k) % bands) for i in range(bands)])
        for k in range(1, bands)
    ]
    late = bands // 2
    early = {k: g for k, g in enumerate(gradients) if k != late or bands == 1}
    others = (0, 1)[:parts]
    size = (bands, replicas * cover)
    terms = kernel_grad(whole, early, [], columns, reach, parts, others, jnp.float32, *size)
    if bands > 1:
        last = {late: gradients[late]}
        own, *theirs = terms
        terms = kernel_grad(whole, last, [own], columns, reach, parts, (0,), jnp.float32, *size)
        if theirs:
            terms += kernel_grad(whole, last, theirs, columns, reach, parts, (1,), jnp.bfloat16, *size)
    if parts == 2:
        theirs = terms[1].astype(jnp.bfloat16)
        terms = [terms[0], lax.ppermute(theirs, "dp", [(i, i ^ 1) for i in range(replicas)])]
    if cover % 16 == 0 and count <= 8:
        blocks = split_up(terms, parts, count)
        came = [blocks[0]]
        for k in reversed(range(1, count)):
            pairs = [(i, parts * partner(i // parts, k, count) + i % parts) for i in range(replicas)]
            came.append(lax.ppermute(blocks[k], "dp", pairs))
    else:
        blocks = split_up(terms, parts, 1)[0].reshape(count, cover, taps * width)
        groups = [list(range(c, replicas, parts)) for c in range(parts)]
        came = list(lax.all_to_all(blocks, "dp", 0, 0, axis_index_groups=groups))
    weight_grad = final(came, width, replicas)
    if not even:
        start = jnp.array(offsets)[lax.axis_index("space"), lax.axis_index("dp")]
        weight_grad = lax.dynamic_slice_in_dim(weight_grad, start, block_rows)

    grad = feature_grad(gradient, gradients[1 % bands], gradients[-1], weight, columns, reach, bands)
    return grad.reshape(1, band_rows, columns, channels), weight_grad


def solution(mesh):
    placed = (
        P("dp", "space", None, None),
        P("dp", "space", None),
        P("dp", "space", None),
        P(),
        P(),
        P(),
    )
    return jax.shard_map(
        on_device,
        mesh=mesh,
        in_specs=placed,
        out_specs=(P("dp", "space", None, None), P(("dp", "space"), None)),
        check_vma=False,
    )
```

```python
import functools

import jax
import jax.numpy as jnp
from jax import lax
from jax.experimental import pallas as pl
from jax.experimental.pallas import tpu as pltpu
from jax.sharding import PartitionSpec as P

DILATION_SIZE = 6
VMEM_LIMIT = 16 * 1024 * 1024
VMEM_WHOLE = 62 * 1024 * 1024


def channel_plan(channels, taps, replicas, bands):
    rows = channels * taps // (replicas * bands)
    starts = [[(d * bands + s) * rows // taps for d in range(replicas)] for s in range(bands)]
    offsets = [[(d * bands + s) * rows % taps for d in range(replicas)] for s in range(bands)]
    cover = max(-(-(off + rows) // taps) for line in offsets for off in line)
    picks = [
        [min(line[d] + k, channels - 1) for d in replica_order(replicas) for k in range(cover)]
        for line in starts
    ]
    return rows, cover, picks, offsets


def replica_order(replicas):
    if replicas % 2:
        return list(range(replicas))
    return list(range(0, replicas, 2)) + list(range(1, replicas, 2))


def shift_columns(array, by, columns):
    if by == 0:
        return array
    size = array.shape[0]
    column = lax.broadcasted_iota(jnp.int32, array.shape, 0) % columns + by
    moved = pltpu.roll(array, (-by) % size, 0)
    return jnp.where((column >= 0) & (column < columns), moved, 0.0)


def tap_row(x, w_ref, a, columns, reach):
    width = w_ref.shape[2]
    weight = jnp.concatenate([w_ref[3 * a + b] for b in range(3)], axis=1)
    product = jnp.dot(x, weight, preferred_element_type=jnp.float32)
    return sum(
        shift_columns(product[:, b * width : (b + 1) * width], (b - 1) * reach, columns)
        for b in range(3)
    )


def load_kernel(replicas, cover, x_hbm, w_hbm, x_ref, w_ref, *refs):
    *outs, room, x_sem, w_sem, out_sems = refs
    x_load = pltpu.make_async_copy(x_hbm, x_ref, x_sem)
    w_load = pltpu.make_async_copy(w_hbm, w_ref, w_sem)
    x_load.start()
    w_load.start()
    x_load.wait()
    copies = []
    for out in outs:
        bands = room.shape[0]
        x = x_ref[...]
        for s in range(bands):
            room[s] = jnp.concatenate(
                [
                    x[:, (d * bands + s) * cover : (d * bands + s + 1) * cover]
                    for d in replica_order(replicas)
                ],
                axis=1,
            )
            copies.append(pltpu.make_async_copy(room.at[s], out.at[s], out_sems.at[s]))
            copies[-1].start()
    w_load.wait()
    for copy in copies:
        copy.wait()


def load(flat, weight, bands, replicas, cover, blocks):
    pixels, channels = flat.shape
    hbm = pl.BlockSpec(memory_space=pltpu.HBM)
    vmem = pl.BlockSpec(memory_space=pltpu.VMEM)
    shape = (bands, pixels, replicas * cover)
    count = 1 if blocks else 0
    return pl.pallas_call(
        functools.partial(load_kernel, replicas, cover),
        in_specs=[hbm, hbm],
        out_specs=[vmem, vmem] + [hbm] * count,
        out_shape=[
            pltpu.VMEM(flat.shape, flat.dtype),
            pltpu.VMEM(weight.shape, weight.dtype),
        ]
        + [pltpu.HBM(shape, flat.dtype)] * count,
        scratch_shapes=[
            pltpu.VMEM(shape, flat.dtype),
            pltpu.SemaphoreType.DMA,
            pltpu.SemaphoreType.DMA,
            pltpu.SemaphoreType.DMA((bands,)),
        ],
        compiler_params=pltpu.CompilerParams(vmem_limit_bytes=VMEM_LIMIT),
        cost_estimate=pl.CostEstimate(
            flops=0,
            bytes_accessed=2 * weight.size + 4 * pixels * channels,
            transcendentals=0,
        ),
        name="load",
    )(
        pltpu.with_memory_space_constraint(flat, pltpu.HBM),
        pltpu.with_memory_space_constraint(weight, pltpu.HBM),
    )


def halo_sums(x_ref, w_ref, columns, reach):
    pixels, edge = x_ref.shape[0], reach * columns
    width = w_ref.shape[2]
    if pixels > edge:
        down = tap_row(x_ref[pixels - edge :], w_ref, 0, columns, reach)
        up = tap_row(x_ref[:edge], w_ref, 2, columns, reach)
        return down, up
    weight = jnp.concatenate([w_ref[t] for t in (0, 1, 2, 6, 7, 8)], axis=1)
    product = jnp.dot(x_ref[...], weight, preferred_element_type=jnp.float32)
    return [
        sum(
            shift_columns(
                product[:, (3 * k + b) * width : (3 * k + b + 1) * width], (b - 1) * reach, columns
            )
            for b in range(3)
        )
        for k in range(2)
    ]


def lay_out_kernel(columns, reach, replicas, cover, x_hbm, w_hbm, x_ref, w_ref, *refs):
    *blocks, sums_ref, room, x_sem, w_sems = refs
    bands = len(blocks)
    band = lax.axis_index("space")
    lanes = room.shape[2]
    x_load = pltpu.make_async_copy(x_hbm, x_ref, x_sem)
    x_load.start()
    w_loads = []
    for n, (t, size) in enumerate(((0, 3), (6, 3), (3, 3))):
        here = pl.ds(t, size)
        w_loads.append(pltpu.make_async_copy(w_hbm.at[here], w_ref.at[here], w_sems.at[n]))
        w_loads[-1].start()
    x_load.wait()
    x = x_ref[...]
    for s in range(bands):
        room[s] = jnp.concatenate(
            [
                x[:, (d * bands + s) * cover : (d * bands + s + 1) * cover]
                for d in replica_order(replicas)
            ],
            axis=1,
        )
    for k, block in enumerate(blocks):
        block[:, :lanes] = room[jnp.bitwise_xor(band, k)]
    w_loads[0].wait()
    w_loads[1].wait()
    down, up = halo_sums(x_ref, w_ref, columns, reach)
    sums_ref[...] = jnp.where(band < 2, down, up).astype(x.dtype)
    blocks[1][:, lanes:] = jnp.where(lax.rem(band, 2) == 0, down, up).astype(x.dtype)
    w_loads[2].wait()


def lay_out(flat, weight, columns, reach, bands, replicas, cover):
    pixels, channels = flat.shape
    width = weight.shape[2]
    hbm = pl.BlockSpec(memory_space=pltpu.HBM)
    vmem = pl.BlockSpec(memory_space=pltpu.VMEM)
    lanes = replicas * cover
    shapes = [(pixels, lanes + (width if k == 1 else 0)) for k in range(bands)] + [(pixels, width)]
    return pl.pallas_call(
        functools.partial(lay_out_kernel, columns, reach, replicas, cover),
        in_specs=[hbm, hbm],
        out_specs=[vmem] * (3 + bands),
        out_shape=[
            pltpu.VMEM(flat.shape, flat.dtype),
            pltpu.VMEM(weight.shape, weight.dtype),
        ]
        + [pltpu.VMEM(shape, flat.dtype) for shape in shapes],
        scratch_shapes=[
            pltpu.VMEM((bands, pixels, lanes), flat.dtype),
            pltpu.SemaphoreType.DMA,
            pltpu.SemaphoreType.DMA((3,)),
        ],
        compiler_params=pltpu.CompilerParams(vmem_limit_bytes=VMEM_LIMIT),
        cost_estimate=pl.CostEstimate(
            flops=12 * pixels * channels * width,
            bytes_accessed=2 * weight.size + 4 * pixels * channels,
            transcendentals=0,
        ),
        name="lay_out",
    )(
        pltpu.with_memory_space_constraint(flat, pltpu.HBM),
        pltpu.with_memory_space_constraint(weight, pltpu.HBM),
    )


def halo_kernel(columns, reach, x_ref, w_ref, down_ref, up_ref):
    down, up = halo_sums(x_ref, w_ref, columns, reach)
    down_ref[...] = down.astype(down_ref.dtype)
    up_ref[...] = up.astype(up_ref.dtype)


def halo(flat, weight, columns, reach):
    _, channels = flat.shape
    width = weight.shape[2]
    edge = reach * columns
    return pl.pallas_call(
        functools.partial(halo_kernel, columns, reach),
        out_shape=[pltpu.VMEM((edge, width), jnp.bfloat16)] * 2,
        compiler_params=pltpu.CompilerParams(vmem_limit_bytes=VMEM_LIMIT),
        cost_estimate=pl.CostEstimate(
            flops=12 * edge * channels * width,
            bytes_accessed=12 * channels * width + 2 * edge * channels,
            transcendentals=0,
        ),
        name="halo",
    )(flat, weight)


def middle_kernel(columns, reach, x_ref, w_ref, after_ref, out_ref):
    del after_ref
    pixels, edge = x_ref.shape[0], reach * columns
    out_ref[...] = tap_row(x_ref[...], w_ref, 1, columns, reach)
    if pixels > edge:
        out_ref[edge:] += tap_row(x_ref[: pixels - edge], w_ref, 0, columns, reach)
        out_ref[: pixels - edge] += tap_row(x_ref[edge:], w_ref, 2, columns, reach)


def middle_taps(flat, weight, after, columns, reach):
    pixels, channels = flat.shape
    width = weight.shape[2]
    vmem = pl.BlockSpec(memory_space=pltpu.VMEM)
    return pl.pallas_call(
        functools.partial(middle_kernel, columns, reach),
        in_specs=[vmem, vmem, vmem],
        out_shape=pltpu.VMEM((pixels, width), jnp.float32),
        compiler_params=pltpu.CompilerParams(vmem_limit_bytes=VMEM_LIMIT),
        cost_estimate=pl.CostEstimate(
            flops=6 * pixels * channels * width,
            bytes_accessed=6 * channels * width + 2 * pixels * channels,
            transcendentals=0,
        ),
        name="middle_taps",
    )(flat, weight, after)


def as_column(rows_ref):
    values = rows_ref[...].astype(jnp.float32)
    rows, columns = values.shape
    shape = (columns, columns)
    same = lax.broadcasted_iota(jnp.int32, shape, 0) == lax.broadcasted_iota(jnp.int32, shape, 1)
    return jnp.concatenate(
        [
            jnp.sum(jnp.where(same, values[r : r + 1], 0.0), axis=1, keepdims=True)
            for r in range(rows)
        ],
        axis=0,
    )


def pointwise_kernel(*refs):
    middle_ref, above_ref, below_ref, bias_ref, class_ref, label_ref, scale_ref, out_ref = refs[-8:]
    pixels, width = middle_ref.shape
    edge = above_ref.shape[0]
    above = above_ref[:, above_ref.shape[1] - width :].astype(jnp.float32)
    below = below_ref[:, below_ref.shape[1] - width :].astype(jnp.float32)
    if pixels > edge:
        none = jnp.zeros((pixels - edge, width), jnp.float32)
        above = jnp.concatenate([above, none], axis=0)
        below = jnp.concatenate([none, below], axis=0)
    preact = middle_ref[...] + above + below + bias_ref[...]
    sigmoid_z = jax.nn.sigmoid(preact)
    hidden = (preact * sigmoid_z).astype(jnp.bfloat16)
    classes = class_ref[...]
    logits = lax.dot_general(
        hidden, classes, (((1,), (1,)), ((), ())), preferred_element_type=jnp.float32
    )
    exponent = jnp.exp(logits)
    chances = exponent / jnp.sum(exponent, axis=1, keepdims=True)
    index = lax.broadcasted_iota(jnp.int32, chances.shape, 1).astype(jnp.float32)
    onehot = jnp.where(as_column(label_ref) == index, 1.0, 0.0)
    grad_logits = as_column(scale_ref) * (chances - onehot)
    wide = classes.astype(jnp.float32)
    hidden_grad = sum(
        grad_logits[:, k : k + 1] * wide[k : k + 1] for k in range(classes.shape[0])
    )
    gradient = hidden_grad * sigmoid_z * (1.0 + preact * (1.0 - sigmoid_z))
    out_ref[...] = gradient.astype(out_ref.dtype)


def pointwise(middle, above, below, bias, classes, labels, scale, after):
    pixels, width = middle.shape
    return pl.pallas_call(
        pointwise_kernel,
        out_shape=jax.ShapeDtypeStruct((pixels, width), jnp.bfloat16),
        compiler_params=pltpu.CompilerParams(vmem_limit_bytes=VMEM_LIMIT),
        cost_estimate=pl.CostEstimate(
            flops=30 * pixels * width,
            bytes_accessed=10 * pixels * width,
            transcendentals=pixels * width,
        ),
        name="pointwise",
    )(*after, middle, above, below, bias, classes, labels, scale)


def shifted_taps(gradient, columns, reach):
    wide = gradient.astype(jnp.float32)
    return jnp.concatenate(
        [shift_columns(wide, (1 - b) * reach, columns).astype(jnp.bfloat16) for b in range(3)],
        axis=1,
    )


def kernel_grad_kernel(columns, reach, parts, others, distances, before, given, lanes, *refs):
    x_refs, refs = refs[:given], refs[given:]
    count = len(distances)
    g_refs, sums, outs = refs[:count], refs[count : count + before], refs[count + before : -1]
    padded = refs[-1]
    pixels, width = g_refs[0].shape
    total = padded.shape[1] - 2 * reach * columns
    bands = total // pixels
    edge = reach * columns
    extra = lanes // parts
    band = lax.axis_index("space")
    slots = given > 1
    shifted = [shifted_taps(g_ref[...], columns, reach) for g_ref in g_refs]
    for n, (other, out_ref) in enumerate(zip(others, outs)):
        part = lax.rem(lax.axis_index("dp") + other, parts)
        for k, x_ref in enumerate(x_refs):
            if extra % 128 == 0:
                features = x_ref[..., pl.ds(pl.multiple_of(part * extra, 128), extra)]
            else:
                features = x_ref[..., :extra]
                for j in range(1, parts):
                    other_part = x_ref[..., j * extra : (j + 1) * extra]
                    features = jnp.where(part == j, other_part, features)
            if slots:
                padded[n, k * pixels : (k + 1) * pixels] = features
            else:
                padded[n, edge : edge + total] = features.reshape(total, extra)
        if slots:
            padded[n, total : total + pixels] = jnp.zeros((pixels, extra), padded.dtype)
        else:
            padded[n, :edge] = jnp.zeros((edge, extra), padded.dtype)
            padded[n, edge + total :] = jnp.zeros((edge, extra), padded.dtype)
        for a in range(3):
            here = pl.ds(3 * a * width, 3 * width)
            grad = sums[n][:, here] if before else None
            for k, right in zip(distances, shifted):
                from_band = lax.rem(band + bands - k, bands)
                if slots:
                    row = from_band + (a - 1)
                    inside = (row >= 0) & (row < bands)
                    slot = jnp.bitwise_xor(band, jnp.clip(row, 0, bands - 1))
                    first = jnp.where(inside, slot, bands) * pixels
                else:
                    first = from_band * pixels + a * edge
                left = padded[n, pl.ds(pl.multiple_of(first, 16), pixels)]
                term = lax.dot_general(
                    left, right, (((0,), (0,)), ((), ())), preferred_element_type=jnp.float32
                )
                grad = term if grad is None else grad + term
            out_ref[:, here] = grad.astype(out_ref.dtype)


def kernel_grad(features, gradients, sums, columns, reach, parts, others, dtype, bands, lanes):
    distances = tuple(gradients)
    pixels, width = gradients[distances[0]].shape
    extra = lanes // parts
    work = len(others) * len(distances) * pixels * extra * width
    return pl.pallas_call(
        functools.partial(
            kernel_grad_kernel,
            columns,
            reach,
            parts,
            others,
            distances,
            len(sums),
            len(features),
            lanes,
        ),
        out_shape=[pltpu.VMEM((extra, 9 * width), dtype)] * len(others),
        scratch_shapes=[pltpu.VMEM((len(others), bands * pixels + 2 * reach * columns, extra), jnp.bfloat16)],
        compiler_params=pltpu.CompilerParams(vmem_limit_bytes=VMEM_LIMIT),
        cost_estimate=pl.CostEstimate(
            flops=18 * work, bytes_accessed=2 * bands * pixels * lanes, transcendentals=0
        ),
        name="kernel_grad",
    )(*features, *gradients.values(), *sums)


def partner(i, k, count):
    return i ^ k if count & (count - 1) == 0 else (i + k) % count


def split_kernel(parts, terms, *refs):
    ins, outs = refs[:terms], refs[terms:]
    count = len(outs)
    cover = outs[0].shape[0]
    me = lax.axis_index("dp") // parts
    for k, out in enumerate(outs):
        if count == 1:
            rows = pl.ds(0, cover)
        else:
            block = jnp.bitwise_xor(me, k) if count & (count - 1) == 0 else lax.rem(me + k, count)
            rows = pl.ds(pl.multiple_of(block * cover, cover), cover)
        total = ins[0][rows, :].astype(jnp.float32)
        for ref in ins[1:]:
            total += ref[rows, :].astype(jnp.float32)
        out[...] = total.astype(out.dtype)


def split_up(terms, parts, count):
    rows, lanes = terms[0].shape
    return pl.pallas_call(
        functools.partial(split_kernel, parts, len(terms)),
        out_shape=[jax.ShapeDtypeStruct((rows // count, lanes), jnp.bfloat16)] * count,
        compiler_params=pltpu.CompilerParams(vmem_limit_bytes=VMEM_LIMIT),
        name="split_up",
    )(*terms)


def final_kernel(replicas, *refs):
    *ins, out_ref = refs
    cover, lanes = ins[0].shape
    width = out_ref.shape[1]
    taps = lanes // width
    total = ins[0][...].astype(jnp.float32)
    for ref in ins[1:]:
        total += ref[...].astype(jnp.float32)
    total = total / replicas
    for t in range(taps):
        out_ref[pl.ds(t, cover, stride=taps), :] = total[:, t * width : (t + 1) * width]


def final(blocks, width, replicas):
    cover, lanes = blocks[0].shape
    return pl.pallas_call(
        functools.partial(final_kernel, replicas),
        out_shape=jax.ShapeDtypeStruct((cover * lanes // width, width), jnp.float32),
        compiler_params=pltpu.CompilerParams(vmem_limit_bytes=VMEM_LIMIT),
        name="final_sum",
    )(*blocks)


def feature_grad_kernel(columns, reach, bands, own_ref, above_ref, below_ref, w_ref, out, room, sems):
    band = lax.axis_index("space")
    pixels, width = own_ref.shape
    edge = reach * columns
    own = own_ref[...]
    above = above_ref[pixels - edge :]
    below = below_ref[:edge]
    above = jnp.where(band > 0, above, jnp.zeros_like(above))
    below = jnp.where(band + 1 < bands, below, jnp.zeros_like(below))
    stack = shifted_taps(jnp.concatenate([above, own, below], axis=0), columns, reach)
    taps = jnp.concatenate(
        [stack[(2 - a) * edge : (2 - a) * edge + pixels] for a in range(3)], axis=1
    )
    steps, _, step = room.shape
    copies = []
    for n in range(steps):
        here = pl.ds(n * step, step)
        weight = jnp.concatenate([w_ref[t, here, :] for t in range(w_ref.shape[0])], axis=1)
        room[n] = lax.dot_general(
            taps, weight, (((1,), (1,)), ((), ())), preferred_element_type=jnp.float32
        )
        copies.append(pltpu.make_async_copy(room.at[n], out.at[:, here], sems.at[n]))
        copies[-1].start()
    for copy in copies:
        copy.wait()


def feature_grad(own, above, below, weight, columns, reach, bands):
    pixels, _ = own.shape
    taps, channels, width = weight.shape
    step = 256 if channels % 256 == 0 else channels
    vmem = pl.BlockSpec(memory_space=pltpu.VMEM)
    return pl.pallas_call(
        functools.partial(feature_grad_kernel, columns, reach, bands),
        in_specs=[vmem] * 4,
        out_specs=pl.BlockSpec(memory_space=pltpu.HBM),
        out_shape=pltpu.HBM((pixels, channels), jnp.float32),
        scratch_shapes=[
            pltpu.VMEM((channels // step, pixels, step), jnp.float32),
            pltpu.SemaphoreType.DMA((channels // step,)),
        ],
        compiler_params=pltpu.CompilerParams(vmem_limit_bytes=VMEM_LIMIT),
        cost_estimate=pl.CostEstimate(
            flops=2 * pixels * taps * channels * width,
            bytes_accessed=2 * taps * channels * width + 4 * pixels * channels,
            transcendentals=0,
        ),
        name="feature_grad",
    )(own, above, below, weight)


def on_device(features, labels, pixel_weight, conv_weight, conv_bias, class_weight):
    image = features[0]
    band_rows, columns, channels = image.shape
    taps, width = conv_weight.shape[1:]
    pixels = band_rows * columns
    replicas = lax.axis_size("dp")
    bands = lax.axis_size("space")
    reach = DILATION_SIZE

    flat = image.reshape(pixels, channels)
    weight = conv_weight.transpose(1, 0, 2)
    block_rows, cover, picks, offsets = channel_plan(channels, taps, replicas, bands)
    even = block_rows % taps == 0
    parts = 2 if replicas % 2 == 0 else 1
    count = replicas // parts
    paired = bands == 4 and band_rows == reach and even
    if paired:
        flat, weight, own, *blocks, sums = lay_out(
            flat, weight, columns, reach, bands, replicas, cover
        )
        below = lax.ppermute(sums, "space", [(1, 2), (2, 1)])
        whole = [own] + [
            lax.ppermute(block, "space", [(i, i ^ k) for i in range(bands)])
            for k, block in enumerate(blocks, 1)
        ]
        above, after = whole[1], sums
    else:
        flat, weight, *split = load(flat, weight, bands, replicas, cover, even)
        if not even:
            order = jnp.array([c for line in picks for c in line], jnp.int32)
            split = jnp.take(flat, order, axis=1).reshape(pixels, bands, replicas * cover)
            split = [split.transpose(1, 0, 2)]
        whole = [lax.all_to_all(split[0], "space", 0, 0)]
        down, up = halo(flat, weight, columns, reach)
        above = lax.ppermute(down, "space", [(i, i + 1) for i in range(bands - 1)])
        below = lax.ppermute(up, "space", [(i + 1, i) for i in range(bands - 1)])
        after = up
    middle = middle_taps(flat, weight, after, columns, reach)

    gradient = pointwise(
        middle,
        above,
        below,
        conv_bias.reshape(1, width),
        class_weight.T,
        labels.reshape(band_rows, columns),
        pixel_weight.reshape(band_rows, columns),
        whole[2:3],
    )
    gradients = [gradient] + [
        lax.ppermute(gradient, "space", [(i, (i + k) % bands) for i in range(bands)])
        for k in range(1, bands)
    ]
    late = bands // 2
    early = {k: g for k, g in enumerate(gradients) if k != late or bands == 1}
    others = (0, 1)[:parts]
    size = (bands, replicas * cover)
    terms = kernel_grad(whole, early, [], columns, reach, parts, others, jnp.float32, *size)
    if bands > 1:
        last = {late: gradients[late]}
        own, *theirs = terms
        terms = kernel_grad(whole, last, [own], columns, reach, parts, (0,), jnp.float32, *size)
        if theirs:
            terms += kernel_grad(whole, last, theirs, columns, reach, parts, (1,), jnp.bfloat16, *size)
    if parts == 2:
        theirs = terms[1].astype(jnp.bfloat16)
        terms = [terms[0], lax.ppermute(theirs, "dp", [(i, i ^ 1) for i in range(replicas)])]
    if cover % 16 == 0 and count <= 8:
        blocks = split_up(terms, parts, count)
        came = [blocks[0]]
        for k in reversed(range(1, count)):
            pairs = [(i, parts * partner(i // parts, k, count) + i % parts) for i in range(replicas)]
            came.append(lax.ppermute(blocks[k], "dp", pairs))
    else:
        blocks = split_up(terms, parts, 1)[0].reshape(count, cover, taps * width)
        groups = [list(range(c, replicas, parts)) for c in range(parts)]
        came = list(lax.all_to_all(blocks, "dp", 0, 0, axis_index_groups=groups))
    weight_grad = final(came, width, replicas)
    if not even:
        start = jnp.array(offsets)[lax.axis_index("space"), lax.axis_index("dp")]
        weight_grad = lax.dynamic_slice_in_dim(weight_grad, start, block_rows)

    grad = feature_grad(gradient, gradients[1 % bands], gradients[-1], weight, columns, reach, bands)
    return grad.reshape(1, band_rows, columns, channels), weight_grad


def solution(mesh):
    placed = (
        P("dp", "space", None, None),
        P("dp", "space", None),
        P("dp", "space", None),
        P(),
        P(),
        P(),
    )
    return jax.shard_map(
        on_device,
        mesh=mesh,
        in_specs=placed,
        out_specs=(P("dp", "space", None, None), P(("dp", "space"), None)),
        check_vma=False,
    )
```

```python
import functools

import jax
import jax.numpy as jnp
from jax import lax
from jax.experimental import pallas as pl
from jax.experimental.pallas import tpu as pltpu
from jax.sharding import PartitionSpec as P

DILATION_SIZE = 6
VMEM_LIMIT = 16 * 1024 * 1024
VMEM_WHOLE = 62 * 1024 * 1024


def channel_plan(channels, taps, replicas, bands):
    rows = channels * taps // (replicas * bands)
    starts = [[(d * bands + s) * rows // taps for d in range(replicas)] for s in range(bands)]
    offsets = [[(d * bands + s) * rows % taps for d in range(replicas)] for s in range(bands)]
    cover = max(-(-(off + rows) // taps) for line in offsets for off in line)
    picks = [
        [min(line[d] + k, channels - 1) for d in replica_order(replicas) for k in range(cover)]
        for line in starts
    ]
    return rows, cover, picks, offsets


def replica_order(replicas):
    if replicas % 2:
        return list(range(replicas))
    return list(range(0, replicas, 2)) + list(range(1, replicas, 2))


def shift_columns(array, by, columns):
    if by == 0:
        return array
    size = array.shape[0]
    column = lax.broadcasted_iota(jnp.int32, array.shape, 0) % columns + by
    moved = pltpu.roll(array, (-by) % size, 0)
    return jnp.where((column >= 0) & (column < columns), moved, 0.0)


def tap_row(x, w_ref, a, columns, reach):
    width = w_ref.shape[2]
    weight = jnp.concatenate([w_ref[3 * a + b] for b in range(3)], axis=1)
    product = jnp.dot(x, weight, preferred_element_type=jnp.float32)
    return sum(
        shift_columns(product[:, b * width : (b + 1) * width], (b - 1) * reach, columns)
        for b in range(3)
    )


def load_kernel(replicas, cover, x_hbm, w_hbm, x_ref, w_ref, *refs):
    *outs, room, x_sem, w_sem, out_sems = refs
    x_load = pltpu.make_async_copy(x_hbm, x_ref, x_sem)
    w_load = pltpu.make_async_copy(w_hbm, w_ref, w_sem)
    x_load.start()
    w_load.start()
    x_load.wait()
    copies = []
    for out in outs:
        bands = room.shape[0]
        x = x_ref[...]
        for s in range(bands):
            room[s] = jnp.concatenate(
                [
                    x[:, (d * bands + s) * cover : (d * bands + s + 1) * cover]
                    for d in replica_order(replicas)
                ],
                axis=1,
            )
            copies.append(pltpu.make_async_copy(room.at[s], out.at[s], out_sems.at[s]))
            copies[-1].start()
    w_load.wait()
    for copy in copies:
        copy.wait()


def load(flat, weight, bands, replicas, cover, blocks):
    pixels, channels = flat.shape
    hbm = pl.BlockSpec(memory_space=pltpu.HBM)
    vmem = pl.BlockSpec(memory_space=pltpu.VMEM)
    shape = (bands, pixels, replicas * cover)
    count = 1 if blocks else 0
    return pl.pallas_call(
        functools.partial(load_kernel, replicas, cover),
        in_specs=[hbm, hbm],
        out_specs=[vmem, vmem] + [hbm] * count,
        out_shape=[
            pltpu.VMEM(flat.shape, flat.dtype),
            pltpu.VMEM(weight.shape, weight.dtype),
        ]
        + [pltpu.HBM(shape, flat.dtype)] * count,
        scratch_shapes=[
            pltpu.VMEM(shape, flat.dtype),
            pltpu.SemaphoreType.DMA,
            pltpu.SemaphoreType.DMA,
            pltpu.SemaphoreType.DMA((bands,)),
        ],
        compiler_params=pltpu.CompilerParams(vmem_limit_bytes=VMEM_LIMIT),
        cost_estimate=pl.CostEstimate(
            flops=0,
            bytes_accessed=2 * weight.size + 4 * pixels * channels,
            transcendentals=0,
        ),
        name="load",
    )(
        pltpu.with_memory_space_constraint(flat, pltpu.HBM),
        pltpu.with_memory_space_constraint(weight, pltpu.HBM),
    )


def halo_sums(x_ref, w_ref, columns, reach):
    pixels, edge = x_ref.shape[0], reach * columns
    width = w_ref.shape[2]
    if pixels > edge:
        down = tap_row(x_ref[pixels - edge :], w_ref, 0, columns, reach)
        up = tap_row(x_ref[:edge], w_ref, 2, columns, reach)
        return down, up
    weight = jnp.concatenate([w_ref[t] for t in (0, 1, 2, 6, 7, 8)], axis=1)
    product = jnp.dot(x_ref[...], weight, preferred_element_type=jnp.float32)
    return [
        sum(
            shift_columns(
                product[:, (3 * k + b) * width : (3 * k + b + 1) * width], (b - 1) * reach, columns
            )
            for b in range(3)
        )
        for k in range(2)
    ]


def lay_out_kernel(columns, reach, replicas, cover, x_hbm, w_hbm, x_ref, w_ref, *refs):
    *blocks, sums_ref, room, x_sem, w_sems = refs
    bands = len(blocks)
    band = lax.axis_index("space")
    lanes = room.shape[2]
    x_load = pltpu.make_async_copy(x_hbm, x_ref, x_sem)
    x_load.start()
    w_loads = []
    for n, (t, size) in enumerate(((0, 3), (6, 3), (3, 3))):
        here = pl.ds(t, size)
        w_loads.append(pltpu.make_async_copy(w_hbm.at[here], w_ref.at[here], w_sems.at[n]))
        w_loads[-1].start()
    x_load.wait()
    x = x_ref[...]
    for s in range(bands):
        room[s] = jnp.concatenate(
            [
                x[:, (d * bands + s) * cover : (d * bands + s + 1) * cover]
                for d in replica_order(replicas)
            ],
            axis=1,
        )
    for k, block in enumerate(blocks):
        block[:, :lanes] = room[jnp.bitwise_xor(band, k)]
    w_loads[0].wait()
    w_loads[1].wait()
    down, up = halo_sums(x_ref, w_ref, columns, reach)
    sums_ref[...] = jnp.where(band < 2, down, up).astype(x.dtype)
    blocks[1][:, lanes:] = jnp.where(lax.rem(band, 2) == 0, down, up).astype(x.dtype)
    w_loads[2].wait()


def lay_out(flat, weight, columns, reach, bands, replicas, cover):
    pixels, channels = flat.shape
    width = weight.shape[2]
    hbm = pl.BlockSpec(memory_space=pltpu.HBM)
    vmem = pl.BlockSpec(memory_space=pltpu.VMEM)
    lanes = replicas * cover
    shapes = [(pixels, lanes + (width if k == 1 else 0)) for k in range(bands)] + [(pixels, width)]
    return pl.pallas_call(
        functools.partial(lay_out_kernel, columns, reach, replicas, cover),
        in_specs=[hbm, hbm],
        out_specs=[vmem] * (3 + bands),
        out_shape=[
            pltpu.VMEM(flat.shape, flat.dtype),
            pltpu.VMEM(weight.shape, weight.dtype),
        ]
        + [pltpu.VMEM(shape, flat.dtype) for shape in shapes],
        scratch_shapes=[
            pltpu.VMEM((bands, pixels, lanes), flat.dtype),
            pltpu.SemaphoreType.DMA,
            pltpu.SemaphoreType.DMA((3,)),
        ],
        compiler_params=pltpu.CompilerParams(vmem_limit_bytes=VMEM_LIMIT),
        cost_estimate=pl.CostEstimate(
            flops=12 * pixels * channels * width,
            bytes_accessed=2 * weight.size + 4 * pixels * channels,
            transcendentals=0,
        ),
        name="lay_out",
    )(
        pltpu.with_memory_space_constraint(flat, pltpu.HBM),
        pltpu.with_memory_space_constraint(weight, pltpu.HBM),
    )


def halo_kernel(columns, reach, x_ref, w_ref, down_ref, up_ref):
    down, up = halo_sums(x_ref, w_ref, columns, reach)
    down_ref[...] = down.astype(down_ref.dtype)
    up_ref[...] = up.astype(up_ref.dtype)


def halo(flat, weight, columns, reach):
    _, channels = flat.shape
    width = weight.shape[2]
    edge = reach * columns
    return pl.pallas_call(
        functools.partial(halo_kernel, columns, reach),
        out_shape=[pltpu.VMEM((edge, width), jnp.bfloat16)] * 2,
        compiler_params=pltpu.CompilerParams(vmem_limit_bytes=VMEM_LIMIT),
        cost_estimate=pl.CostEstimate(
            flops=12 * edge * channels * width,
            bytes_accessed=12 * channels * width + 2 * edge * channels,
            transcendentals=0,
        ),
        name="halo",
    )(flat, weight)


def middle_kernel(columns, reach, x_ref, w_ref, after_ref, out_ref):
    del after_ref
    pixels, edge = x_ref.shape[0], reach * columns
    out_ref[...] = tap_row(x_ref[...], w_ref, 1, columns, reach)
    if pixels > edge:
        out_ref[edge:] += tap_row(x_ref[: pixels - edge], w_ref, 0, columns, reach)
        out_ref[: pixels - edge] += tap_row(x_ref[edge:], w_ref, 2, columns, reach)


def middle_taps(flat, weight, after, columns, reach):
    pixels, channels = flat.shape
    width = weight.shape[2]
    vmem = pl.BlockSpec(memory_space=pltpu.VMEM)
    return pl.pallas_call(
        functools.partial(middle_kernel, columns, reach),
        in_specs=[vmem, vmem, vmem],
        out_shape=pltpu.VMEM((pixels, width), jnp.float32),
        compiler_params=pltpu.CompilerParams(vmem_limit_bytes=VMEM_LIMIT),
        cost_estimate=pl.CostEstimate(
            flops=6 * pixels * channels * width,
            bytes_accessed=6 * channels * width + 2 * pixels * channels,
            transcendentals=0,
        ),
        name="middle_taps",
    )(flat, weight, after)


def as_column(rows_ref):
    values = rows_ref[...].astype(jnp.float32)
    rows, columns = values.shape
    shape = (columns, columns)
    same = lax.broadcasted_iota(jnp.int32, shape, 0) == lax.broadcasted_iota(jnp.int32, shape, 1)
    return jnp.concatenate(
        [
            jnp.sum(jnp.where(same, values[r : r + 1], 0.0), axis=1, keepdims=True)
            for r in range(rows)
        ],
        axis=0,
    )


def pointwise_kernel(*refs):
    middle_ref, below_ref, above_ref, bias_ref, class_ref, label_ref, scale_ref, out_ref = refs[-8:]
    pixels, width = middle_ref.shape
    edge = above_ref.shape[0]
    above = above_ref[:, above_ref.shape[1] - width :].astype(jnp.float32)
    below = below_ref[:, below_ref.shape[1] - width :].astype(jnp.float32)
    if pixels > edge:
        none = jnp.zeros((pixels - edge, width), jnp.float32)
        above = jnp.concatenate([above, none], axis=0)
        below = jnp.concatenate([none, below], axis=0)
    preact = middle_ref[...] + above + below + bias_ref[...]
    sigmoid_z = jax.nn.sigmoid(preact)
    hidden = (preact * sigmoid_z).astype(jnp.bfloat16)
    classes = class_ref[...]
    logits = lax.dot_general(
        hidden, classes, (((1,), (1,)), ((), ())), preferred_element_type=jnp.float32
    )
    exponent = jnp.exp(logits)
    chances = exponent / jnp.sum(exponent, axis=1, keepdims=True)
    index = lax.broadcasted_iota(jnp.int32, chances.shape, 1).astype(jnp.float32)
    onehot = jnp.where(as_column(label_ref) == index, 1.0, 0.0)
    grad_logits = as_column(scale_ref) * (chances - onehot)
    wide = classes.astype(jnp.float32)
    hidden_grad = sum(
        grad_logits[:, k : k + 1] * wide[k : k + 1] for k in range(classes.shape[0])
    )
    gradient = hidden_grad * sigmoid_z * (1.0 + preact * (1.0 - sigmoid_z))
    out_ref[...] = gradient.astype(out_ref.dtype)


def pointwise(middle, above, below, bias, classes, labels, scale, after):
    pixels, width = middle.shape
    return pl.pallas_call(
        pointwise_kernel,
        out_shape=jax.ShapeDtypeStruct((pixels, width), jnp.bfloat16),
        compiler_params=pltpu.CompilerParams(vmem_limit_bytes=VMEM_LIMIT),
        cost_estimate=pl.CostEstimate(
            flops=30 * pixels * width,
            bytes_accessed=10 * pixels * width,
            transcendentals=pixels * width,
        ),
        name="pointwise",
    )(*after, middle, below, above, bias, classes, labels, scale)


def shifted_taps(gradient, columns, reach):
    wide = gradient.astype(jnp.float32)
    return jnp.concatenate(
        [shift_columns(wide, (1 - b) * reach, columns).astype(jnp.bfloat16) for b in range(3)],
        axis=1,
    )


def kernel_grad_kernel(columns, reach, parts, others, distances, before, given, lanes, *refs):
    x_refs, refs = refs[:given], refs[given:]
    count = len(distances)
    g_refs, sums, outs = refs[:count], refs[count : count + before], refs[count + before : -1]
    padded = refs[-1]
    pixels, width = g_refs[0].shape
    total = padded.shape[1] - 2 * reach * columns
    bands = total // pixels
    edge = reach * columns
    extra = lanes // parts
    band = lax.axis_index("space")
    slots = given > 1
    shifted = [shifted_taps(g_ref[...], columns, reach) for g_ref in g_refs]
    for n, (other, out_ref) in enumerate(zip(others, outs)):
        part = lax.rem(lax.axis_index("dp") + other, parts)
        for k, x_ref in enumerate(x_refs):
            if extra % 128 == 0:
                features = x_ref[..., pl.ds(pl.multiple_of(part * extra, 128), extra)]
            else:
                features = x_ref[..., :extra]
                for j in range(1, parts):
                    other_part = x_ref[..., j * extra : (j + 1) * extra]
                    features = jnp.where(part == j, other_part, features)
            if slots:
                padded[n, k * pixels : (k + 1) * pixels] = features
            else:
                padded[n, edge : edge + total] = features.reshape(total, extra)
        if slots:
            padded[n, total : total + pixels] = jnp.zeros((pixels, extra), padded.dtype)
        else:
            padded[n, :edge] = jnp.zeros((edge, extra), padded.dtype)
            padded[n, edge + total :] = jnp.zeros((edge, extra), padded.dtype)
        for a in range(3):
            here = pl.ds(3 * a * width, 3 * width)
            grad = sums[n][:, here] if before else None
            for k, right in zip(distances, shifted):
                from_band = lax.rem(band + bands - k, bands)
                if slots:
                    row = from_band + (a - 1)
                    inside = (row >= 0) & (row < bands)
                    slot = jnp.bitwise_xor(band, jnp.clip(row, 0, bands - 1))
                    first = jnp.where(inside, slot, bands) * pixels
                else:
                    first = from_band * pixels + a * edge
                left = padded[n, pl.ds(pl.multiple_of(first, 16), pixels)]
                term = lax.dot_general(
                    left, right, (((0,), (0,)), ((), ())), preferred_element_type=jnp.float32
                )
                grad = term if grad is None else grad + term
            out_ref[:, here] = grad.astype(out_ref.dtype)


def kernel_grad(features, gradients, sums, columns, reach, parts, others, dtype, bands, lanes):
    distances = tuple(gradients)
    pixels, width = gradients[distances[0]].shape
    extra = lanes // parts
    work = len(others) * len(distances) * pixels * extra * width
    return pl.pallas_call(
        functools.partial(
            kernel_grad_kernel,
            columns,
            reach,
            parts,
            others,
            distances,
            len(sums),
            len(features),
            lanes,
        ),
        out_shape=[pltpu.VMEM((extra, 9 * width), dtype)] * len(others),
        scratch_shapes=[pltpu.VMEM((len(others), bands * pixels + 2 * reach * columns, extra), jnp.bfloat16)],
        compiler_params=pltpu.CompilerParams(vmem_limit_bytes=VMEM_LIMIT),
        cost_estimate=pl.CostEstimate(
            flops=18 * work, bytes_accessed=2 * bands * pixels * lanes, transcendentals=0
        ),
        name="kernel_grad",
    )(*features, *gradients.values(), *sums)


def partner(i, k, count):
    return i ^ k if count & (count - 1) == 0 else (i + k) % count


def split_kernel(parts, terms, *refs):
    ins, outs = refs[:terms], refs[terms:]
    count = len(outs)
    cover = outs[0].shape[0]
    me = lax.axis_index("dp") // parts
    for k, out in enumerate(outs):
        if count == 1:
            rows = pl.ds(0, cover)
        else:
            block = jnp.bitwise_xor(me, k) if count & (count - 1) == 0 else lax.rem(me + k, count)
            rows = pl.ds(pl.multiple_of(block * cover, cover), cover)
        total = ins[0][rows, :].astype(jnp.float32)
        for ref in ins[1:]:
            total += ref[rows, :].astype(jnp.float32)
        out[...] = total.astype(out.dtype)


def split_up(terms, parts, count):
    rows, lanes = terms[0].shape
    return pl.pallas_call(
        functools.partial(split_kernel, parts, len(terms)),
        out_shape=[jax.ShapeDtypeStruct((rows // count, lanes), jnp.bfloat16)] * count,
        compiler_params=pltpu.CompilerParams(vmem_limit_bytes=VMEM_LIMIT),
        name="split_up",
    )(*terms)


def final_kernel(replicas, *refs):
    *ins, out_ref = refs
    cover, lanes = ins[0].shape
    width = out_ref.shape[1]
    taps = lanes // width
    total = ins[0][...].astype(jnp.float32)
    for ref in ins[1:]:
        total += ref[...].astype(jnp.float32)
    total = total / replicas
    for t in range(taps):
        out_ref[pl.ds(t, cover, stride=taps), :] = total[:, t * width : (t + 1) * width]


def final(blocks, width, replicas):
    cover, lanes = blocks[0].shape
    return pl.pallas_call(
        functools.partial(final_kernel, replicas),
        out_shape=jax.ShapeDtypeStruct((cover * lanes // width, width), jnp.float32),
        compiler_params=pltpu.CompilerParams(vmem_limit_bytes=VMEM_LIMIT),
        name="final_sum",
    )(*blocks)


def feature_grad_kernel(columns, reach, bands, own_ref, above_ref, below_ref, w_ref, out, room, sems):
    band = lax.axis_index("space")
    pixels, width = own_ref.shape
    edge = reach * columns
    own = own_ref[...]
    above = above_ref[pixels - edge :]
    below = below_ref[:edge]
    above = jnp.where(band > 0, above, jnp.zeros_like(above))
    below = jnp.where(band + 1 < bands, below, jnp.zeros_like(below))
    stack = shifted_taps(jnp.concatenate([above, own, below], axis=0), columns, reach)
    taps = jnp.concatenate(
        [stack[(2 - a) * edge : (2 - a) * edge + pixels] for a in range(3)], axis=1
    )
    steps, _, step = room.shape
    copies = []
    for n in range(steps):
        here = pl.ds(n * step, step)
        weight = jnp.concatenate([w_ref[t, here, :] for t in range(w_ref.shape[0])], axis=1)
        room[n] = lax.dot_general(
            taps, weight, (((1,), (1,)), ((), ())), preferred_element_type=jnp.float32
        )
        copies.append(pltpu.make_async_copy(room.at[n], out.at[:, here], sems.at[n]))
        copies[-1].start()
    for copy in copies:
        copy.wait()


def feature_grad(own, above, below, weight, columns, reach, bands):
    pixels, _ = own.shape
    taps, channels, width = weight.shape
    step = 256 if channels % 256 == 0 else channels
    vmem = pl.BlockSpec(memory_space=pltpu.VMEM)
    return pl.pallas_call(
        functools.partial(feature_grad_kernel, columns, reach, bands),
        in_specs=[vmem] * 4,
        out_specs=pl.BlockSpec(memory_space=pltpu.HBM),
        out_shape=pltpu.HBM((pixels, channels), jnp.float32),
        scratch_shapes=[
            pltpu.VMEM((channels // step, pixels, step), jnp.float32),
            pltpu.SemaphoreType.DMA((channels // step,)),
        ],
        compiler_params=pltpu.CompilerParams(vmem_limit_bytes=VMEM_LIMIT),
        cost_estimate=pl.CostEstimate(
            flops=2 * pixels * taps * channels * width,
            bytes_accessed=2 * taps * channels * width + 4 * pixels * channels,
            transcendentals=0,
        ),
        name="feature_grad",
    )(own, above, below, weight)


def on_device(features, labels, pixel_weight, conv_weight, conv_bias, class_weight):
    image = features[0]
    band_rows, columns, channels = image.shape
    taps, width = conv_weight.shape[1:]
    pixels = band_rows * columns
    replicas = lax.axis_size("dp")
    bands = lax.axis_size("space")
    reach = DILATION_SIZE

    flat = image.reshape(pixels, channels)
    weight = conv_weight.transpose(1, 0, 2)
    block_rows, cover, picks, offsets = channel_plan(channels, taps, replicas, bands)
    even = block_rows % taps == 0
    parts = 2 if replicas % 2 == 0 else 1
    count = replicas // parts
    paired = bands == 4 and band_rows == reach and even
    if paired:
        flat, weight, own, *blocks, sums = lay_out(
            flat, weight, columns, reach, bands, replicas, cover
        )
        below = lax.ppermute(sums, "space", [(1, 2), (2, 1)])
        whole = [own] + [
            lax.ppermute(block, "space", [(i, i ^ k) for i in range(bands)])
            for k, block in enumerate(blocks, 1)
        ]
        above, after = whole[1], sums
    else:
        flat, weight, *split = load(flat, weight, bands, replicas, cover, even)
        if not even:
            order = jnp.array([c for line in picks for c in line], jnp.int32)
            split = jnp.take(flat, order, axis=1).reshape(pixels, bands, replicas * cover)
            split = [split.transpose(1, 0, 2)]
        whole = [lax.all_to_all(split[0], "space", 0, 0)]
        down, up = halo(flat, weight, columns, reach)
        above = lax.ppermute(down, "space", [(i, i + 1) for i in range(bands - 1)])
        below = lax.ppermute(up, "space", [(i + 1, i) for i in range(bands - 1)])
        after = up
    middle = middle_taps(flat, weight, after, columns, reach)

    gradient = pointwise(
        middle,
        above,
        below,
        conv_bias.reshape(1, width),
        class_weight.T,
        labels.reshape(band_rows, columns),
        pixel_weight.reshape(band_rows, columns),
        whole[2:3],
    )
    gradients = [gradient] + [
        lax.ppermute(gradient, "space", [(i, (i + k) % bands) for i in range(bands)])
        for k in range(1, bands)
    ]
    late = bands // 2
    early = {k: g for k, g in enumerate(gradients) if k != late or bands == 1}
    others = (0, 1)[:parts]
    size = (bands, replicas * cover)
    terms = kernel_grad(whole, early, [], columns, reach, parts, others, jnp.float32, *size)
    if bands > 1:
        last = {late: gradients[late]}
        own, *theirs = terms
        terms = kernel_grad(whole, last, [own], columns, reach, parts, (0,), jnp.float32, *size)
        if theirs:
            terms += kernel_grad(whole, last, theirs, columns, reach, parts, (1,), jnp.bfloat16, *size)
    if parts == 2:
        theirs = terms[1].astype(jnp.bfloat16)
        terms = [terms[0], lax.ppermute(theirs, "dp", [(i, i ^ 1) for i in range(replicas)])]
    if cover % 16 == 0 and count <= 8:
        blocks = split_up(terms, parts, count)
        came = [blocks[0]]
        for k in reversed(range(1, count)):
            pairs = [(i, parts * partner(i // parts, k, count) + i % parts) for i in range(replicas)]
            came.append(lax.ppermute(blocks[k], "dp", pairs))
    else:
        blocks = split_up(terms, parts, 1)[0].reshape(count, cover, taps * width)
        groups = [list(range(c, replicas, parts)) for c in range(parts)]
        came = list(lax.all_to_all(blocks, "dp", 0, 0, axis_index_groups=groups))
    weight_grad = final(came, width, replicas)
    if not even:
        start = jnp.array(offsets)[lax.axis_index("space"), lax.axis_index("dp")]
        weight_grad = lax.dynamic_slice_in_dim(weight_grad, start, block_rows)

    grad = feature_grad(gradient, gradients[1 % bands], gradients[-1], weight, columns, reach, bands)
    return grad.reshape(1, band_rows, columns, channels), weight_grad


def solution(mesh):
    placed = (
        P("dp", "space", None, None),
        P("dp", "space", None),
        P("dp", "space", None),
        P(),
        P(),
        P(),
    )
    return jax.shard_map(
        on_device,
        mesh=mesh,
        in_specs=placed,
        out_specs=(P("dp", "space", None, None), P(("dp", "space"), None)),
        check_vma=False,
    )
```

```python
import functools

import jax
import jax.numpy as jnp
from jax import lax
from jax.experimental import pallas as pl
from jax.experimental.pallas import tpu as pltpu
from jax.sharding import PartitionSpec as P

DILATION_SIZE = 6
VMEM_LIMIT = 16 * 1024 * 1024
VMEM_WHOLE = 62 * 1024 * 1024


def channel_plan(channels, taps, replicas, bands):
    rows = channels * taps // (replicas * bands)
    starts = [[(d * bands + s) * rows // taps for d in range(replicas)] for s in range(bands)]
    offsets = [[(d * bands + s) * rows % taps for d in range(replicas)] for s in range(bands)]
    cover = max(-(-(off + rows) // taps) for line in offsets for off in line)
    picks = [
        [min(line[d] + k, channels - 1) for d in replica_order(replicas) for k in range(cover)]
        for line in starts
    ]
    return rows, cover, picks, offsets


def replica_order(replicas):
    if replicas % 2:
        return list(range(replicas))
    return list(range(0, replicas, 2)) + list(range(1, replicas, 2))


def shift_columns(array, by, columns):
    if by == 0:
        return array
    size = array.shape[0]
    column = lax.broadcasted_iota(jnp.int32, array.shape, 0) % columns + by
    moved = pltpu.roll(array, (-by) % size, 0)
    return jnp.where((column >= 0) & (column < columns), moved, 0.0)


def tap_row(x, w_ref, a, columns, reach):
    width = w_ref.shape[2]
    weight = jnp.concatenate([w_ref[3 * a + b] for b in range(3)], axis=1)
    product = jnp.dot(x, weight, preferred_element_type=jnp.float32)
    return sum(
        shift_columns(product[:, b * width : (b + 1) * width], (b - 1) * reach, columns)
        for b in range(3)
    )


def load_kernel(replicas, cover, x_hbm, w_hbm, x_ref, w_ref, *refs):
    *outs, room, x_sem, w_sem, out_sems = refs
    x_load = pltpu.make_async_copy(x_hbm, x_ref, x_sem)
    w_load = pltpu.make_async_copy(w_hbm, w_ref, w_sem)
    x_load.start()
    w_load.start()
    x_load.wait()
    copies = []
    for out in outs:
        bands = room.shape[0]
        x = x_ref[...]
        for s in range(bands):
            room[s] = jnp.concatenate(
                [
                    x[:, (d * bands + s) * cover : (d * bands + s + 1) * cover]
                    for d in replica_order(replicas)
                ],
                axis=1,
            )
            copies.append(pltpu.make_async_copy(room.at[s], out.at[s], out_sems.at[s]))
            copies[-1].start()
    w_load.wait()
    for copy in copies:
        copy.wait()


def load(flat, weight, bands, replicas, cover, blocks):
    pixels, channels = flat.shape
    hbm = pl.BlockSpec(memory_space=pltpu.HBM)
    vmem = pl.BlockSpec(memory_space=pltpu.VMEM)
    shape = (bands, pixels, replicas * cover)
    count = 1 if blocks else 0
    return pl.pallas_call(
        functools.partial(load_kernel, replicas, cover),
        in_specs=[hbm, hbm],
        out_specs=[vmem, vmem] + [hbm] * count,
        out_shape=[
            pltpu.VMEM(flat.shape, flat.dtype),
            pltpu.VMEM(weight.shape, weight.dtype),
        ]
        + [pltpu.HBM(shape, flat.dtype)] * count,
        scratch_shapes=[
            pltpu.VMEM(shape, flat.dtype),
            pltpu.SemaphoreType.DMA,
            pltpu.SemaphoreType.DMA,
            pltpu.SemaphoreType.DMA((bands,)),
        ],
        compiler_params=pltpu.CompilerParams(vmem_limit_bytes=VMEM_LIMIT),
        cost_estimate=pl.CostEstimate(
            flops=0,
            bytes_accessed=2 * weight.size + 4 * pixels * channels,
            transcendentals=0,
        ),
        name="load",
    )(
        pltpu.with_memory_space_constraint(flat, pltpu.HBM),
        pltpu.with_memory_space_constraint(weight, pltpu.HBM),
    )


def halo_sums(x_ref, w_ref, columns, reach):
    pixels, edge = x_ref.shape[0], reach * columns
    width = w_ref.shape[2]
    if pixels > edge:
        down = tap_row(x_ref[pixels - edge :], w_ref, 0, columns, reach)
        up = tap_row(x_ref[:edge], w_ref, 2, columns, reach)
        return down, up
    weight = jnp.concatenate([w_ref[t] for t in (0, 1, 2, 6, 7, 8)], axis=1)
    product = jnp.dot(x_ref[...], weight, preferred_element_type=jnp.float32)
    return [
        sum(
            shift_columns(
                product[:, (3 * k + b) * width : (3 * k + b + 1) * width], (b - 1) * reach, columns
            )
            for b in range(3)
        )
        for k in range(2)
    ]


def lay_out_kernel(columns, reach, replicas, cover, x_hbm, w_hbm, x_ref, w_ref, *refs):
    *blocks, sums_ref, room, x_sem, w_sems = refs
    bands = len(blocks)
    band = lax.axis_index("space")
    lanes = room.shape[2]
    x_load = pltpu.make_async_copy(x_hbm, x_ref, x_sem)
    x_load.start()
    w_loads = []
    for n, (t, size) in enumerate(((0, 3), (6, 3), (3, 3))):
        here = pl.ds(t, size)
        w_loads.append(pltpu.make_async_copy(w_hbm.at[here], w_ref.at[here], w_sems.at[n]))
        w_loads[-1].start()
    x_load.wait()
    x = x_ref[...]
    for s in range(bands):
        room[s] = jnp.concatenate(
            [
                x[:, (d * bands + s) * cover : (d * bands + s + 1) * cover]
                for d in replica_order(replicas)
            ],
            axis=1,
        )
    for k, block in enumerate(blocks):
        block[:, :lanes] = room[jnp.bitwise_xor(band, k)]
    w_loads[0].wait()
    w_loads[1].wait()
    down, up = halo_sums(x_ref, w_ref, columns, reach)
    sums_ref[...] = jnp.where(band < 2, down, up).astype(x.dtype)
    blocks[1][:, lanes:] = jnp.where(lax.rem(band, 2) == 0, down, up).astype(x.dtype)
    w_loads[2].wait()


def lay_out(flat, weight, columns, reach, bands, replicas, cover):
    pixels, channels = flat.shape
    width = weight.shape[2]
    hbm = pl.BlockSpec(memory_space=pltpu.HBM)
    vmem = pl.BlockSpec(memory_space=pltpu.VMEM)
    lanes = replicas * cover
    shapes = [(pixels, lanes + (width if k == 1 else 0)) for k in range(bands)] + [(pixels, width)]
    return pl.pallas_call(
        functools.partial(lay_out_kernel, columns, reach, replicas, cover),
        in_specs=[hbm, hbm],
        out_specs=[vmem] * (3 + bands),
        out_shape=[
            pltpu.VMEM(flat.shape, flat.dtype),
            pltpu.VMEM(weight.shape, weight.dtype),
        ]
        + [pltpu.VMEM(shape, flat.dtype) for shape in shapes],
        scratch_shapes=[
            pltpu.VMEM((bands, pixels, lanes), flat.dtype),
            pltpu.SemaphoreType.DMA,
            pltpu.SemaphoreType.DMA((3,)),
        ],
        compiler_params=pltpu.CompilerParams(vmem_limit_bytes=VMEM_LIMIT),
        cost_estimate=pl.CostEstimate(
            flops=12 * pixels * channels * width,
            bytes_accessed=2 * weight.size + 4 * pixels * channels,
            transcendentals=0,
        ),
        name="lay_out",
    )(
        pltpu.with_memory_space_constraint(flat, pltpu.HBM),
        pltpu.with_memory_space_constraint(weight, pltpu.HBM),
    )


def halo_kernel(columns, reach, x_ref, w_ref, down_ref, up_ref):
    down, up = halo_sums(x_ref, w_ref, columns, reach)
    down_ref[...] = down.astype(down_ref.dtype)
    up_ref[...] = up.astype(up_ref.dtype)


def halo(flat, weight, columns, reach):
    _, channels = flat.shape
    width = weight.shape[2]
    edge = reach * columns
    return pl.pallas_call(
        functools.partial(halo_kernel, columns, reach),
        out_shape=[pltpu.VMEM((edge, width), jnp.bfloat16)] * 2,
        compiler_params=pltpu.CompilerParams(vmem_limit_bytes=VMEM_LIMIT),
        cost_estimate=pl.CostEstimate(
            flops=12 * edge * channels * width,
            bytes_accessed=12 * channels * width + 2 * edge * channels,
            transcendentals=0,
        ),
        name="halo",
    )(flat, weight)


def middle_kernel(columns, reach, x_ref, w_ref, after_ref, out_ref):
    del after_ref
    pixels, edge = x_ref.shape[0], reach * columns
    out_ref[...] = tap_row(x_ref[...], w_ref, 1, columns, reach)
    if pixels > edge:
        out_ref[edge:] += tap_row(x_ref[: pixels - edge], w_ref, 0, columns, reach)
        out_ref[: pixels - edge] += tap_row(x_ref[edge:], w_ref, 2, columns, reach)


def middle_taps(flat, weight, after, columns, reach):
    pixels, channels = flat.shape
    width = weight.shape[2]
    vmem = pl.BlockSpec(memory_space=pltpu.VMEM)
    return pl.pallas_call(
        functools.partial(middle_kernel, columns, reach),
        in_specs=[vmem, vmem, vmem],
        out_shape=pltpu.VMEM((pixels, width), jnp.float32),
        compiler_params=pltpu.CompilerParams(vmem_limit_bytes=VMEM_LIMIT),
        cost_estimate=pl.CostEstimate(
            flops=6 * pixels * channels * width,
            bytes_accessed=6 * channels * width + 2 * pixels * channels,
            transcendentals=0,
        ),
        name="middle_taps",
    )(flat, weight, after)


def as_column(rows_ref):
    values = rows_ref[...].astype(jnp.float32)
    rows, columns = values.shape
    shape = (columns, columns)
    same = lax.broadcasted_iota(jnp.int32, shape, 0) == lax.broadcasted_iota(jnp.int32, shape, 1)
    return jnp.concatenate(
        [
            jnp.sum(jnp.where(same, values[r : r + 1], 0.0), axis=1, keepdims=True)
            for r in range(rows)
        ],
        axis=0,
    )


def pointwise_kernel(*refs):
    middle_ref, above_ref, below_ref, bias_ref, class_ref, label_ref, scale_ref, out_ref = refs[-8:]
    pixels, width = middle_ref.shape
    edge = above_ref.shape[0]
    above = above_ref[:, above_ref.shape[1] - width :].astype(jnp.float32)
    below = below_ref[:, below_ref.shape[1] - width :].astype(jnp.float32)
    if pixels > edge:
        none = jnp.zeros((pixels - edge, width), jnp.float32)
        above = jnp.concatenate([above, none], axis=0)
        below = jnp.concatenate([none, below], axis=0)
    preact = middle_ref[...] + above + below + bias_ref[...]
    sigmoid_z = jax.nn.sigmoid(preact)
    hidden = (preact * sigmoid_z).astype(jnp.bfloat16)
    classes = class_ref[...]
    logits = lax.dot_general(
        hidden, classes, (((1,), (1,)), ((), ())), preferred_element_type=jnp.float32
    )
    exponent = jnp.exp(logits)
    chances = exponent / jnp.sum(exponent, axis=1, keepdims=True)
    index = lax.broadcasted_iota(jnp.int32, chances.shape, 1).astype(jnp.float32)
    onehot = jnp.where(as_column(label_ref) == index, 1.0, 0.0)
    grad_logits = as_column(scale_ref) * (chances - onehot)
    wide = classes.astype(jnp.float32)
    hidden_grad = sum(
        grad_logits[:, k : k + 1] * wide[k : k + 1] for k in range(classes.shape[0])
    )
    gradient = hidden_grad * sigmoid_z * (1.0 + preact * (1.0 - sigmoid_z))
    out_ref[...] = gradient.astype(out_ref.dtype)


def pointwise(middle, above, below, bias, classes, labels, scale, after):
    pixels, width = middle.shape
    return pl.pallas_call(
        pointwise_kernel,
        out_shape=jax.ShapeDtypeStruct((pixels, width), jnp.bfloat16),
        compiler_params=pltpu.CompilerParams(vmem_limit_bytes=VMEM_LIMIT),
        cost_estimate=pl.CostEstimate(
            flops=30 * pixels * width,
            bytes_accessed=10 * pixels * width,
            transcendentals=pixels * width,
        ),
        name="pointwise",
    )(*after, middle, above, below, bias, classes, labels, scale)


def shifted_taps(gradient, columns, reach):
    wide = gradient.astype(jnp.float32)
    return jnp.concatenate(
        [shift_columns(wide, (1 - b) * reach, columns).astype(jnp.bfloat16) for b in range(3)],
        axis=1,
    )


def kernel_grad_kernel(columns, reach, parts, others, distances, before, given, lanes, *refs):
    x_refs, refs = refs[:given], refs[given:]
    count = len(distances)
    g_refs, sums, outs = refs[:count], refs[count : count + before], refs[count + before : -1]
    padded = refs[-1]
    pixels, width = g_refs[0].shape
    total = padded.shape[1] - 2 * reach * columns
    bands = total // pixels
    edge = reach * columns
    extra = lanes // parts
    band = lax.axis_index("space")
    slots = given > 1
    shifted = [shifted_taps(g_ref[...], columns, reach) for g_ref in g_refs]
    for n, (other, out_ref) in enumerate(zip(others, outs)):
        part = lax.rem(lax.axis_index("dp") + other, parts)
        for k, x_ref in enumerate(x_refs):
            if extra % 128 == 0:
                features = x_ref[..., pl.ds(pl.multiple_of(part * extra, 128), extra)]
            else:
                features = x_ref[..., :extra]
                for j in range(1, parts):
                    other_part = x_ref[..., j * extra : (j + 1) * extra]
                    features = jnp.where(part == j, other_part, features)
            if slots:
                padded[n, k * pixels : (k + 1) * pixels] = features
            else:
                padded[n, edge : edge + total] = features.reshape(total, extra)
        if slots:
            padded[n, total : total + pixels] = jnp.zeros((pixels, extra), padded.dtype)
        else:
            padded[n, :edge] = jnp.zeros((edge, extra), padded.dtype)
            padded[n, edge + total :] = jnp.zeros((edge, extra), padded.dtype)
        for a in range(3):
            here = pl.ds(3 * a * width, 3 * width)
            grad = sums[n][:, here] if before else None
            for k, right in zip(distances, shifted):
                from_band = lax.rem(band + bands - k, bands)
                if slots:
                    row = from_band + (a - 1)
                    inside = (row >= 0) & (row < bands)
                    slot = jnp.bitwise_xor(band, jnp.clip(row, 0, bands - 1))
                    first = jnp.where(inside, slot, bands) * pixels
                else:
                    first = from_band * pixels + a * edge
                left = padded[n, pl.ds(pl.multiple_of(first, 16), pixels)]
                term = lax.dot_general(
                    left, right, (((0,), (0,)), ((), ())), preferred_element_type=jnp.float32
                )
                grad = term if grad is None else grad + term
            out_ref[:, here] = grad.astype(out_ref.dtype)


def kernel_grad(features, gradients, sums, columns, reach, parts, others, dtype, bands, lanes):
    distances = tuple(gradients)
    pixels, width = gradients[distances[0]].shape
    extra = lanes // parts
    work = len(others) * len(distances) * pixels * extra * width
    return pl.pallas_call(
        functools.partial(
            kernel_grad_kernel,
            columns,
            reach,
            parts,
            others,
            distances,
            len(sums),
            len(features),
            lanes,
        ),
        out_shape=[pltpu.VMEM((extra, 9 * width), dtype)] * len(others),
        scratch_shapes=[pltpu.VMEM((len(others), bands * pixels + 2 * reach * columns, extra), jnp.bfloat16)],
        compiler_params=pltpu.CompilerParams(vmem_limit_bytes=VMEM_LIMIT),
        cost_estimate=pl.CostEstimate(
            flops=18 * work, bytes_accessed=2 * bands * pixels * lanes, transcendentals=0
        ),
        name="kernel_grad",
    )(*features, *gradients.values(), *sums)


def partner(i, k, count):
    return i ^ k if count & (count - 1) == 0 else (i + k) % count


def split_kernel(parts, terms, *refs):
    ins, outs = refs[:terms], refs[terms:]
    count = len(outs)
    cover = outs[0].shape[0]
    me = lax.axis_index("dp") // parts
    for k, out in enumerate(outs):
        if count == 1:
            rows = pl.ds(0, cover)
        else:
            block = jnp.bitwise_xor(me, k) if count & (count - 1) == 0 else lax.rem(me + k, count)
            rows = pl.ds(pl.multiple_of(block * cover, cover), cover)
        total = ins[0][rows, :].astype(jnp.float32)
        for ref in ins[1:]:
            total += ref[rows, :].astype(jnp.float32)
        out[...] = total.astype(out.dtype)


def split_up(terms, parts, count):
    rows, lanes = terms[0].shape
    return pl.pallas_call(
        functools.partial(split_kernel, parts, len(terms)),
        out_shape=[jax.ShapeDtypeStruct((rows // count, lanes), jnp.bfloat16)] * count,
        compiler_params=pltpu.CompilerParams(vmem_limit_bytes=VMEM_LIMIT),
        name="split_up",
    )(*terms)


def final_kernel(replicas, *refs):
    *ins, out_ref = refs
    cover, lanes = ins[0].shape
    width = out_ref.shape[1]
    taps = lanes // width
    total = ins[0][...].astype(jnp.float32)
    for ref in ins[1:]:
        total += ref[...].astype(jnp.float32)
    total = total / replicas
    for t in range(taps):
        out_ref[pl.ds(t, cover, stride=taps), :] = total[:, t * width : (t + 1) * width]


def final(blocks, width, replicas):
    cover, lanes = blocks[0].shape
    return pl.pallas_call(
        functools.partial(final_kernel, replicas),
        out_shape=jax.ShapeDtypeStruct((cover * lanes // width, width), jnp.float32),
        compiler_params=pltpu.CompilerParams(vmem_limit_bytes=VMEM_LIMIT),
        name="final_sum",
    )(*blocks)


def feature_grad_kernel(columns, reach, bands, own_ref, above_ref, below_ref, w_ref, out, room, sems):
    band = lax.axis_index("space")
    pixels, width = own_ref.shape
    edge = reach * columns
    own = own_ref[...]
    above = above_ref[pixels - edge :]
    below = below_ref[:edge]
    above = jnp.where(band > 0, above, jnp.zeros_like(above))
    below = jnp.where(band + 1 < bands, below, jnp.zeros_like(below))
    stack = shifted_taps(jnp.concatenate([above, own, below], axis=0), columns, reach)
    taps = jnp.concatenate(
        [stack[(2 - a) * edge : (2 - a) * edge + pixels] for a in range(3)], axis=1
    )
    steps, _, step = room.shape
    copies = []
    for n in range(steps):
        here = pl.ds(n * step, step)
        weight = jnp.concatenate([w_ref[t, here, :] for t in range(w_ref.shape[0])], axis=1)
        room[n] = lax.dot_general(
            taps, weight, (((1,), (1,)), ((), ())), preferred_element_type=jnp.float32
        )
        copies.append(pltpu.make_async_copy(room.at[n], out.at[:, here], sems.at[n]))
        copies[-1].start()
    for copy in copies:
        copy.wait()


def feature_grad(own, above, below, weight, columns, reach, bands):
    pixels, _ = own.shape
    taps, channels, width = weight.shape
    step = 256 if channels % 256 == 0 else channels
    vmem = pl.BlockSpec(memory_space=pltpu.VMEM)
    return pl.pallas_call(
        functools.partial(feature_grad_kernel, columns, reach, bands),
        in_specs=[vmem] * 4,
        out_specs=pl.BlockSpec(memory_space=pltpu.HBM),
        out_shape=pltpu.HBM((pixels, channels), jnp.float32),
        scratch_shapes=[
            pltpu.VMEM((channels // step, pixels, step), jnp.float32),
            pltpu.SemaphoreType.DMA((channels // step,)),
        ],
        compiler_params=pltpu.CompilerParams(vmem_limit_bytes=VMEM_LIMIT),
        cost_estimate=pl.CostEstimate(
            flops=2 * pixels * taps * channels * width,
            bytes_accessed=2 * taps * channels * width + 4 * pixels * channels,
            transcendentals=0,
        ),
        name="feature_grad",
    )(own, above, below, weight)


def on_device(features, labels, pixel_weight, conv_weight, conv_bias, class_weight):
    image = features[0]
    band_rows, columns, channels = image.shape
    taps, width = conv_weight.shape[1:]
    pixels = band_rows * columns
    replicas = lax.axis_size("dp")
    bands = lax.axis_size("space")
    reach = DILATION_SIZE

    flat = image.reshape(pixels, channels)
    weight = conv_weight.transpose(1, 0, 2)
    block_rows, cover, picks, offsets = channel_plan(channels, taps, replicas, bands)
    even = block_rows % taps == 0
    parts = 2 if replicas % 2 == 0 else 1
    count = replicas // parts
    paired = bands == 4 and band_rows == reach and even
    if paired:
        flat, weight, own, *blocks, sums = lay_out(
            flat, weight, columns, reach, bands, replicas, cover
        )
        below = lax.ppermute(sums, "space", [(1, 2), (2, 1)])
        whole = [own] + [
            lax.ppermute(block, "space", [(i, i ^ k) for i in range(bands)])
            for k, block in enumerate(blocks, 1)
        ]
        above, after = whole[1], sums
    else:
        flat, weight, *split = load(flat, weight, bands, replicas, cover, even)
        if not even:
            order = jnp.array([c for line in picks for c in line], jnp.int32)
            split = jnp.take(flat, order, axis=1).reshape(pixels, bands, replicas * cover)
            split = [split.transpose(1, 0, 2)]
        whole = [lax.all_to_all(split[0], "space", 0, 0)]
        down, up = halo(flat, weight, columns, reach)
        above = lax.ppermute(down, "space", [(i, i + 1) for i in range(bands - 1)])
        below = lax.ppermute(up, "space", [(i + 1, i) for i in range(bands - 1)])
        after = up
    middle = middle_taps(flat, weight, after, columns, reach)

    gradient = pointwise(
        middle,
        above,
        below,
        conv_bias.reshape(1, width),
        class_weight.T,
        labels.reshape(band_rows, columns),
        pixel_weight.reshape(band_rows, columns),
        whole[2:3],
    )
    gradients = [gradient] + [
        lax.ppermute(gradient, "space", [(i, (i + k) % bands) for i in range(bands)])
        for k in range(1, bands)
    ]
    late = range(bands // 2, min(bands // 2 + 2, bands))
    early = {k: g for k, g in enumerate(gradients) if k not in late or bands == 1}
    others = (0, 1)[:parts]
    size = (bands, replicas * cover)
    terms = kernel_grad(whole, early, [], columns, reach, parts, others, jnp.float32, *size)
    if bands > 1:
        last = {k: gradients[k] for k in late}
        own, *theirs = terms
        terms = kernel_grad(whole, last, [own], columns, reach, parts, (0,), jnp.float32, *size)
        if theirs:
            terms += kernel_grad(whole, last, theirs, columns, reach, parts, (1,), jnp.bfloat16, *size)
    if parts == 2:
        theirs = terms[1].astype(jnp.bfloat16)
        terms = [terms[0], lax.ppermute(theirs, "dp", [(i, i ^ 1) for i in range(replicas)])]
    if cover % 16 == 0 and count <= 8:
        blocks = split_up(terms, parts, count)
        came = [blocks[0]]
        for k in reversed(range(1, count)):
            pairs = [(i, parts * partner(i // parts, k, count) + i % parts) for i in range(replicas)]
            came.append(lax.ppermute(blocks[k], "dp", pairs))
    else:
        blocks = split_up(terms, parts, 1)[0].reshape(count, cover, taps * width)
        groups = [list(range(c, replicas, parts)) for c in range(parts)]
        came = list(lax.all_to_all(blocks, "dp", 0, 0, axis_index_groups=groups))
    weight_grad = final(came, width, replicas)
    if not even:
        start = jnp.array(offsets)[lax.axis_index("space"), lax.axis_index("dp")]
        weight_grad = lax.dynamic_slice_in_dim(weight_grad, start, block_rows)

    grad = feature_grad(gradient, gradients[1 % bands], gradients[-1], weight, columns, reach, bands)
    return grad.reshape(1, band_rows, columns, channels), weight_grad


def solution(mesh):
    placed = (
        P("dp", "space", None, None),
        P("dp", "space", None),
        P("dp", "space", None),
        P(),
        P(),
        P(),
    )
    return jax.shard_map(
        on_device,
        mesh=mesh,
        in_specs=placed,
        out_specs=(P("dp", "space", None, None), P(("dp", "space"), None)),
        check_vma=False,
    )
```
